32 devices in a mesh: rep: 1, row: 8 (over y, x, core), col: 4 (over z).
Axes of the slice: x: 2, y: 2, z: 4, core: 2. Of those that a mesh axis runs over, the one named last changes fastest.
Arguments:
- tokens: bfloat16 [4096, 1024], P(('rep', 'row', 'col')), may hold values from -6 to 6
- out_grad: bfloat16 [4096, 1024], P(('rep', 'row', 'col')), may hold values from -6 to 6
- expert_ids: int32 [4096, 2], P(('rep', 'row', 'col')), may hold values from 0 to 31, all different within a row; in each aligned block of 128 rows (0 to 127, 128 to 255, ...) at most 12 rows name the same one
- gates: float32 [4096, 2], P(('rep', 'row', 'col')), may hold values from 0.25 to 1
- up_weight: bfloat16 [32, 1024, 4096], P(('row', 'col'), None, 'rep'), may hold values from -0.1875 to 0.1875
- down_weight: bfloat16 [32, 4096, 1024], P(('row', 'col'), 'rep'), may hold values from -0.09375 to 0.09375
Outputs:
- input_grad: bfloat16 [4096, 1024], P(('rep', 'row', 'col'))
- down_grad: bfloat16 [32, 4096, 1024], P(('row', 'col'), 'rep')
The draws below stay inside these ranges and needn't reach their ends.
Inputs may be any that keep to these rules, and one draw needn't show every extreme that they name: `expert_ids`: in the 128 rows of one device no expert is named more than 12 times; in every draw some expert is named exactly 12 times in such a block.
All inputs are finite; a program needn't handle non-finite values.
Results may differ from the reference program's by a relative error of at most 0.013.
Values may be sent and summed in bfloat16 or wider, within the bound.
No kernel may reach another device: no remote copies, remote signals or barrier semaphores. Data moves between devices by JAX's collectives and lax.ppermute only.
A program may use at most 64 MiB of HBM per device.

```python
import math
import jax
import jax.numpy as jnp
import numpy as np
from jax import lax

D = 1024
FF = 4096
TOP = 2
TOK_DEV = 128
EXPERTS = 32
CAP = 12
TOKENS = 4096
N_REP = 1
N_ROW = 8
N_COL = 4


def shard_levels(key, dims, shards, low, high):
    level, own = 1.0, jax.random.fold_in(key, 6)
    for dim, parts in shards:
        heights = jnp.exp(jax.random.uniform(jax.random.fold_in(own, dim), (parts,), jnp.float32, low / len(shards), high / len(shards)))
        level = level * jnp.repeat(heights, dims[dim] // parts).reshape([-1 if axis == dim else 1 for axis in range(len(dims))])
    return level


def assign_block(own_key, own, number, rows, amount, top, most, skew):
    ranking = jax.random.permutation(own_key, amount)
    crowded, usual = load_shares(amount, rows * top, most, skew, True), load_shares(amount, rows * top, most, skew, False)
    places = jnp.arange(amount)

    def named(tallies, rotation):
        used = int((tallies > 0).sum())
        fixed = max(1, used // 4)
        shifted = fixed + (places - fixed + rotation * (used - fixed)) % max(1, amount - fixed)
        return jnp.zeros((amount,), jnp.int32).at[ranking[jnp.where(places < fixed, places, shifted)]].set(jnp.asarray(tallies, jnp.int32))

    tallies = jnp.where(number % 4 == 0, named(crowded, number // 4), named(usual, number - number // 4 - 1))
    mixed = jax.random.permutation(jax.random.fold_in(own, 3), amount)
    source_of, sink = mixed[0:amount // 2 * 2:2], mixed[1:amount // 2 * 2:2]
    slack = jnp.minimum(tallies[source_of] - 1, most - tallies[sink]) // 2
    slack = jnp.where((source_of == ranking[0]) | (sink == ranking[0]) | (tallies[sink] == 0), 0, jnp.maximum(slack, 0))
    shifted = jax.random.randint(jax.random.fold_in(own, 4), (amount // 2,), 0, 1 << 20) % (slack + 1)
    tallies = tallies.at[source_of].add(-shifted).at[sink].add(shifted)
    members = jnp.searchsorted(jnp.cumsum(tallies), jnp.arange(rows * top), side="right").astype(jnp.int32)
    grid = members.reshape(top, rows).T
    grid = grid[jax.random.permutation(jax.random.fold_in(own, 1), rows)]
    rotation = jax.random.randint(jax.random.fold_in(own, 2), (rows, 1), 0, top)
    return jnp.take_along_axis(grid, (jnp.arange(top)[None, :] + rotation) % top, axis=1)


def load_shares(number_of, total, reach, lean, full):
    weights = [(1 << 20) // math.isqrt(standing ** lean) + 1 for standing in range(1, number_of + 1)]
    largest = reach if full else min(reach, max(-(-total // number_of), total * weights[0] // sum(weights)))
    least = 1 if total - largest >= number_of - 1 else 0
    holding, surplus = [largest] + [least] * (number_of - 1), total - largest - least * (number_of - 1)
    while surplus > 0:
        movable = [i for i in range(1, number_of) if holding[i] < largest] or [i for i in range(1, number_of) if holding[i] < reach]
        pool, budget = sum([weights[i] for i in movable]), surplus
        for i in movable:
            more = min(reach - holding[i], max(1, budget * weights[i] // pool), surplus)
            holding[i] = holding[i] + more
            surplus = surplus - more
    return np.array(holding)


def gaussian(key, extent, width, limit, cuts=(), kind=jnp.bfloat16):
    result = jax.random.normal(key, extent, jnp.float32) * width
    if len(cuts) > 0:
        result = shard_levels(key, extent, cuts, -0.22, 0.18) * result
    return jnp.clip(result, min=-limit, max=limit).astype(kind)


def setup_inputs(seed: int = 0) -> dict:
    key_list = jax.random.split(jax.random.key(seed), 7)
    tokens = gaussian(key_list[0], (TOKENS, D), 1.0, 6.0, ((0, 32),))
    out_grad = gaussian(key_list[1], (TOKENS, D), 1.0, 6.0, ((0, 32),))
    expert_ids_keys = jax.random.split(jax.random.fold_in(key_list[2], 1), TOKENS // TOK_DEV)
    expert_ids_turns = jax.random.permutation(jax.random.fold_in(key_list[2], 3), TOKENS // TOK_DEV)
    expert_ids = jax.vmap(lambda own, number: assign_block(jax.random.fold_in(key_list[2], 2), own, number, TOK_DEV, EXPERTS, TOP, CAP, 2))(expert_ids_keys, expert_ids_turns).reshape((TOKENS, TOP))
    gates = jnp.clip(0.25 + 0.75 * jax.random.uniform(key_list[3], (TOKENS, TOP), jnp.float32) ** shard_levels(key_list[3], (TOKENS, TOP), ((0, 32),), -0.2, 0.2), 0.25, 1.0)
    up_weight = gaussian(key_list[4], (EXPERTS, D, FF), D ** -0.5, 0.1875, ((0, 32),))
    down_weight = gaussian(key_list[5], (EXPERTS, FF, D), FF ** -0.5, 0.09375, ((0, 32),))
    return {"tokens": tokens, "out_grad": out_grad, "expert_ids": expert_ids, "gates": gates, "up_weight": up_weight, "down_weight": down_weight}


def expert_step(packed):
    input_rows, grad_rows, up_block, down_block = packed
    preact = jnp.dot(input_rows, up_block, preferred_element_type=jnp.float32)
    hidden = jnp.maximum(preact, 0.0).astype(jnp.bfloat16)
    hidden_grad = jnp.dot(grad_rows, down_block.T, preferred_element_type=jnp.float32)
    preact_grad = jnp.where(preact > 0, hidden_grad, 0.0).astype(jnp.bfloat16)
    group_width = FF // N_REP
    summed = jnp.zeros((input_rows.shape[0], D), jnp.float32)
    for group in range(N_REP):
        lower = group * group_width
        upper = lower + group_width
        part_sum = jnp.dot(preact_grad[:, lower:upper], up_block[:, lower:upper].T, preferred_element_type=jnp.float32)
        summed = summed + part_sum.astype(jnp.bfloat16).astype(jnp.float32)
    returned = summed.astype(jnp.bfloat16)
    weight_grad = jnp.dot(hidden.T, grad_rows, preferred_element_type=jnp.float32).astype(jnp.bfloat16)
    return returned, weight_grad


def reference(tokens, out_grad, expert_ids, gates, up_weight, down_weight):
    device_count = N_REP * N_ROW * N_COL
    per_device = TOK_DEV * TOP
    flat_ids = expert_ids.reshape(device_count, per_device).astype(jnp.int32)
    onehot = (flat_ids[:, :, None] == jnp.arange(EXPERTS, dtype=jnp.int32)[None, None, :]).astype(jnp.int32)
    earlier = jnp.cumsum(onehot, axis=1) - onehot
    slot_index = jnp.sum(earlier * onehot, axis=2)
    owner = jnp.arange(device_count, dtype=jnp.int32)[:, None] * CAP
    position = (owner + slot_index).reshape(-1).astype(jnp.int32)
    expert_flat = flat_ids.reshape(-1)
    token_rows = jnp.repeat(tokens, TOP, axis=0)
    weighted = (gates.reshape(-1)[:, None] * jnp.repeat(out_grad, TOP, axis=0).astype(jnp.float32)).astype(jnp.bfloat16)
    buffer_in = jnp.zeros((EXPERTS, device_count * CAP, D), tokens.dtype).at[expert_flat, position].set(token_rows)
    buffer_grad = jnp.zeros((EXPERTS, device_count * CAP, D), weighted.dtype).at[expert_flat, position].set(weighted)
    returned, down_grad = lax.map(expert_step, (buffer_in, buffer_grad, up_weight, down_weight))
    picked = returned[expert_flat, position].astype(jnp.float32)
    input_grad = jnp.sum(picked.reshape(TOKENS, TOP, D), axis=1).astype(jnp.bfloat16)
    return input_grad, down_grad
```

```python
import functools

import jax
import jax.numpy as jnp
from jax import lax
from jax.experimental import pallas as pl
from jax.experimental.pallas import tpu as pltpu
from jax.sharding import PartitionSpec as P

VMEM_LIMIT = 48 * 1024 * 1024


def fold_of(capacity):
    fold = 1
    while capacity * fold % 8:
        fold *= 2
    return fold


def f32_dot(lhs, rhs, contract=((1,), (0,))):
    return lax.dot_general(lhs, rhs, (contract, ((), ())), preferred_element_type=jnp.float32)


def params():
    return pltpu.CompilerParams(vmem_limit_bytes=VMEM_LIMIT)


def place_rows(ids, experts, capacity, fold):
    tok_rows = ids.shape[1]
    names = lax.broadcasted_iota(jnp.int32, (experts, tok_rows), 0)
    chosen = [names == ids[k : k + 1, :] for k in range(ids.shape[0])]
    member = functools.reduce(jnp.logical_or, chosen).astype(jnp.bfloat16)
    before = (
        lax.broadcasted_iota(jnp.int32, (tok_rows, tok_rows), 0)
        < lax.broadcasted_iota(jnp.int32, (tok_rows, tok_rows), 1)
    ).astype(jnp.bfloat16)
    rank = f32_dot(member, before).astype(jnp.int32)
    place = names * (capacity * fold) + rank
    return [jnp.sum(jnp.where(pick, place, 0), axis=0, keepdims=True) for pick in chosen]


def prep_kernel(capacity, fold, experts, ids_ref, gates_ref, tokens_ref, grad_ref, tok_out, grad_out, place_out):
    places = place_rows(ids_ref[...], experts, capacity, fold)
    for k, place in enumerate(places):
        place_out[k : k + 1, :] = place
    gates = gates_ref[...]
    rows, width = tok_out.shape
    tok_rows = tokens_ref.shape[0]
    at = lax.broadcasted_iota(jnp.int32, (rows, tok_rows), 0)
    tok_sum = jnp.zeros((rows, width), jnp.float32)
    grad_sum = jnp.zeros((rows, width), jnp.float32)
    slot_gate = jnp.zeros((rows, 1), jnp.float32)
    for j in range(fold):
        hits = [at == place + j * capacity for place in places]
        gather = functools.reduce(jnp.logical_or, hits).astype(jnp.bfloat16)
        gate_map = sum(jnp.where(hit, gates[k : k + 1, :], 0.0) for k, hit in enumerate(hits))
        slot_gate += jnp.sum(gate_map, axis=1, keepdims=True)
        part = slice(j * width, (j + 1) * width)
        tok_sum += f32_dot(gather, tokens_ref[:, part])
        grad_sum += f32_dot(gather, grad_ref[:, part])
    tok_out[...] = tok_sum.astype(jnp.bfloat16)
    grad_out[...] = (slot_gate * grad_sum).astype(jnp.bfloat16)


def folded_rows(number, capacity, fold):
    owner = jnp.floor((number.astype(jnp.float32) + 0.5) * (1.0 / capacity)).astype(jnp.int32)
    return number + owner * (capacity * (fold - 1))


def unfold(folded_ref, plain_ref, capacity, fold):
    rows, width = folded_ref.shape
    slots = rows // fold
    at = lax.broadcasted_iota(jnp.int32, (slots, rows), 1)
    source = folded_rows(lax.broadcasted_iota(jnp.int32, (slots, 1), 0), capacity, fold)
    for j in range(fold):
        mover = (at == source + j * capacity).astype(jnp.bfloat16)
        plain_ref[:, j * width : (j + 1) * width] = f32_dot(mover, folded_ref[...]).astype(plain_ref.dtype)


def fold_into(plain, folded_ref, capacity, fold):
    rows, width = folded_ref.shape
    slots = rows // fold
    at = lax.broadcasted_iota(jnp.int32, (rows, slots), 0)
    target = folded_rows(lax.broadcasted_iota(jnp.int32, (1, slots), 1), capacity, fold)
    total = jnp.zeros((rows, width), jnp.float32)
    for j in range(fold):
        mover = (at == target + j * capacity).astype(jnp.bfloat16)
        total += f32_dot(mover, plain[:, j * width : (j + 1) * width])
    folded_ref[...] = total.astype(folded_ref.dtype)


def hidden_kernel(capacity, fold, landed_ref, up_ref, hidden_ref, rows_ref):
    @pl.when(pl.program_id(0) == 0)
    def _():
        unfold(landed_ref, rows_ref, capacity, fold)

    preact = f32_dot(rows_ref[...], up_ref[...])
    hidden_ref[...] = jnp.maximum(preact, 0.0).astype(jnp.bfloat16)


def row_grad_kernel(capacity, fold, landed_ref, up_ref, down_ref, hidden_ref, out_ref, rows_ref, sum_ref):
    step = pl.program_id(0)

    @pl.when(step == 0)
    def _():
        unfold(landed_ref, rows_ref, capacity, fold)

    hidden_grad = f32_dot(rows_ref[...], down_ref[...], ((1,), (1,)))
    preact_grad = jnp.where(hidden_ref[...] > 0, hidden_grad, 0.0).astype(jnp.bfloat16)
    part = f32_dot(preact_grad, up_ref[...], ((1,), (1,)))

    @pl.when(step == 0)
    def _():
        sum_ref[...] = part

    @pl.when(step > 0)
    def _():
        sum_ref[...] += part

    @pl.when(step == pl.num_programs(0) - 1)
    def _():
        fold_into(sum_ref[...].astype(jnp.bfloat16), out_ref, capacity, fold)


def down_grad_kernel(capacity, fold, landed_ref, hidden_ref, out_ref, rows_ref):
    @pl.when(pl.program_id(0) == 0)
    def _():
        unfold(landed_ref, rows_ref, capacity, fold)

    out_ref[...] = f32_dot(hidden_ref[...], rows_ref[...], ((0,), (0,))).astype(jnp.bfloat16)


def pick_kernel(capacity, fold, place_ref, returned_ref, out_ref):
    rows, width = returned_ref.shape
    tok_rows = out_ref.shape[0]
    at = lax.broadcasted_iota(jnp.int32, (rows, tok_rows), 0)
    for j in range(fold):
        hits = [at == place_ref[k : k + 1, :] + j * capacity for k in range(place_ref.shape[0])]
        chosen = functools.reduce(jnp.logical_or, hits).astype(jnp.bfloat16)
        total = f32_dot(chosen, returned_ref[...], ((0,), (0,)))
        out_ref[:, j * width : (j + 1) * width] = total.astype(jnp.bfloat16)


def exchange(rows, experts):
    cut = rows.reshape(experts, rows.shape[0] // experts, rows.shape[1])
    moved = lax.all_to_all(cut, ("row", "col"), split_axis=0, concat_axis=0, tiled=True)
    return moved.reshape(rows.shape)


def shards(tokens, out_grad, expert_ids, gates, up_weight, down_weight):
    tok_rows, features = tokens.shape
    top_count = expert_ids.shape[1]
    units = up_weight.shape[2]
    replicas = lax.axis_size("rep")
    experts = lax.axis_size("row") * lax.axis_size("col")
    capacity = 3 * tok_rows * top_count // (2 * experts)
    fold = fold_of(capacity)
    rows, width = experts * capacity * fold, features // fold
    slots = replicas * experts * capacity
    tile = min(units, 512)
    steps = units // tile
    sizes = (capacity, fold)
    bf16, f32 = jnp.bfloat16, jnp.float32
    flops = 2 * slots * features * units
    weight_bytes = 2 * features * units

    send_inputs, send_grads, places = pl.pallas_call(
        functools.partial(prep_kernel, *sizes, experts),
        out_shape=(
            jax.ShapeDtypeStruct((rows, width), bf16),
            jax.ShapeDtypeStruct((rows, width), bf16),
            jax.ShapeDtypeStruct((top_count, tok_rows), jnp.int32),
        ),
        compiler_params=params(),
        name="prep",
    )(expert_ids.T, gates.T, tokens, out_grad)

    landed_inputs = exchange(send_inputs, experts)
    landed_grads = exchange(send_grads, experts)
    if replicas > 1:
        landed_inputs = lax.all_gather(landed_inputs, "rep", axis=0, tiled=True)
        landed_grads = lax.all_gather(landed_grads, "rep", axis=0, tiled=True)

    landed_spec = pl.BlockSpec((replicas * rows, width), lambda i: (0, 0))
    up_spec = pl.BlockSpec((None, features, tile), lambda i: (0, 0, i))
    down_spec = pl.BlockSpec((None, tile, features), lambda i: (0, i, 0))
    hidden_spec = pl.BlockSpec((slots, tile), lambda i: (0, i))
    plain = pltpu.VMEM((slots, features), bf16)

    hidden = pl.pallas_call(
        functools.partial(hidden_kernel, *sizes),
        out_shape=jax.ShapeDtypeStruct((slots, units), bf16),
        grid=(steps,),
        in_specs=[landed_spec, up_spec],
        out_specs=hidden_spec,
        scratch_shapes=[plain],
        compiler_params=params(),
        cost_estimate=pl.CostEstimate(flops=flops, bytes_accessed=weight_bytes, transcendentals=0),
        name="hidden",
    )(landed_inputs, up_weight)

    summed_rows = pl.pallas_call(
        functools.partial(row_grad_kernel, *sizes),
        out_shape=jax.ShapeDtypeStruct((replicas * rows, width), bf16),
        grid=(steps,),
        in_specs=[landed_spec, up_spec, down_spec, hidden_spec],
        out_specs=landed_spec,
        scratch_shapes=[plain, pltpu.VMEM((slots, features), f32)],
        compiler_params=params(),
        cost_estimate=pl.CostEstimate(flops=2 * flops, bytes_accessed=2 * weight_bytes, transcendentals=0),
        name="row_grad",
    )(landed_grads, up_weight, down_weight, hidden)
    if replicas > 1:
        summed_rows = lax.psum_scatter(summed_rows, "rep", scatter_dimension=0, tiled=True)
    returned = exchange(summed_rows, experts)

    down_grad = pl.pallas_call(
        functools.partial(down_grad_kernel, *sizes),
        out_shape=jax.ShapeDtypeStruct((1, units, features), bf16),
        grid=(steps,),
        in_specs=[landed_spec, hidden_spec],
        out_specs=down_spec,
        scratch_shapes=[plain],
        compiler_params=params(),
        cost_estimate=pl.CostEstimate(flops=flops, bytes_accessed=weight_bytes, transcendentals=0),
        name="down_grad",
    )(landed_grads, hidden)

    input_grad = pl.pallas_call(
        functools.partial(pick_kernel, *sizes),
        out_shape=jax.ShapeDtypeStruct((tok_rows, features), bf16),
        compiler_params=params(),
        name="pick",
    )(places, returned)
    return input_grad, down_grad


def solution(mesh):
    by_token = P(("rep", "row", "col"), None)
    placed = (
        by_token,
        by_token,
        by_token,
        by_token,
        P(("row", "col"), None, "rep"),
        P(("row", "col"), "rep", None),
    )
    return jax.shard_map(
        shards,
        mesh=mesh,
        in_specs=placed,
        out_specs=(by_token, P(("row", "col"), "rep", None)),
        check_vma=False,
    )
```

```python
import functools

import jax
import jax.numpy as jnp
from jax import lax
from jax.experimental import pallas as pl
from jax.experimental.pallas import tpu as pltpu
from jax.sharding import Mesh, PartitionSpec as P

VMEM_LIMIT = 40 * 1024 * 1024
BLOCKS = 2


def f32_dot(lhs, rhs, contract=((1,), (0,))):
    return lax.dot_general(lhs, rhs, (contract, ((), ())), preferred_element_type=jnp.float32)


def params():
    return pltpu.CompilerParams(vmem_limit_bytes=VMEM_LIMIT)


def row_places(ids, half, block, capacity, local, columns):
    tok_rows = ids.shape[1]
    index = lax.broadcasted_iota(jnp.int32, (local, tok_rows), 0)
    group = jnp.floor((index.astype(jnp.float32) + 0.5) * (1.0 / columns)).astype(jnp.int32)
    names = index + (group + half) * columns
    chosen = [names == ids[k : k + 1, :] for k in range(ids.shape[0])]
    member = functools.reduce(jnp.logical_or, chosen).astype(jnp.bfloat16)
    before = (
        lax.broadcasted_iota(jnp.int32, (tok_rows, tok_rows), 0)
        < lax.broadcasted_iota(jnp.int32, (tok_rows, tok_rows), 1)
    ).astype(jnp.bfloat16)
    rank = f32_dot(member, before).astype(jnp.int32)
    place = (index * BLOCKS + block) * capacity + rank + 1
    return [jnp.sum(jnp.where(pick, place, 0), axis=0, keepdims=True) - 1 for pick in chosen]


def load_blocks(block_refs, rows_ref, sems):
    tok_rows = block_refs[0].shape[0]
    copies = [
        pltpu.make_async_copy(ref, rows_ref.at[pl.ds(b * tok_rows, tok_rows)], sems.at[b])
        for b, ref in enumerate(block_refs)
    ]
    for copy in copies:
        copy.start()
    return copies


def prep_tokens_kernel(
    capacity, columns, half_ref, own_ids, far_ids, own_ref, far_ref, out_ref, place_ref, rows_ref, sems
):
    copies = load_blocks((own_ref, far_ref), rows_ref, sems)
    rows = out_ref.shape[0]
    tok_rows = own_ref.shape[0]
    local = rows // (BLOCKS * capacity)
    at = lax.broadcasted_iota(jnp.int32, (rows, tok_rows), 0)
    gathers = []
    top_count = own_ids.shape[0]
    for b, ids in enumerate((own_ids, far_ids)):
        places = row_places(ids[...], half_ref[0], b, capacity, local, columns)
        for k, place in enumerate(places):
            place_ref[b * top_count + k : b * top_count + k + 1, :] = place
        gathers.append(functools.reduce(jnp.logical_or, [at == place for place in places]).astype(jnp.bfloat16))
    gather = jnp.concatenate(gathers, axis=1)
    for copy in copies:
        copy.wait()
    out_ref[...] = f32_dot(gather, rows_ref[...]).astype(jnp.bfloat16)


def prep_grads_kernel(place_ref, own_gates, far_gates, own_ref, far_ref, out_ref, rows_ref, sems):
    copies = load_blocks((own_ref, far_ref), rows_ref, sems)
    rows = out_ref.shape[0]
    tok_rows = own_ref.shape[0]
    top_count = own_gates.shape[0]
    at = lax.broadcasted_iota(jnp.int32, (rows, tok_rows), 0)
    gathers = []
    slot_gate = jnp.zeros((rows, 1), jnp.float32)
    for b, gates in enumerate((own_gates, far_gates)):
        hits = [at == place_ref[b * top_count + k : b * top_count + k + 1, :] for k in range(top_count)]
        gathers.append(functools.reduce(jnp.logical_or, hits).astype(jnp.bfloat16))
        gate_map = sum(jnp.where(hit, gates[k : k + 1, :], 0.0) for k, hit in enumerate(hits))
        slot_gate += jnp.sum(gate_map, axis=1, keepdims=True)
    gather = jnp.concatenate(gathers, axis=1)
    for copy in copies:
        copy.wait()
    out_ref[...] = (slot_gate * f32_dot(gather, rows_ref[...])).astype(jnp.bfloat16)


def hidden_kernel(landed_ref, up_ref, hidden_ref):
    preact = f32_dot(landed_ref[...], up_ref[...])
    hidden_ref[...] = jnp.maximum(preact, 0.0).astype(jnp.bfloat16).T


def row_grad_kernel(landed_ref, up_ref, down_ref, hidden_ref, out_ref, rows_ref, sum_ref):
    step = pl.program_id(0)

    @pl.when(step == 0)
    def _():
        rows_ref[...] = landed_ref[...].T

    hidden_grad = f32_dot(down_ref[...], rows_ref[...])
    preact_grad = jnp.where(hidden_ref[...] > 0, hidden_grad, 0.0).astype(jnp.bfloat16)
    part = f32_dot(up_ref[...], preact_grad)

    @pl.when(step == 0)
    def _():
        sum_ref[...] = part

    @pl.when(step > 0)
    def _():
        sum_ref[...] += part

    @pl.when(step == pl.num_programs(0) - 1)
    def _():
        out_ref[...] = sum_ref[...].astype(jnp.bfloat16).T


def down_grad_kernel(landed_ref, hidden_ref, out_ref):
    out_ref[...] = f32_dot(hidden_ref[...], landed_ref[...]).astype(jnp.bfloat16)


def picked_rows(place_ref, returned_ref, block, top_count):
    rows = returned_ref.shape[0]
    tok_rows = place_ref.shape[1]
    at = lax.broadcasted_iota(jnp.int32, (rows, tok_rows), 0)
    hits = [at == place_ref[block * top_count + k : block * top_count + k + 1, :] for k in range(top_count)]
    chosen = functools.reduce(jnp.logical_or, hits).astype(jnp.bfloat16)
    return f32_dot(chosen, returned_ref[...], ((0,), (0,)))


def pick_far_kernel(top_count, place_ref, returned_ref, out_ref):
    out_ref[...] = picked_rows(place_ref, returned_ref, 1, top_count).astype(jnp.bfloat16)


def pick_own_kernel(top_count, place_ref, returned_ref, far_ref, out_ref):
    own = picked_rows(place_ref, returned_ref, 0, top_count)
    out_ref[...] = (own + far_ref[...].astype(jnp.float32)).astype(jnp.bfloat16)


def exchange(rows, local):
    cut = rows.reshape(local, rows.shape[0] // local, rows.shape[1])
    moved = lax.all_to_all(cut, ("row", "col"), split_axis=0, concat_axis=0, tiled=True)
    return moved.reshape(rows.shape)


def swap(block):
    return lax.ppermute(block, "half", [(0, 1), (1, 0)])


def shards(tokens, out_grad, expert_ids, gates, up_weight, down_weight):
    tok_rows, features = tokens.shape
    top_count = expert_ids.shape[1]
    units = up_weight.shape[2]
    replicas = lax.axis_size("rep")
    columns = lax.axis_size("col")
    local = lax.axis_size("row") * columns
    capacity = 3 * tok_rows * top_count // (2 * BLOCKS * local)
    rows = local * BLOCKS * capacity
    slots = replicas * rows
    tile = min(units, 512)
    steps = units // tile
    bf16, f32 = jnp.bfloat16, jnp.float32
    flops = 2 * slots * features * units
    weight_bytes = 2 * features * units

    own_ids, own_gates = expert_ids.T, gates.T
    far_ids = swap(own_ids)
    far_tokens = swap(tokens)
    far_gates = swap(own_gates)
    far_grad = swap(out_grad)
    half = lax.axis_index("half").astype(jnp.int32).reshape(1)

    smem = pl.BlockSpec(memory_space=pltpu.SMEM)
    vmem = pl.BlockSpec(memory_space=pltpu.VMEM)
    anywhere = pl.BlockSpec(memory_space=pl.ANY)
    loading = [pltpu.VMEM((BLOCKS * tok_rows, features), bf16), pltpu.SemaphoreType.DMA((BLOCKS,))]

    send_inputs, places = pl.pallas_call(
        functools.partial(prep_tokens_kernel, capacity, columns),
        out_shape=(
            jax.ShapeDtypeStruct((rows, features), bf16),
            jax.ShapeDtypeStruct((BLOCKS * top_count, tok_rows), jnp.int32),
        ),
        in_specs=[smem, vmem, vmem, anywhere, anywhere],
        scratch_shapes=loading,
        compiler_params=params(),
        name="prep_tokens",
    )(half, own_ids, far_ids, tokens, far_tokens)
    landed_inputs = exchange(send_inputs, local)

    send_grads = pl.pallas_call(
        prep_grads_kernel,
        out_shape=jax.ShapeDtypeStruct((rows, features), bf16),
        in_specs=[vmem, vmem, vmem, anywhere, anywhere],
        scratch_shapes=loading,
        compiler_params=params(),
        name="prep_grads",
    )(places, own_gates, far_gates, out_grad, far_grad)
    landed_grads = exchange(send_grads, local)
    if replicas > 1:
        landed_inputs = lax.all_gather(landed_inputs, "rep", axis=0, tiled=True)
        landed_grads = lax.all_gather(landed_grads, "rep", axis=0, tiled=True)

    landed_spec = pl.BlockSpec((slots, features), lambda i: (0, 0))
    up_spec = pl.BlockSpec((None, features, tile), lambda i: (0, 0, i))
    down_spec = pl.BlockSpec((None, tile, features), lambda i: (0, i, 0))
    hidden_spec = pl.BlockSpec((tile, slots), lambda i: (i, 0))

    hidden = pl.pallas_call(
        hidden_kernel,
        out_shape=jax.ShapeDtypeStruct((units, slots), bf16),
        grid=(steps,),
        in_specs=[landed_spec, up_spec],
        out_specs=hidden_spec,
        compiler_params=params(),
        cost_estimate=pl.CostEstimate(flops=flops, bytes_accessed=weight_bytes, transcendentals=0),
        name="hidden",
    )(landed_inputs, up_weight)

    summed_rows = pl.pallas_call(
        row_grad_kernel,
        out_shape=jax.ShapeDtypeStruct((slots, features), bf16),
        grid=(steps,),
        in_specs=[landed_spec, up_spec, down_spec, hidden_spec],
        out_specs=landed_spec,
        scratch_shapes=[pltpu.VMEM((features, slots), bf16), pltpu.VMEM((features, slots), f32)],
        compiler_params=params(),
        cost_estimate=pl.CostEstimate(flops=2 * flops, bytes_accessed=2 * weight_bytes, transcendentals=0),
        name="row_grad",
    )(landed_grads, up_weight, down_weight, hidden)
    if replicas > 1:
        summed_rows = lax.psum_scatter(summed_rows, "rep", scatter_dimension=0, tiled=True)
    returned = exchange(summed_rows, local)

    down_grad = pl.pallas_call(
        down_grad_kernel,
        out_shape=jax.ShapeDtypeStruct((1, units, features), bf16),
        grid=(steps,),
        in_specs=[landed_spec, hidden_spec],
        out_specs=down_spec,
        compiler_params=params(),
        cost_estimate=pl.CostEstimate(flops=flops, bytes_accessed=weight_bytes, transcendentals=0),
        name="down_grad",
    )(landed_grads, hidden)

    far_sums = pl.pallas_call(
        functools.partial(pick_far_kernel, top_count),
        out_shape=jax.ShapeDtypeStruct((tok_rows, features), bf16),
        compiler_params=params(),
        name="pick_far",
    )(places, returned)
    input_grad = pl.pallas_call(
        functools.partial(pick_own_kernel, top_count),
        out_shape=jax.ShapeDtypeStruct((tok_rows, features), bf16),
        compiler_params=params(),
        name="pick_own",
    )(places, returned, swap(far_sums))
    return input_grad, down_grad


def solution(mesh):
    sizes = dict(mesh.shape)
    cut = Mesh(
        mesh.devices.reshape(sizes["rep"], sizes["row"], 2, sizes["col"] // 2),
        ("rep", "row", "half", "col"),
    )
    owner = ("row", "half", "col")
    by_token = P(("rep",) + owner, None)
    return jax.shard_map(
        shards,
        mesh=cut,
        in_specs=(by_token,) * 4 + (P(owner, None, "rep"), P(owner, "rep", None)),
        out_specs=(by_token, P(owner, "rep", None)),
        check_vma=False,
    )
```

```python
import functools

import jax
import jax.numpy as jnp
from jax import lax
from jax.experimental import pallas as pl
from jax.experimental.pallas import tpu as pltpu
from jax.sharding import Mesh, PartitionSpec as P

VMEM_LIMIT = 50 * 1024 * 1024
PAIR = 2
NOWHERE = -(1 << 20)


def f32_dot(lhs, rhs, contract=((1,), (0,))):
    return lax.dot_general(lhs, rhs, (contract, ((), ())), preferred_element_type=jnp.float32)


def params():
    return pltpu.CompilerParams(vmem_limit_bytes=VMEM_LIMIT)


def row_places(ids, half, capacity, local, columns):
    tok_rows = ids.shape[1]
    index = lax.broadcasted_iota(jnp.int32, (local, tok_rows), 0)
    group = jnp.floor((index.astype(jnp.float32) + 0.5) * (1.0 / columns)).astype(jnp.int32)
    names = index + (group + half) * columns
    chosen = [names == ids[k : k + 1, :] for k in range(ids.shape[0])]
    member = functools.reduce(jnp.logical_or, chosen).astype(jnp.bfloat16)
    before = (
        lax.broadcasted_iota(jnp.int32, (tok_rows, tok_rows), 0)
        < lax.broadcasted_iota(jnp.int32, (tok_rows, tok_rows), 1)
    ).astype(jnp.bfloat16)
    rank = f32_dot(member, before).astype(jnp.int32)
    place = index * (PAIR * capacity) + rank - NOWHERE
    return [jnp.sum(jnp.where(pick, place, 0), axis=0, keepdims=True) + NOWHERE for pick in chosen]


def hits_at(rows, places):
    at = lax.broadcasted_iota(jnp.int32, (rows, places[0].shape[1]), 0)
    return [at == place for place in places]


def either(hits):
    return functools.reduce(jnp.logical_or, hits).astype(jnp.bfloat16)


def start_copies(sources, targets, sems):
    copies = [pltpu.make_async_copy(*pair, sems.at[i]) for i, pair in enumerate(zip(sources, targets))]
    for copy in copies:
        copy.start()
    return copies


def own_dispatch_kernel(
    capacity, columns, half_ref, ids_ref, gates_ref, tokens_ref, grad_ref, out_ref, place_ref, rows_ref, sems
):
    tok_rows = tokens_ref.shape[0]
    copies = start_copies(
        (tokens_ref, grad_ref),
        (rows_ref.at[pl.ds(0, tok_rows)], rows_ref.at[pl.ds(tok_rows, tok_rows)]),
        sems,
    )
    rows = out_ref.shape[0]
    places = row_places(ids_ref[...], half_ref[0], capacity, rows // (PAIR * capacity), columns)
    gates = gates_ref[...]
    for k, place in enumerate(places):
        place_ref[k : k + 1, :] = place
    token_hits = hits_at(rows, places)
    grad_hits = hits_at(rows, [place + capacity for place in places])
    scales = [jnp.where(hit, 1.0, 0.0) for hit in token_hits]
    scales += [jnp.where(hit, gates[k : k + 1, :], 0.0) for k, hit in enumerate(grad_hits)]
    scale = jnp.sum(sum(scales), axis=1, keepdims=True)
    gather = jnp.concatenate([either(token_hits), either(grad_hits)], axis=1)
    for copy in copies:
        copy.wait()
    out_ref[...] = (scale * f32_dot(gather, rows_ref[...])).astype(jnp.bfloat16)


def far_tokens_kernel(capacity, columns, half_ref, ids_ref, tokens_ref, out_ref, place_ref):
    rows, width = out_ref.shape
    places = row_places(ids_ref[...], half_ref[0], capacity, rows // (PAIR * capacity), columns)
    for k, place in enumerate(places):
        place_ref[k : k + 1, :] = place
    total = jnp.zeros((rows, width), jnp.float32)
    for j in range(PAIR):
        gather = either(hits_at(rows, [place + j * capacity for place in places]))
        total += f32_dot(gather, tokens_ref[:, j * width : (j + 1) * width])
    out_ref[...] = total.astype(jnp.bfloat16)


def far_grads_kernel(capacity, place_ref, gates_ref, grad_ref, out_ref):
    rows, width = out_ref.shape
    top_count = place_ref.shape[0]
    gates = gates_ref[...]
    total = jnp.zeros((rows, width), jnp.float32)
    scale = jnp.zeros((rows, 1), jnp.float32)
    for j in range(PAIR):
        hits = hits_at(rows, [place_ref[k : k + 1, :] + j * capacity for k in range(top_count)])
        scales = [jnp.where(hit, gates[k : k + 1, :], 0.0) for k, hit in enumerate(hits)]
        scale += jnp.sum(sum(scales), axis=1, keepdims=True)
        total += f32_dot(either(hits), grad_ref[:, j * width : (j + 1) * width])
    out_ref[...] = (scale * total).astype(jnp.bfloat16)


def paired_rows(number, capacity):
    owner = jnp.floor((number.astype(jnp.float32) + 0.5) * (1.0 / capacity)).astype(jnp.int32)
    return number + owner * ((PAIR - 1) * capacity)


def taken(landed_ref, j, capacity):
    rows = landed_ref.shape[0]
    slots = rows // PAIR
    at = lax.broadcasted_iota(jnp.int32, (slots, rows), 1)
    source = paired_rows(lax.broadcasted_iota(jnp.int32, (slots, 1), 0), capacity) + j * capacity
    return f32_dot((at == source).astype(jnp.bfloat16), landed_ref[...]).astype(jnp.bfloat16)


def unfold(landed_ref, rows_ref, capacity):
    width = landed_ref.shape[1]
    for j in range(PAIR):
        rows_ref[:, j * width : (j + 1) * width] = taken(landed_ref, j, capacity)


def fold(plain, out_ref, capacity):
    rows, width = out_ref.shape
    slots = rows // PAIR
    at = lax.broadcasted_iota(jnp.int32, (rows, slots), 0)
    target = paired_rows(lax.broadcasted_iota(jnp.int32, (1, slots), 1), capacity)
    total = jnp.zeros((rows, width), jnp.float32)
    for j in range(PAIR):
        mover = (at == target + j * capacity).astype(jnp.bfloat16)
        total += f32_dot(mover, plain[:, j * width : (j + 1) * width])
    out_ref[...] = total.astype(jnp.bfloat16)


def add_row_grad(capacity, hidden, grads_ref, up_ref, down_ref, out_ref, sum_ref):
    step = pl.program_id(0)
    hidden_grad = f32_dot(grads_ref[...], down_ref[...], ((1,), (1,)))
    preact_grad = jnp.where(hidden > 0, hidden_grad, 0.0).astype(jnp.bfloat16)
    part = f32_dot(preact_grad, up_ref[...], ((1,), (1,)))

    @pl.when(step == 0)
    def _():
        sum_ref[...] = part

    @pl.when(step > 0)
    def _():
        sum_ref[...] += part

    @pl.when(step == pl.num_programs(0) - 1)
    def _():
        fold(sum_ref[...].astype(jnp.bfloat16), out_ref, capacity)


def relu(preact):
    return jnp.maximum(preact, 0.0).astype(jnp.bfloat16)


def own_expert_kernel(capacity, landed_ref, up_ref, down_ref, hidden_ref, out_ref, rows_ref, grads_ref, sum_ref):
    @pl.when(pl.program_id(0) == 0)
    def _():
        rows_ref[...] = taken(landed_ref, 0, capacity)
        grads_ref[...] = taken(landed_ref, 1, capacity)

    hidden = relu(f32_dot(rows_ref[...], up_ref[...]))
    hidden_ref[...] = hidden
    add_row_grad(capacity, hidden, grads_ref, up_ref, down_ref, out_ref, sum_ref)


def far_hidden_kernel(capacity, landed_ref, up_ref, hidden_ref, rows_ref):
    @pl.when(pl.program_id(0) == 0)
    def _():
        unfold(landed_ref, rows_ref, capacity)

    hidden_ref[...] = relu(f32_dot(rows_ref[...], up_ref[...]))


def far_row_grad_kernel(capacity, landed_ref, up_ref, down_ref, hidden_ref, out_ref, grads_ref, sum_ref):
    @pl.when(pl.program_id(0) == 0)
    def _():
        unfold(landed_ref, grads_ref, capacity)

    add_row_grad(capacity, hidden_ref[...], grads_ref, up_ref, down_ref, out_ref, sum_ref)


def down_grad_kernel(
    capacity, own_ref, far_ref, own_hidden_ref, far_hidden_ref, out_ref, own_grads_ref, far_grads_ref
):
    @pl.when(pl.program_id(0) == 0)
    def _():
        own_grads_ref[...] = taken(own_ref, 1, capacity)
        unfold(far_ref, far_grads_ref, capacity)

    own = f32_dot(own_hidden_ref[...], own_grads_ref[...], ((0,), (0,)))
    far = f32_dot(far_hidden_ref[...], far_grads_ref[...], ((0,), (0,)))
    out_ref[...] = (own + far).astype(jnp.bfloat16)


def picked(place_ref, returned_ref, j, capacity):
    top_count = place_ref.shape[0]
    hits = hits_at(returned_ref.shape[0], [place_ref[k : k + 1, :] + j * capacity for k in range(top_count)])
    return f32_dot(either(hits), returned_ref[...], ((0,), (0,)))


def pick_far_kernel(capacity, place_ref, returned_ref, out_ref):
    width = returned_ref.shape[1]
    for j in range(PAIR):
        out_ref[:, j * width : (j + 1) * width] = picked(place_ref, returned_ref, j, capacity).astype(jnp.bfloat16)


def pick_own_kernel(capacity, place_ref, returned_ref, far_ref, out_ref):
    width = returned_ref.shape[1]
    for j in range(PAIR):
        part = slice(j * width, (j + 1) * width)
        own = picked(place_ref, returned_ref, j, capacity)
        out_ref[:, part] = (own + far_ref[:, part].astype(jnp.float32)).astype(jnp.bfloat16)


def exchange(rows, local):
    cut = rows.reshape(local, rows.shape[0] // local, rows.shape[1])
    moved = lax.all_to_all(cut, ("row", "col"), split_axis=0, concat_axis=0, tiled=True)
    moved = moved.reshape(rows.shape)
    if lax.axis_size("rep") > 1:
        moved = lax.all_gather(moved, "rep", axis=0, tiled=True)
    return moved


def give_back(rows, local):
    if lax.axis_size("rep") > 1:
        rows = lax.psum_scatter(rows, "rep", scatter_dimension=0, tiled=True)
    cut = rows.reshape(local, rows.shape[0] // local, rows.shape[1])
    moved = lax.all_to_all(cut, ("row", "col"), split_axis=0, concat_axis=0, tiled=True)
    return moved.reshape(rows.shape)


def swap(block):
    return lax.ppermute(block, "half", [(0, 1), (1, 0)])


def shards(tokens, out_grad, expert_ids, gates, up_weight, down_weight):
    tok_rows, features = tokens.shape
    top_count = expert_ids.shape[1]
    units = up_weight.shape[2]
    replicas = lax.axis_size("rep")
    columns = lax.axis_size("col")
    local = lax.axis_size("row") * columns
    capacity = 3 * tok_rows * top_count // (4 * local)
    rows = local * PAIR * capacity
    width = features // PAIR
    pooled = replicas * rows
    slots = pooled // PAIR
    tile = min(units, 512)
    steps = units // tile
    bf16, f32 = jnp.bfloat16, jnp.float32
    flops = 2 * slots * features * units
    weight_bytes = 2 * features * units
    shape = jax.ShapeDtypeStruct

    def cost(matmuls, weights):
        return pl.CostEstimate(flops=matmuls * flops, bytes_accessed=weights * weight_bytes, transcendentals=0)

    own_ids, own_gates = expert_ids.T, gates.T
    far_tokens, far_ids = swap(tokens), swap(own_ids)
    far_grad, far_gates = swap(out_grad), swap(own_gates)
    half = lax.axis_index("half").astype(jnp.int32).reshape(1)

    smem = pl.BlockSpec(memory_space=pltpu.SMEM)
    vmem = pl.BlockSpec(memory_space=pltpu.VMEM)
    hbm = pl.BlockSpec(memory_space=pltpu.HBM)

    send_own, own_places = pl.pallas_call(
        functools.partial(own_dispatch_kernel, capacity, columns),
        out_shape=(shape((rows, features), bf16), shape((top_count, tok_rows), jnp.int32)),
        in_specs=[smem, vmem, vmem, hbm, hbm],
        scratch_shapes=[pltpu.VMEM((2 * tok_rows, features), bf16), pltpu.SemaphoreType.DMA((2,))],
        compiler_params=params(),
        name="own_dispatch",
    )(half, own_ids, own_gates, tokens, out_grad)
    landed_own = exchange(send_own, local)

    send_tokens, far_places = pl.pallas_call(
        functools.partial(far_tokens_kernel, capacity, columns),
        out_shape=(shape((rows, width), bf16), shape((top_count, tok_rows), jnp.int32)),
        in_specs=[smem, vmem, vmem],
        compiler_params=params(),
        name="far_tokens",
    )(half, far_ids, far_tokens)
    landed_tokens = exchange(send_tokens, local)

    send_grads = pl.pallas_call(
        functools.partial(far_grads_kernel, capacity),
        out_shape=shape((rows, width), bf16),
        compiler_params=params(),
        name="far_grads",
    )(far_places, far_gates, far_grad)
    landed_grads = exchange(send_grads, local)

    own_spec = pl.BlockSpec((pooled, features), lambda i: (0, 0))
    folded_spec = pl.BlockSpec((pooled, width), lambda i: (0, 0))
    up_spec = pl.BlockSpec((None, features, tile), lambda i: (0, 0, i))
    down_spec = pl.BlockSpec((None, tile, features), lambda i: (0, i, 0))
    hidden_spec = pl.BlockSpec((slots, tile), lambda i: (0, i))
    plain = pltpu.VMEM((slots, features), bf16)
    total = pltpu.VMEM((slots, features), f32)

    own_hidden, own_back = pl.pallas_call(
        functools.partial(own_expert_kernel, capacity),
        out_shape=(shape((slots, units), bf16), shape((pooled, width), bf16)),
        grid=(steps,),
        in_specs=[own_spec, up_spec, down_spec],
        out_specs=(hidden_spec, folded_spec),
        scratch_shapes=[plain, plain, total],
        compiler_params=params(),
        cost_estimate=cost(3, 2),
        name="own_expert",
    )(landed_own, up_weight, down_weight)

    far_hidden = pl.pallas_call(
        functools.partial(far_hidden_kernel, capacity),
        out_shape=shape((slots, units), bf16),
        grid=(steps,),
        in_specs=[folded_spec, up_spec],
        out_specs=hidden_spec,
        scratch_shapes=[plain],
        compiler_params=params(),
        cost_estimate=cost(1, 1),
        name="far_hidden",
    )(landed_tokens, up_weight)

    far_back = pl.pallas_call(
        functools.partial(far_row_grad_kernel, capacity),
        out_shape=shape((pooled, width), bf16),
        grid=(steps,),
        in_specs=[folded_spec, up_spec, down_spec, hidden_spec],
        out_specs=folded_spec,
        scratch_shapes=[plain, total],
        compiler_params=params(),
        cost_estimate=cost(2, 2),
        name="far_row_grad",
    )(landed_grads, up_weight, down_weight, far_hidden)
    returned_far = give_back(far_back, local)

    far_sums = pl.pallas_call(
        functools.partial(pick_far_kernel, capacity),
        out_shape=shape((tok_rows, features), bf16),
        compiler_params=params(),
        name="pick_far",
    )(far_places, returned_far)
    arrived = swap(far_sums)
    returned_own = give_back(own_back, local)

    down_grad = pl.pallas_call(
        functools.partial(down_grad_kernel, capacity),
        out_shape=shape((1, units, features), bf16),
        grid=(steps,),
        in_specs=[own_spec, folded_spec, hidden_spec, hidden_spec],
        out_specs=down_spec,
        scratch_shapes=[plain, plain],
        compiler_params=params(),
        cost_estimate=cost(2, 1),
        name="down_grad",
    )(landed_own, landed_grads, own_hidden, far_hidden)

    input_grad = pl.pallas_call(
        functools.partial(pick_own_kernel, capacity),
        out_shape=shape((tok_rows, features), bf16),
        compiler_params=params(),
        name="pick_own",
    )(own_places, returned_own, arrived)
    return input_grad, down_grad


def solution(mesh):
    sizes = dict(mesh.shape)
    cut = Mesh(
        mesh.devices.reshape(sizes["rep"], sizes["row"], 2, sizes["col"] // 2),
        ("rep", "row", "half", "col"),
    )
    owner = ("row", "half", "col")
    by_token = P(("rep",) + owner, None)
    return jax.shard_map(
        shards,
        mesh=cut,
        in_specs=(by_token,) * 4 + (P(owner, None, "rep"), P(owner, "rep", None)),
        out_specs=(by_token, P(owner, "rep", None)),
        check_vma=False,
    )
```

```python
import functools

import jax
import jax.numpy as jnp
from jax import lax
from jax.experimental import pallas as pl
from jax.experimental.pallas import tpu as pltpu
from jax.sharding import PartitionSpec as P

VMEM_LIMIT = 46 * 1024 * 1024
PAIR = 2
NOWHERE = -(1 << 20)


def f32_dot(lhs, rhs, contract=((1,), (0,))):
    return lax.dot_general(lhs, rhs, (contract, ((), ())), preferred_element_type=jnp.float32)


def params():
    return pltpu.CompilerParams(vmem_limit_bytes=VMEM_LIMIT)


def row_places(ids, me, capacity, blocks, columns, far):
    tok_rows = ids.shape[1]
    index = lax.broadcasted_iota(jnp.int32, (blocks, tok_rows), 0)
    group = jnp.floor((index.astype(jnp.float32) + 0.5) * (1.0 / columns)).astype(jnp.int32)
    names = (index + (group + far) * columns) ^ me
    chosen = [names == ids[k : k + 1, :] for k in range(ids.shape[0])]
    member = functools.reduce(jnp.logical_or, chosen).astype(jnp.bfloat16)
    before = (
        lax.broadcasted_iota(jnp.int32, (tok_rows, tok_rows), 0)
        < lax.broadcasted_iota(jnp.int32, (tok_rows, tok_rows), 1)
    ).astype(jnp.bfloat16)
    rank = f32_dot(member, before).astype(jnp.int32)
    place = index * (PAIR * capacity) + rank - NOWHERE
    return [jnp.sum(jnp.where(pick, place, 0), axis=0, keepdims=True) + NOWHERE for pick in chosen]


def hits_at(rows, places):
    at = lax.broadcasted_iota(jnp.int32, (rows, places[0].shape[1]), 0)
    return [at == place for place in places]


def either(hits):
    return functools.reduce(jnp.logical_or, hits).astype(jnp.bfloat16)


def scatter_blocks(value, block_refs):
    size = block_refs[0].shape[0]
    for p, ref in enumerate(block_refs):
        ref[...] = value[p * size : (p + 1) * size, :].astype(jnp.bfloat16)


def stack_blocks(block_refs, stack_ref):
    size = block_refs[0].shape[0]
    for p, ref in enumerate(block_refs):
        stack_ref[p * size : (p + 1) * size, :] = ref[...].astype(jnp.float32)
    return stack_ref[...].astype(jnp.bfloat16)


def far_dispatch_kernel(capacity, columns, blocks, me_ref, ids_ref, gates_ref, tokens_ref, grad_ref, *outs):
    token_outs, grad_outs, place_ref = outs[:blocks], outs[blocks : 2 * blocks], outs[2 * blocks]
    width = token_outs[0].shape[1]
    rows = blocks * PAIR * capacity
    places = row_places(ids_ref[...], me_ref[0], capacity, blocks, columns, 1)
    gates = gates_ref[...]
    for k, place in enumerate(places):
        place_ref[k : k + 1, :] = place
    token_sum = jnp.zeros((rows, width), jnp.float32)
    grad_sum = jnp.zeros((rows, width), jnp.float32)
    scale = jnp.zeros((rows, 1), jnp.float32)
    for j in range(PAIR):
        hits = hits_at(rows, [place + j * capacity for place in places])
        scales = [jnp.where(hit, gates[k : k + 1, :], 0.0) for k, hit in enumerate(hits)]
        scale += jnp.sum(sum(scales), axis=1, keepdims=True)
        gather = either(hits)
        part = slice(j * width, (j + 1) * width)
        token_sum += f32_dot(gather, tokens_ref[:, part])
        grad_sum += f32_dot(gather, grad_ref[:, part])
    scatter_blocks(token_sum, token_outs)
    scatter_blocks(scale * grad_sum, grad_outs)


def near_dispatch_kernel(
    capacity, columns, blocks, me_ref, ids_ref, gates_ref, tokens_ref, grad_ref, after_ref, *outs
):
    block_outs, place_ref = outs[:blocks], outs[blocks]
    rows = blocks * PAIR * capacity
    places = row_places(ids_ref[...], me_ref[0], capacity, blocks, columns, 0)
    gates = gates_ref[...]
    for k, place in enumerate(places):
        place_ref[k : k + 1, :] = place
    token_hits = hits_at(rows, places)
    grad_hits = hits_at(rows, [place + capacity for place in places])
    scales = [jnp.where(hit, gates[k : k + 1, :], 0.0) for k, hit in enumerate(grad_hits)]
    scale = jnp.sum(sum(scales), axis=1, keepdims=True)
    value = f32_dot(either(token_hits), tokens_ref[...]) + scale * f32_dot(either(grad_hits), grad_ref[...])
    scatter_blocks(value, block_outs)


def paired_rows(number, capacity):
    owner = jnp.floor((number.astype(jnp.float32) + 0.5) * (1.0 / capacity)).astype(jnp.int32)
    return number + owner * ((PAIR - 1) * capacity)


def taken(landed, j, capacity):
    rows = landed.shape[0]
    slots = rows // PAIR
    at = lax.broadcasted_iota(jnp.int32, (slots, rows), 1)
    source = paired_rows(lax.broadcasted_iota(jnp.int32, (slots, 1), 0), capacity) + j * capacity
    return f32_dot((at == source).astype(jnp.bfloat16), landed).astype(jnp.bfloat16)


def unfold(landed, rows_ref, capacity):
    width = landed.shape[1]
    for j in range(PAIR):
        rows_ref[:, j * width : (j + 1) * width] = taken(landed, j, capacity)


def fold(plain, capacity):
    slots = plain.shape[0]
    rows, width = PAIR * slots, plain.shape[1] // PAIR
    at = lax.broadcasted_iota(jnp.int32, (rows, slots), 0)
    target = paired_rows(lax.broadcasted_iota(jnp.int32, (1, slots), 1), capacity)
    total = jnp.zeros((rows, width), jnp.float32)
    for j in range(PAIR):
        mover = (at == target + j * capacity).astype(jnp.bfloat16)
        total += f32_dot(mover, plain[:, j * width : (j + 1) * width])
    return total


def add_row_grad(capacity, hidden, grads_ref, up_ref, down_ref, outs, sum_ref):
    step = pl.program_id(0)
    hidden_grad = f32_dot(grads_ref[...], down_ref[...], ((1,), (1,)))
    preact_grad = jnp.where(hidden > 0, hidden_grad, 0.0).astype(jnp.bfloat16)
    part = f32_dot(preact_grad, up_ref[...], ((1,), (1,)))

    @pl.when(step == 0)
    def _():
        sum_ref[...] = part

    @pl.when(step > 0)
    def _():
        sum_ref[...] += part

    @pl.when(step == pl.num_programs(0) - 1)
    def _():
        scatter_blocks(fold(sum_ref[...].astype(jnp.bfloat16), capacity), outs)


def relu(preact):
    return jnp.maximum(preact, 0.0).astype(jnp.bfloat16)


def near_expert_kernel(capacity, blocks, *refs):
    landed, (up_ref, down_ref), refs = refs[:blocks], refs[blocks : blocks + 2], refs[blocks + 2 :]
    hidden_ref, grads_ref, outs, (rows_ref, sum_ref, stack_ref) = refs[0], refs[1], refs[2:-3], refs[-3:]

    @pl.when(pl.program_id(0) == 0)
    def _():
        mixed = stack_blocks(landed, stack_ref)
        rows_ref[...] = taken(mixed, 0, capacity)
        grads_ref[...] = taken(mixed, 1, capacity)

    hidden = relu(f32_dot(rows_ref[...], up_ref[...]))
    hidden_ref[...] = hidden
    add_row_grad(capacity, hidden, grads_ref, up_ref, down_ref, outs, sum_ref)


def far_hidden_kernel(capacity, blocks, *refs):
    landed, (up_ref, after_ref, hidden_ref, rows_ref, stack_ref) = refs[:blocks], refs[blocks:]

    @pl.when(pl.program_id(0) == 0)
    def _():
        unfold(stack_blocks(landed, stack_ref), rows_ref, capacity)

    hidden_ref[...] = relu(f32_dot(rows_ref[...], up_ref[...]))


def far_row_grad_kernel(capacity, blocks, *refs):
    landed, (up_ref, down_ref, hidden_ref), refs = refs[:blocks], refs[blocks : blocks + 3], refs[blocks + 3 :]
    grads_ref, outs, (sum_ref, stack_ref) = refs[0], refs[1:-2], refs[-2:]

    @pl.when(pl.program_id(0) == 0)
    def _():
        unfold(stack_blocks(landed, stack_ref), grads_ref, capacity)

    add_row_grad(capacity, hidden_ref[...], grads_ref, up_ref, down_ref, outs, sum_ref)


def down_grad_kernel(near_grads_ref, far_grads_ref, near_hidden_ref, far_hidden_ref, out_ref):
    near = f32_dot(near_hidden_ref[...], near_grads_ref[...], ((0,), (0,)))
    far = f32_dot(far_hidden_ref[...], far_grads_ref[...], ((0,), (0,)))
    out_ref[...] = (near + far).astype(jnp.bfloat16)


def pick_kernel(capacity, blocks, *refs):
    near, far, (near_place, far_place, out_ref, near_stack, far_stack) = (
        refs[:blocks],
        refs[blocks : 2 * blocks],
        refs[2 * blocks :],
    )
    groups = (
        (near_place, stack_blocks(near, near_stack)),
        (far_place, stack_blocks(far, far_stack)),
    )
    width = near_stack.shape[1]
    for j in range(PAIR):
        total = jnp.zeros((out_ref.shape[0], width), jnp.float32)
        for place_ref, returned in groups:
            places = [place_ref[k : k + 1, :] + j * capacity for k in range(place_ref.shape[0])]
            total += f32_dot(either(hits_at(returned.shape[0], places)), returned, ((0,), (0,)))
        out_ref[:, j * width : (j + 1) * width] = total.astype(jnp.bfloat16)


def send_block(block, r, experts):
    if r:
        block = lax.ppermute(block, ("row", "col"), [(i, i ^ r) for i in range(experts)])
    return block


def send_blocks(blocks, offsets, experts):
    return [send_block(block, r, experts) for block, r in zip(blocks, offsets)]


def shards(tokens, out_grad, expert_ids, gates, up_weight, down_weight):
    tok_rows, features = tokens.shape
    top_count = expert_ids.shape[1]
    units = up_weight.shape[2]
    columns = lax.axis_size("col") // 2
    experts = lax.axis_size("row") * lax.axis_size("col")
    capacity = 3 * tok_rows * top_count // (2 * experts)
    near = [r for r in range(experts) if not r & columns]
    far = [r for r in range(experts) if r & columns]
    blocks = len(near)
    size, width = PAIR * capacity, features // PAIR
    slots = blocks * capacity
    tile = min(units, 512)
    steps = units // tile
    bf16, f32 = jnp.bfloat16, jnp.float32
    shape = jax.ShapeDtypeStruct
    whole_block, half_block = shape((size, features), bf16), shape((size, width), bf16)
    place_shape = shape((top_count, tok_rows), jnp.int32)

    own_ids, own_gates = expert_ids.T, gates.T
    me = (lax.axis_index("row") * (2 * columns) + lax.axis_index("col")).astype(jnp.int32).reshape(1)

    smem = pl.BlockSpec(memory_space=pltpu.SMEM)
    vmem = pl.BlockSpec(memory_space=pltpu.VMEM)
    hbm = pl.BlockSpec(memory_space=pl.ANY)

    sent = pl.pallas_call(
        functools.partial(far_dispatch_kernel, capacity, columns, blocks),
        out_shape=(half_block,) * (2 * blocks) + (place_shape,),
        in_specs=[smem, vmem, vmem, vmem, vmem],
        compiler_params=params(),
        name="far_dispatch",
    )(me, own_ids, own_gates, tokens, out_grad)
    far_places = sent[-1]
    far_tokens = send_blocks(sent[:blocks], far, experts)
    far_grads = send_blocks(sent[blocks : 2 * blocks], far, experts)
    sent = pl.pallas_call(
        functools.partial(near_dispatch_kernel, capacity, columns, blocks),
        out_shape=(whole_block,) * blocks + (place_shape,),
        in_specs=[smem, vmem, vmem, vmem, vmem, vmem],
        compiler_params=params(),
        name="near_dispatch",
    )(me, own_ids, own_gates, tokens, out_grad, far_places)
    near_places = sent[-1]
    near_rows = send_blocks(sent[:blocks], near, experts)

    def fixed(rows, columns):
        return pl.BlockSpec((rows, columns), lambda i: (0, 0))

    up_spec = pl.BlockSpec((None, features, tile), lambda i: (0, 0, i))
    down_spec = pl.BlockSpec((None, tile, features), lambda i: (0, i, 0))
    hidden_spec = pl.BlockSpec((slots, tile), lambda i: (0, i))
    plain_spec, plain_shape = fixed(slots, features), shape((slots, features), bf16)
    plain, total = pltpu.VMEM((slots, features), bf16), pltpu.VMEM((slots, features), f32)
    whole_stack, half_stack = pltpu.VMEM((blocks * size, features), f32), pltpu.VMEM((blocks * size, width), f32)
    hidden_shape = shape((slots, units), bf16)

    done = pl.pallas_call(
        functools.partial(near_expert_kernel, capacity, blocks),
        out_shape=(hidden_shape, plain_shape) + (half_block,) * blocks,
        grid=(steps,),
        in_specs=[vmem] * blocks + [up_spec, down_spec],
        out_specs=(hidden_spec, plain_spec) + (fixed(size, width),) * blocks,
        scratch_shapes=[plain, total, whole_stack],
        compiler_params=params(),
        name="near_expert",
    )(*near_rows, up_weight, down_weight)
    near_hidden, near_plain = done[:2]
    near_back = send_blocks(done[2:], near, experts)

    far_hidden = pl.pallas_call(
        functools.partial(far_hidden_kernel, capacity, blocks),
        out_shape=hidden_shape,
        grid=(steps,),
        in_specs=[vmem] * blocks + [up_spec, hbm],
        out_specs=hidden_spec,
        scratch_shapes=[plain, half_stack],
        compiler_params=params(),
        name="far_hidden",
    )(*far_tokens, up_weight, near_plain)

    done = pl.pallas_call(
        functools.partial(far_row_grad_kernel, capacity, blocks),
        out_shape=(plain_shape,) + (half_block,) * blocks,
        grid=(steps,),
        in_specs=[vmem] * blocks + [up_spec, down_spec, hidden_spec],
        out_specs=(plain_spec,) + (fixed(size, width),) * blocks,
        scratch_shapes=[total, half_stack],
        compiler_params=params(),
        name="far_row_grad",
    )(*far_grads, up_weight, down_weight, far_hidden)
    far_plain = done[0]
    far_back = send_blocks(done[1:], far, experts)

    down_grad = pl.pallas_call(
        down_grad_kernel,
        out_shape=shape((1, units, features), bf16),
        grid=(steps,),
        in_specs=[plain_spec, plain_spec, hidden_spec, hidden_spec],
        out_specs=down_spec,
        compiler_params=params(),
        name="down_grad",
    )(near_plain, far_plain, near_hidden, far_hidden)

    one_stack = pltpu.VMEM((blocks * size, width), f32)
    input_grad = pl.pallas_call(
        functools.partial(pick_kernel, capacity, blocks),
        out_shape=shape((tok_rows, features), bf16),
        scratch_shapes=[one_stack, one_stack],
        compiler_params=params(),
        name="pick",
    )(*near_back, *far_back, near_places, far_places)
    return input_grad, down_grad


def pooled_shards(tokens, out_grad, expert_ids, gates, up_weight, down_weight):
    tok_rows = tokens.shape[0]
    top_count = expert_ids.shape[1]
    features = tokens.shape[1]
    groups = lax.axis_size("row")
    col_count = lax.axis_size("col")
    experts = groups * col_count
    capacity = 3 * tok_rows * top_count // (2 * experts)
    flat_ids = expert_ids.reshape(-1)
    onehot = (flat_ids[:, None] == jnp.arange(experts, dtype=jnp.int32)[None, :]).astype(jnp.int32)
    earlier = jnp.cumsum(onehot, axis=0) - onehot
    slot_index = jnp.sum(earlier * onehot, axis=1)
    target = flat_ids * capacity + slot_index
    placer = (jnp.arange(experts * capacity, dtype=jnp.int32)[:, None] == target[None, :]).astype(
        jnp.bfloat16
    )
    token_rows = jnp.repeat(tokens, top_count, axis=0)
    weighted = (
        gates.reshape(-1)[:, None] * jnp.repeat(out_grad, top_count, axis=0).astype(jnp.float32)
    ).astype(jnp.bfloat16)
    send_inputs = jnp.dot(placer, token_rows, preferred_element_type=jnp.float32).astype(
        jnp.bfloat16
    )
    send_grads = jnp.dot(placer, weighted, preferred_element_type=jnp.float32).astype(jnp.bfloat16)
    landed_inputs, landed_grads = (
        lax.all_to_all(
            send_inputs.reshape(experts, capacity, features),
            ("row", "col"),
            split_axis=0,
            concat_axis=0,
            tiled=True,
        ),
        lax.all_to_all(
            send_grads.reshape(experts, capacity, features),
            ("row", "col"),
            split_axis=0,
            concat_axis=0,
            tiled=True,
        ),
    )
    pooled_inputs, pooled_grads = (
        lax.all_gather(landed_inputs, "rep", axis=0, tiled=True),
        lax.all_gather(landed_grads, "rep", axis=0, tiled=True),
    )
    slot_rows = pooled_inputs.shape[0] * capacity
    input_rows = pooled_inputs.reshape(slot_rows, features)
    grad_rows = pooled_grads.reshape(slot_rows, features)
    up_block = up_weight[0]
    down_block = down_weight[0]
    preact = jnp.dot(input_rows, up_block, preferred_element_type=jnp.float32)
    hidden = jnp.maximum(preact, 0.0).astype(jnp.bfloat16)
    hidden_grad = lax.dot_general(
        grad_rows, down_block, (((1,), (1,)), ((), ())), preferred_element_type=jnp.float32
    )
    preact_grad = jnp.where(preact > 0, hidden_grad, 0.0).astype(jnp.bfloat16)
    weight_grad = lax.dot_general(
        hidden, grad_rows, (((0,), (0,)), ((), ())), preferred_element_type=jnp.float32
    )
    down_grad = weight_grad.astype(jnp.bfloat16)[None]
    summed_rows = lax.psum_scatter(
        lax.dot_general(
            preact_grad, up_block, (((1,), (1,)), ((), ())), preferred_element_type=jnp.float32
        ).astype(jnp.bfloat16),
        "rep",
        scatter_dimension=0,
        tiled=True,
    )
    returned = lax.all_to_all(
        summed_rows.reshape(experts, capacity, features),
        ("row", "col"),
        split_axis=0,
        concat_axis=0,
        tiled=True,
    )
    returned = returned.reshape(experts * capacity, features)
    picked = lax.dot_general(
        placer, returned, (((0,), (0,)), ((), ())), preferred_element_type=jnp.float32
    )
    input_grad = jnp.sum(picked.reshape(tok_rows, top_count, features), axis=1).astype(jnp.bfloat16)
    return (input_grad, down_grad)


def solution(mesh):
    by_token = P(("rep", "row", "col"), None)
    by_expert = (P(("row", "col"), None, "rep"), P(("row", "col"), "rep", None))
    return jax.shard_map(
        shards if mesh.shape["rep"] == 1 else pooled_shards,
        mesh=mesh,
        in_specs=(by_token,) * 4 + by_expert,
        out_specs=(by_token, by_expert[1]),
        check_vma=False,
    )
```

```python
import functools

import jax
import jax.numpy as jnp
from jax import lax
from jax.experimental import pallas as pl
from jax.experimental.pallas import tpu as pltpu
from jax.sharding import Mesh, PartitionSpec as P

VMEM_LIMIT = 16 * 1024 * 1024
PAIR = 2
TILE = 512
NOWHERE = -(1 << 20)


def f32_dot(lhs, rhs, contract=((1,), (0,))):
    return lax.dot_general(lhs, rhs, (contract, ((), ())), preferred_element_type=jnp.float32)


def params():
    return pltpu.CompilerParams(vmem_limit_bytes=VMEM_LIMIT)


def row_places(ids, names, capacity):
    tok_rows = ids.shape[1]
    index = lax.broadcasted_iota(jnp.int32, names.shape, 0)
    chosen = [names == ids[k : k + 1, :] for k in range(ids.shape[0])]
    member = functools.reduce(jnp.logical_or, chosen).astype(jnp.bfloat16)
    before = (
        lax.broadcasted_iota(jnp.int32, (tok_rows, tok_rows), 0)
        < lax.broadcasted_iota(jnp.int32, (tok_rows, tok_rows), 1)
    ).astype(jnp.bfloat16)
    rank = f32_dot(member, before).astype(jnp.int32)
    place = index * (PAIR * capacity) + rank - NOWHERE
    return [jnp.sum(jnp.where(pick, place, 0), axis=0, keepdims=True) + NOWHERE for pick in chosen]


def hits_at(rows, places):
    at = lax.broadcasted_iota(jnp.int32, (rows, places[0].shape[1]), 0)
    return [at == place for place in places]


def either(hits):
    return functools.reduce(jnp.logical_or, hits).astype(jnp.bfloat16)


def load_kernel(up_ref, down_ref, up_out, down_out, sems):
    parts = sems.shape[1]
    copies = []
    for n, (source, target) in enumerate(((up_ref, up_out), (down_ref, down_out))):
        size = source.shape[0] // parts
        for i in range(parts):
            at = pl.ds(i * size, size)
            copies.append(pltpu.make_async_copy(source.at[at], target.at[at], sems.at[n, i]))
    for copy in copies:
        copy.start()
    for copy in copies:
        copy.wait()


def dispatch_kernel(capacity, columns, half_ref, ids_ref, gates_ref, tokens_ref, grad_ref, *refs):
    out_ref = refs[-1]
    rows = out_ref.shape[0]
    ids, gates = ids_ref[...], gates_ref[...]
    index = lax.broadcasted_iota(jnp.int32, (rows // (PAIR * capacity), ids.shape[1]), 0)
    group = jnp.floor((index.astype(jnp.float32) + 0.5) * (1.0 / columns)).astype(jnp.int32)
    places = row_places(ids, index + (group + half_ref[0]) * columns, capacity)
    token_hits = hits_at(rows, places)
    grad_hits = hits_at(rows, [place + capacity for place in places])
    scales = [jnp.where(hit, gates[k : k + 1, :], 0.0) for k, hit in enumerate(grad_hits)]
    scale = jnp.sum(sum(scales), axis=1, keepdims=True)
    value = f32_dot(either(token_hits), tokens_ref[...]) + scale * f32_dot(either(grad_hits), grad_ref[...])
    out_ref[...] = value.astype(jnp.bfloat16)


def paired_rows(number, capacity):
    owner = jnp.floor((number.astype(jnp.float32) + 0.5) * (1.0 / capacity)).astype(jnp.int32)
    return number + owner * ((PAIR - 1) * capacity)


def taken(landed, j, capacity):
    rows = landed.shape[0]
    slots = rows // PAIR
    at = lax.broadcasted_iota(jnp.int32, (slots, rows), 1)
    source = paired_rows(lax.broadcasted_iota(jnp.int32, (slots, 1), 0), capacity) + j * capacity
    return f32_dot((at == source).astype(jnp.bfloat16), landed).astype(jnp.bfloat16)


def fold(plain, capacity):
    slots = plain.shape[0]
    rows, width = PAIR * slots, plain.shape[1] // PAIR
    at = lax.broadcasted_iota(jnp.int32, (rows, slots), 0)
    target = paired_rows(lax.broadcasted_iota(jnp.int32, (1, slots), 1), capacity)
    total = jnp.zeros((rows, width), jnp.float32)
    for j in range(PAIR):
        mover = (at == target + j * capacity).astype(jnp.bfloat16)
        total += f32_dot(mover, plain[:, j * width : (j + 1) * width])
    return total.astype(jnp.bfloat16)


def expert_kernel(capacity, landed_ref, up_ref, down_ref, hidden_ref, grads_ref, back_ref, rows_ref, sum_ref):
    landed = landed_ref[...]
    rows_ref[...] = taken(landed, 0, capacity)
    grads_ref[...] = taken(landed, 1, capacity)
    sum_ref[...] = jnp.zeros_like(sum_ref)
    units = up_ref.shape[1]
    tile = min(units, TILE)

    def step(i, carry):
        at = pl.ds(pl.multiple_of(i * tile, tile), tile)
        preact = f32_dot(rows_ref[...], up_ref[:, at])
        hidden_ref[:, at] = jnp.maximum(preact, 0.0).astype(jnp.bfloat16)
        hidden_grad = f32_dot(grads_ref[...], down_ref[at, :], ((1,), (1,)))
        preact_grad = jnp.where(preact > 0, hidden_grad, 0.0).astype(jnp.bfloat16)
        sum_ref[...] += f32_dot(preact_grad, up_ref[:, at], ((1,), (1,)))
        return carry

    lax.fori_loop(0, units // tile, step, 0)
    back_ref[...] = fold(sum_ref[...].astype(jnp.bfloat16), capacity)


def far_expert_kernel(capacity, columns, half_ref, own_ref, landed_ref, up_ref, down_ref, *refs):
    hidden_ref, grads_ref, both_ref, rows_ref, sum_ref, back_ref = refs
    expert_kernel(capacity, landed_ref, up_ref, down_ref, hidden_ref, grads_ref, back_ref, rows_ref, sum_ref)
    size = columns * PAIR * capacity
    for source, half in ((own_ref, half_ref[0]), (back_ref, 1 - half_ref[0])):
        for group in range(own_ref.shape[0] // size):
            target = pl.multiple_of((2 * group + half) * size, size)
            both_ref[pl.ds(target, size), :] = source[group * size : (group + 1) * size, :]


def down_grad_kernel(own_grads_ref, far_grads_ref, own_hidden_ref, far_hidden_ref, out_ref):
    own = f32_dot(own_hidden_ref[...], own_grads_ref[...], ((0,), (0,)))
    far = f32_dot(far_hidden_ref[...], far_grads_ref[...], ((0,), (0,)))
    out_ref[...] = (own + far).astype(jnp.bfloat16)


def pick_kernel(capacity, ids_ref, returned_ref, out_ref):
    rows, width = returned_ref.shape
    ids = ids_ref[...]
    names = lax.broadcasted_iota(jnp.int32, (rows // (PAIR * capacity), ids.shape[1]), 0)
    places = row_places(ids, names, capacity)
    for j in range(PAIR):
        chosen = either(hits_at(rows, [place + j * capacity for place in places]))
        total = f32_dot(chosen, returned_ref[...], ((0,), (0,)))
        out_ref[:, j * width : (j + 1) * width] = total.astype(jnp.bfloat16)


def exchange(rows, axes):
    peers = lax.axis_size(axes)
    cut = rows.reshape(peers, rows.shape[0] // peers, rows.shape[1])
    return lax.all_to_all(cut, axes, split_axis=0, concat_axis=0, tiled=True).reshape(rows.shape)


def swap(block):
    return lax.ppermute(block, "half", [(0, 1), (1, 0)])


def shards(tokens, out_grad, expert_ids, gates, up_weight, down_weight):
    tok_rows, features = tokens.shape
    top_count = expert_ids.shape[1]
    units = up_weight.shape[2]
    columns = lax.axis_size("col")
    peers = lax.axis_size(("row", "col"))
    capacity = 3 * tok_rows * top_count // (4 * peers)
    slots, rows, width = peers * capacity, peers * PAIR * capacity, features // PAIR
    bf16, f32 = jnp.bfloat16, jnp.float32
    shape = jax.ShapeDtypeStruct
    flops = 2 * slots * features * units
    weight_bytes = 2 * features * units

    def cost(matmuls, weights):
        return pl.CostEstimate(flops=matmuls * flops, bytes_accessed=weights * weight_bytes, transcendentals=0)

    own_ids, own_gates = expert_ids.T, gates.T
    far_tokens, far_grad = swap(tokens), swap(out_grad)
    far_ids, far_gates = swap(own_ids), swap(own_gates)
    half = lax.axis_index("half").astype(jnp.int32).reshape(1)

    smem = pl.BlockSpec(memory_space=pltpu.SMEM)
    vmem = pl.BlockSpec(memory_space=pltpu.VMEM)
    hbm = pl.BlockSpec(memory_space=pltpu.HBM)
    anywhere = pl.BlockSpec(memory_space=pl.ANY)

    up, down = pl.pallas_call(
        load_kernel,
        out_shape=(pltpu.VMEM((features, units), bf16), pltpu.VMEM((units, features), bf16)),
        in_specs=[hbm, hbm],
        out_specs=(vmem, vmem),
        scratch_shapes=[pltpu.SemaphoreType.DMA((2, 8))],
        compiler_params=params(),
        cost_estimate=cost(0, 2),
        name="load",
    )(*[pltpu.with_memory_space_constraint(weight[0], pltpu.HBM) for weight in (up_weight, down_weight)])

    def dispatch(ids, gates, tokens, out_grad, after, name):
        return pl.pallas_call(
            functools.partial(dispatch_kernel, capacity, columns),
            out_shape=shape((rows, features), bf16),
            in_specs=[smem, vmem, vmem, vmem, vmem] + [anywhere] * len(after),
            compiler_params=params(),
            name=name,
        )(half, ids, gates, tokens, out_grad, *after)

    landed_own = exchange(dispatch(own_ids, own_gates, tokens, out_grad, (), "own_dispatch"), ("row", "col"))
    landed_far = exchange(
        dispatch(far_ids, far_gates, far_tokens, far_grad, (landed_own, up), "far_dispatch"), ("row", "col")
    )

    hidden_shape, grads_shape = shape((slots, units), bf16), shape((slots, features), bf16)
    scratch = [pltpu.VMEM((slots, features), bf16), pltpu.VMEM((slots, features), f32)]
    own_hidden, own_grads, own_back = pl.pallas_call(
        functools.partial(expert_kernel, capacity),
        out_shape=(hidden_shape, grads_shape, shape((rows, width), bf16)),
        in_specs=[vmem, vmem, vmem],
        scratch_shapes=scratch,
        compiler_params=params(),
        cost_estimate=cost(3, 0),
        name="own_expert",
    )(landed_own, up, down)
    far_hidden, far_grads, back = pl.pallas_call(
        functools.partial(far_expert_kernel, capacity, columns),
        out_shape=(hidden_shape, grads_shape, shape((2 * rows, width), bf16)),
        in_specs=[smem, vmem, vmem, vmem, vmem],
        scratch_shapes=scratch + [pltpu.VMEM((rows, width), bf16)],
        compiler_params=params(),
        cost_estimate=cost(3, 0),
        name="far_expert",
    )(half, own_back, landed_far, up, down)
    returned = exchange(back, ("row", "half", "col"))

    tile = min(units, TILE)
    grads_spec = pl.BlockSpec((slots, features), lambda i: (0, 0))
    hidden_spec = pl.BlockSpec((slots, tile), lambda i: (0, i))
    down_grad = pl.pallas_call(
        down_grad_kernel,
        out_shape=shape((1, units, features), bf16),
        grid=(units // tile,),
        in_specs=[grads_spec, grads_spec, hidden_spec, hidden_spec],
        out_specs=pl.BlockSpec((None, tile, features), lambda i: (0, i, 0)),
        compiler_params=params(),
        cost_estimate=cost(2, 1),
        name="down_grad",
    )(own_grads, far_grads, own_hidden, far_hidden)

    input_grad = pl.pallas_call(
        functools.partial(pick_kernel, capacity),
        out_shape=shape((tok_rows, features), bf16),
        compiler_params=params(),
        name="pick",
    )(own_ids, returned)
    return input_grad, down_grad


def pooled_shards(tokens, out_grad, expert_ids, gates, up_weight, down_weight):
    tok_rows = tokens.shape[0]
    top_count = expert_ids.shape[1]
    features = tokens.shape[1]
    groups = lax.axis_size("row")
    col_count = lax.axis_size("col")
    experts = groups * col_count
    capacity = 3 * tok_rows * top_count // (2 * experts)
    flat_ids = expert_ids.reshape(-1)
    onehot = (flat_ids[:, None] == jnp.arange(experts, dtype=jnp.int32)[None, :]).astype(jnp.int32)
    earlier = jnp.cumsum(onehot, axis=0) - onehot
    slot_index = jnp.sum(earlier * onehot, axis=1)
    target = flat_ids * capacity + slot_index
    placer = (jnp.arange(experts * capacity, dtype=jnp.int32)[:, None] == target[None, :]).astype(
        jnp.bfloat16
    )
    token_rows = jnp.repeat(tokens, top_count, axis=0)
    weighted = (
        gates.reshape(-1)[:, None] * jnp.repeat(out_grad, top_count, axis=0).astype(jnp.float32)
    ).astype(jnp.bfloat16)
    send_inputs = jnp.dot(placer, token_rows, preferred_element_type=jnp.float32).astype(
        jnp.bfloat16
    )
    send_grads = jnp.dot(placer, weighted, preferred_element_type=jnp.float32).astype(jnp.bfloat16)
    landed_inputs, landed_grads = (
        lax.all_to_all(
            send_inputs.reshape(experts, capacity, features),
            ("row", "col"),
            split_axis=0,
            concat_axis=0,
            tiled=True,
        ),
        lax.all_to_all(
            send_grads.reshape(experts, capacity, features),
            ("row", "col"),
            split_axis=0,
            concat_axis=0,
            tiled=True,
        ),
    )
    pooled_inputs, pooled_grads = (
        lax.all_gather(landed_inputs, "rep", axis=0, tiled=True),
        lax.all_gather(landed_grads, "rep", axis=0, tiled=True),
    )
    slot_rows = pooled_inputs.shape[0] * capacity
    input_rows = pooled_inputs.reshape(slot_rows, features)
    grad_rows = pooled_grads.reshape(slot_rows, features)
    up_block = up_weight[0]
    down_block = down_weight[0]
    preact = jnp.dot(input_rows, up_block, preferred_element_type=jnp.float32)
    hidden = jnp.maximum(preact, 0.0).astype(jnp.bfloat16)
    hidden_grad = lax.dot_general(
        grad_rows, down_block, (((1,), (1,)), ((), ())), preferred_element_type=jnp.float32
    )
    preact_grad = jnp.where(preact > 0, hidden_grad, 0.0).astype(jnp.bfloat16)
    weight_grad = lax.dot_general(
        hidden, grad_rows, (((0,), (0,)), ((), ())), preferred_element_type=jnp.float32
    )
    down_grad = weight_grad.astype(jnp.bfloat16)[None]
    summed_rows = lax.psum_scatter(
        lax.dot_general(
            preact_grad, up_block, (((1,), (1,)), ((), ())), preferred_element_type=jnp.float32
        ).astype(jnp.bfloat16),
        "rep",
        scatter_dimension=0,
        tiled=True,
    )
    returned = lax.all_to_all(
        summed_rows.reshape(experts, capacity, features),
        ("row", "col"),
        split_axis=0,
        concat_axis=0,
        tiled=True,
    )
    returned = returned.reshape(experts * capacity, features)
    picked = lax.dot_general(
        placer, returned, (((0,), (0,)), ((), ())), preferred_element_type=jnp.float32
    )
    input_grad = jnp.sum(picked.reshape(tok_rows, top_count, features), axis=1).astype(jnp.bfloat16)
    return (input_grad, down_grad)


def solution(mesh):
    sizes = dict(mesh.shape)
    body, axes, owner = pooled_shards, mesh, ("row", "col")
    if sizes["rep"] == 1:
        cut = mesh.devices.reshape(1, sizes["row"], 2, sizes["col"] // 2)
        body, axes, owner = shards, Mesh(cut, ("rep", "row", "half", "col")), ("row", "half", "col")
    by_token = P(("rep",) + owner, None)
    by_expert = (P(owner, None, "rep"), P(owner, "rep", None))
    return jax.shard_map(
        body,
        mesh=axes,
        in_specs=(by_token,) * 4 + by_expert,
        out_specs=(by_token, by_expert[1]),
        check_vma=False,
    )
```

```python
import functools

import jax
import jax.numpy as jnp
from jax import lax
from jax.experimental import pallas as pl
from jax.experimental.pallas import tpu as pltpu
from jax.sharding import Mesh, PartitionSpec as P

VMEM_LIMIT = 36 * 1024 * 1024
PAIR = 2
TILE = 512
NOWHERE = -(1 << 20)


def f32_dot(lhs, rhs, contract=((1,), (0,))):
    return lax.dot_general(lhs, rhs, (contract, ((), ())), preferred_element_type=jnp.float32)


def params():
    return pltpu.CompilerParams(vmem_limit_bytes=VMEM_LIMIT)


def row_places(ids, names, capacity):
    tok_rows = ids.shape[1]
    index = lax.broadcasted_iota(jnp.int32, names.shape, 0)
    chosen = [names == ids[k : k + 1, :] for k in range(ids.shape[0])]
    member = functools.reduce(jnp.logical_or, chosen).astype(jnp.bfloat16)
    before = (
        lax.broadcasted_iota(jnp.int32, (tok_rows, tok_rows), 0)
        < lax.broadcasted_iota(jnp.int32, (tok_rows, tok_rows), 1)
    ).astype(jnp.bfloat16)
    rank = f32_dot(member, before).astype(jnp.int32)
    place = index * (PAIR * capacity) + rank - NOWHERE
    return [jnp.sum(jnp.where(pick, place, 0), axis=0, keepdims=True) + NOWHERE for pick in chosen]


def hits_at(rows, places):
    at = lax.broadcasted_iota(jnp.int32, (rows, places[0].shape[1]), 0)
    return [at == place for place in places]


def either(hits):
    return functools.reduce(jnp.logical_or, hits).astype(jnp.bfloat16)


def started(pairs, sems):
    copies = [pltpu.make_async_copy(*pair, sems.at[i]) for i, pair in enumerate(pairs)]
    for copy in copies:
        copy.start()
    return copies


def wait_all(copies):
    for copy in copies:
        copy.wait()


def dispatch_kernel(capacity, columns, half_ref, ids_ref, gates_ref, tokens_ref, grad_ref, out_ref):
    rows = out_ref.shape[0]
    ids, gates = ids_ref[...], gates_ref[...]
    index = lax.broadcasted_iota(jnp.int32, (rows // (PAIR * capacity), ids.shape[1]), 0)
    group = jnp.floor((index.astype(jnp.float32) + 0.5) * (1.0 / columns)).astype(jnp.int32)
    places = row_places(ids, index + (group + half_ref[0]) * columns, capacity)
    token_hits = hits_at(rows, places)
    grad_hits = hits_at(rows, [place + capacity for place in places])
    scales = [jnp.where(hit, gates[k : k + 1, :], 0.0) for k, hit in enumerate(grad_hits)]
    scale = jnp.sum(sum(scales), axis=1, keepdims=True)
    value = f32_dot(either(token_hits), tokens_ref[...]) + scale * f32_dot(either(grad_hits), grad_ref[...])
    out_ref[...] = value.astype(jnp.bfloat16)


def own_dispatch_kernel(capacity, columns, half_ref, *refs):
    sources, out_ref, held, sems = refs[:4], refs[4], refs[5:9], refs[9]
    wait_all(started(zip(sources, held), sems))
    dispatch_kernel(capacity, columns, half_ref, *held, out_ref)


def paired_rows(number, capacity):
    owner = jnp.floor((number.astype(jnp.float32) + 0.5) * (1.0 / capacity)).astype(jnp.int32)
    return number + owner * ((PAIR - 1) * capacity)


def taken(landed, j, capacity):
    rows = landed.shape[0]
    slots = rows // PAIR
    at = lax.broadcasted_iota(jnp.int32, (slots, rows), 1)
    source = paired_rows(lax.broadcasted_iota(jnp.int32, (slots, 1), 0), capacity) + j * capacity
    return f32_dot((at == source).astype(jnp.bfloat16), landed).astype(jnp.bfloat16)


def fold(plain, capacity):
    slots = plain.shape[0]
    rows, width = PAIR * slots, plain.shape[1] // PAIR
    at = lax.broadcasted_iota(jnp.int32, (rows, slots), 0)
    target = paired_rows(lax.broadcasted_iota(jnp.int32, (1, slots), 1), capacity)
    total = jnp.zeros((rows, width), jnp.float32)
    for j in range(PAIR):
        mover = (at == target + j * capacity).astype(jnp.bfloat16)
        total += f32_dot(mover, plain[:, j * width : (j + 1) * width])
    return total.astype(jnp.bfloat16)


def expert(capacity, landed_ref, up_ref, down_ref, hidden_out, grads_out, scratch):
    landed, up, down, rows, grads, hidden, total, weight_sems, hidden_sems, sems = scratch
    tile = up.shape[1] // weight_sems.shape[1]

    def tile_at(i):
        return pl.ds(pl.multiple_of(i * tile, tile), tile)

    def up_copy(i):
        return pltpu.make_async_copy(up_ref.at[:, tile_at(i)], up.at[:, tile_at(i)], weight_sems.at[0, i])

    def down_copy(i):
        return pltpu.make_async_copy(down_ref.at[tile_at(i)], down.at[tile_at(i)], weight_sems.at[1, i])

    def hidden_copy(i):
        return pltpu.make_async_copy(hidden.at[:, tile_at(i)], hidden_out.at[:, tile_at(i)], hidden_sems.at[i])

    arrival = pltpu.make_async_copy(landed_ref, landed, sems.at[0])
    arrival.start()
    steps = weight_sems.shape[1]
    for i in range(steps):
        up_copy(i).start()
        down_copy(i).start()
    total[...] = jnp.zeros_like(total)
    arrival.wait()
    mixed = landed[...]
    rows[...] = taken(mixed, 0, capacity)
    grads[...] = taken(mixed, 1, capacity)
    departure = pltpu.make_async_copy(grads, grads_out, sems.at[1])
    departure.start()

    def step(i, carry):
        at = tile_at(i)
        up_copy(i).wait()
        preact = f32_dot(rows[...], up[:, at])
        hidden[:, at] = jnp.maximum(preact, 0.0).astype(jnp.bfloat16)
        hidden_copy(i).start()
        down_copy(i).wait()
        hidden_grad = f32_dot(grads[...], down[at, :], ((1,), (1,)))
        preact_grad = jnp.where(preact > 0, hidden_grad, 0.0).astype(jnp.bfloat16)
        total[...] += f32_dot(preact_grad, up[:, at], ((1,), (1,)))
        return carry

    lax.fori_loop(0, steps, step, 0)
    departure.wait()
    for i in range(steps):
        hidden_copy(i).wait()
    return fold(total[...].astype(jnp.bfloat16), capacity)


def own_expert_kernel(capacity, landed_ref, up_ref, down_ref, hidden_out, grads_out, back_ref, *scratch):
    back_ref[...] = expert(capacity, landed_ref, up_ref, down_ref, hidden_out, grads_out, scratch)


def far_expert_kernel(capacity, columns, half_ref, own_ref, landed_ref, up_ref, down_ref, *refs):
    hidden_out, grads_out, both_out, both_ref, own_held, sems = refs[:6]
    arrival = pltpu.make_async_copy(own_ref, own_held, sems.at[0])
    arrival.start()
    back = expert(capacity, landed_ref, up_ref, down_ref, hidden_out, grads_out, refs[6:])
    arrival.wait()
    size = columns * PAIR * capacity
    for source, half in ((own_held, half_ref[0]), (back, 1 - half_ref[0])):
        for group in range(back.shape[0] // size):
            target = pl.multiple_of((2 * group + half) * size, size)
            both_ref[pl.ds(target, size), :] = source[group * size : (group + 1) * size, :]
    departure = pltpu.make_async_copy(both_ref, both_out, sems.at[1])
    departure.start()
    departure.wait()


def down_grad_kernel(own_grads_ref, far_grads_ref, own_hidden_ref, far_hidden_ref, out_ref):
    own = f32_dot(own_hidden_ref[...], own_grads_ref[...], ((0,), (0,)))
    far = f32_dot(far_hidden_ref[...], far_grads_ref[...], ((0,), (0,)))
    out_ref[...] = (own + far).astype(jnp.bfloat16)


def pick_kernel(capacity, ids_ref, returned_ref, out_ref):
    rows, width = returned_ref.shape
    ids = ids_ref[...]
    names = lax.broadcasted_iota(jnp.int32, (rows // (PAIR * capacity), ids.shape[1]), 0)
    places = row_places(ids, names, capacity)
    for j in range(PAIR):
        chosen = either(hits_at(rows, [place + j * capacity for place in places]))
        total = f32_dot(chosen, returned_ref[...], ((0,), (0,)))
        out_ref[:, j * width : (j + 1) * width] = total.astype(jnp.bfloat16)


def exchange(rows, axes):
    peers = lax.axis_size(axes)
    cut = rows.reshape(peers, rows.shape[0] // peers, rows.shape[1])
    return lax.all_to_all(cut, axes, split_axis=0, concat_axis=0, tiled=True).reshape(rows.shape)


def swap(block):
    return lax.ppermute(block, "half", [(0, 1), (1, 0)])


def shards(tokens, out_grad, expert_ids, gates, up_weight, down_weight):
    tok_rows, features = tokens.shape
    top_count = expert_ids.shape[1]
    units = up_weight.shape[2]
    columns = lax.axis_size("col")
    peers = lax.axis_size(("row", "col"))
    capacity = 3 * tok_rows * top_count // (4 * peers)
    slots, rows, width = peers * capacity, peers * PAIR * capacity, features // PAIR
    bf16, f32 = jnp.bfloat16, jnp.float32
    shape = jax.ShapeDtypeStruct
    flops = 2 * slots * features * units
    weight_bytes = 2 * features * units

    def cost(matmuls, weights):
        return pl.CostEstimate(flops=matmuls * flops, bytes_accessed=weights * weight_bytes, transcendentals=0)

    own_ids, own_gates = expert_ids.T, gates.T
    far_tokens, far_grad = swap(tokens), swap(out_grad)
    far_ids, far_gates = swap(own_ids), swap(own_gates)
    half = lax.axis_index("half").astype(jnp.int32).reshape(1)

    smem = pl.BlockSpec(memory_space=pltpu.SMEM)
    vmem = pl.BlockSpec(memory_space=pltpu.VMEM)
    hbm = pl.BlockSpec(memory_space=pltpu.HBM)

    def in_hbm(array):
        return pltpu.with_memory_space_constraint(array, pltpu.HBM)

    def held(rows, columns, kind=bf16):
        return pltpu.VMEM((rows, columns), kind)

    send_own = pl.pallas_call(
        functools.partial(own_dispatch_kernel, capacity, columns),
        out_shape=shape((rows, features), bf16),
        in_specs=[smem, hbm, hbm, hbm, hbm],
        scratch_shapes=[
            held(top_count, tok_rows, jnp.int32),
            held(top_count, tok_rows, f32),
            held(tok_rows, features),
            held(tok_rows, features),
            pltpu.SemaphoreType.DMA((4,)),
        ],
        compiler_params=params(),
        name="own_dispatch",
    )(half, *[in_hbm(array) for array in (own_ids, own_gates, tokens, out_grad)])
    landed_own = exchange(send_own, ("row", "col"))

    send_far = pl.pallas_call(
        functools.partial(dispatch_kernel, capacity, columns),
        out_shape=shape((rows, features), bf16),
        in_specs=[smem, vmem, vmem, vmem, vmem],
        compiler_params=params(),
        cost_estimate=cost(64, 64),
        name="far_dispatch",
    )(half, far_ids, far_gates, far_tokens, far_grad)
    landed_far = exchange(send_far, ("row", "col"))

    tile = min(units, TILE)
    steps = units // tile
    weights = in_hbm(up_weight[0]), in_hbm(down_weight[0])
    results = pltpu.HBM((slots, units), bf16), pltpu.HBM((slots, features), bf16)
    scratch = [
        held(rows, features),
        held(features, units),
        held(units, features),
        held(slots, features),
        held(slots, features),
        held(slots, units),
        held(slots, features, f32),
        pltpu.SemaphoreType.DMA((2, steps)),
        pltpu.SemaphoreType.DMA((steps,)),
        pltpu.SemaphoreType.DMA((2,)),
    ]
    own_hidden, own_grads, own_back = pl.pallas_call(
        functools.partial(own_expert_kernel, capacity),
        out_shape=results + (shape((rows, width), bf16),),
        in_specs=[hbm, hbm, hbm],
        out_specs=(hbm, hbm, vmem),
        scratch_shapes=scratch,
        compiler_params=params(),
        cost_estimate=cost(3, 2),
        name="own_expert",
    )(in_hbm(landed_own), *weights)
    far_hidden, far_grads, back = pl.pallas_call(
        functools.partial(far_expert_kernel, capacity, columns),
        out_shape=results + (pltpu.HBM((2 * rows, width), bf16),),
        in_specs=[smem, hbm, hbm, hbm, hbm],
        out_specs=(hbm, hbm, hbm),
        scratch_shapes=[held(2 * rows, width), held(rows, width), pltpu.SemaphoreType.DMA((2,))] + scratch,
        compiler_params=params(),
        cost_estimate=cost(3, 2),
        name="far_expert",
    )(half, own_back, in_hbm(landed_far), *weights)
    returned = exchange(back, ("row", "half", "col"))

    grads_spec = pl.BlockSpec((slots, features), lambda i: (0, 0))
    hidden_spec = pl.BlockSpec((slots, tile), lambda i: (0, i))
    down_grad = pl.pallas_call(
        down_grad_kernel,
        out_shape=shape((1, units, features), bf16),
        grid=(steps,),
        in_specs=[grads_spec, grads_spec, hidden_spec, hidden_spec],
        out_specs=pl.BlockSpec((None, tile, features), lambda i: (0, i, 0)),
        compiler_params=params(),
        cost_estimate=cost(2, 1),
        name="down_grad",
    )(*[in_hbm(array) for array in (own_grads, far_grads, own_hidden, far_hidden)])

    input_grad = pl.pallas_call(
        functools.partial(pick_kernel, capacity),
        out_shape=shape((tok_rows, features), bf16),
        compiler_params=params(),
        name="pick",
    )(own_ids, returned)
    return input_grad, down_grad


def pooled_shards(tokens, out_grad, expert_ids, gates, up_weight, down_weight):
    tok_rows = tokens.shape[0]
    top_count = expert_ids.shape[1]
    features = tokens.shape[1]
    groups = lax.axis_size("row")
    col_count = lax.axis_size("col")
    experts = groups * col_count
    capacity = 3 * tok_rows * top_count // (2 * experts)
    flat_ids = expert_ids.reshape(-1)
    onehot = (flat_ids[:, None] == jnp.arange(experts, dtype=jnp.int32)[None, :]).astype(jnp.int32)
    earlier = jnp.cumsum(onehot, axis=0) - onehot
    slot_index = jnp.sum(earlier * onehot, axis=1)
    target = flat_ids * capacity + slot_index
    placer = (jnp.arange(experts * capacity, dtype=jnp.int32)[:, None] == target[None, :]).astype(
        jnp.bfloat16
    )
    token_rows = jnp.repeat(tokens, top_count, axis=0)
    weighted = (
        gates.reshape(-1)[:, None] * jnp.repeat(out_grad, top_count, axis=0).astype(jnp.float32)
    ).astype(jnp.bfloat16)
    send_inputs = jnp.dot(placer, token_rows, preferred_element_type=jnp.float32).astype(
        jnp.bfloat16
    )
    send_grads = jnp.dot(placer, weighted, preferred_element_type=jnp.float32).astype(jnp.bfloat16)
    landed_inputs, landed_grads = (
        lax.all_to_all(
            send_inputs.reshape(experts, capacity, features),
            ("row", "col"),
            split_axis=0,
            concat_axis=0,
            tiled=True,
        ),
        lax.all_to_all(
            send_grads.reshape(experts, capacity, features),
            ("row", "col"),
            split_axis=0,
            concat_axis=0,
            tiled=True,
        ),
    )
    pooled_inputs, pooled_grads = (
        lax.all_gather(landed_inputs, "rep", axis=0, tiled=True),
        lax.all_gather(landed_grads, "rep", axis=0, tiled=True),
    )
    slot_rows = pooled_inputs.shape[0] * capacity
    input_rows = pooled_inputs.reshape(slot_rows, features)
    grad_rows = pooled_grads.reshape(slot_rows, features)
    up_block = up_weight[0]
    down_block = down_weight[0]
    preact = jnp.dot(input_rows, up_block, preferred_element_type=jnp.float32)
    hidden = jnp.maximum(preact, 0.0).astype(jnp.bfloat16)
    hidden_grad = lax.dot_general(
        grad_rows, down_block, (((1,), (1,)), ((), ())), preferred_element_type=jnp.float32
    )
    preact_grad = jnp.where(preact > 0, hidden_grad, 0.0).astype(jnp.bfloat16)
    weight_grad = lax.dot_general(
        hidden, grad_rows, (((0,), (0,)), ((), ())), preferred_element_type=jnp.float32
    )
    down_grad = weight_grad.astype(jnp.bfloat16)[None]
    summed_rows = lax.psum_scatter(
        lax.dot_general(
            preact_grad, up_block, (((1,), (1,)), ((), ())), preferred_element_type=jnp.float32
        ).astype(jnp.bfloat16),
        "rep",
        scatter_dimension=0,
        tiled=True,
    )
    returned = lax.all_to_all(
        summed_rows.reshape(experts, capacity, features),
        ("row", "col"),
        split_axis=0,
        concat_axis=0,
        tiled=True,
    )
    returned = returned.reshape(experts * capacity, features)
    picked = lax.dot_general(
        placer, returned, (((0,), (0,)), ((), ())), preferred_element_type=jnp.float32
    )
    input_grad = jnp.sum(picked.reshape(tok_rows, top_count, features), axis=1).astype(jnp.bfloat16)
    return (input_grad, down_grad)


def solution(mesh):
    sizes = dict(mesh.shape)
    body, axes, owner = pooled_shards, mesh, ("row", "col")
    if sizes["rep"] == 1:
        cut = mesh.devices.reshape(1, sizes["row"], 2, sizes["col"] // 2)
        body, axes, owner = shards, Mesh(cut, ("rep", "row", "half", "col")), ("row", "half", "col")
    by_token = P(("rep",) + owner, None)
    by_expert = (P(owner, None, "rep"), P(owner, "rep", None))
    return jax.shard_map(
        body,
        mesh=axes,
        in_specs=(by_token,) * 4 + by_expert,
        out_specs=(by_token, by_expert[1]),
        check_vma=False,
    )
```

```python
import functools

import jax
import jax.numpy as jnp
from jax import lax
from jax.experimental import pallas as pl
from jax.experimental.pallas import tpu as pltpu
from jax.sharding import PartitionSpec as P

VMEM_LIMIT = 44 * 1024 * 1024
PAIR = 2
TILE = 512
AHEAD = 3
NOWHERE = -(1 << 20)


def f32_dot(lhs, rhs, contract=((1,), (0,))):
    return lax.dot_general(lhs, rhs, (contract, ((), ())), preferred_element_type=jnp.float32)


def params():
    return pltpu.CompilerParams(vmem_limit_bytes=VMEM_LIMIT)


def row_places(ids, experts, capacity):
    tok_rows = ids.shape[1]
    names = lax.broadcasted_iota(jnp.int32, (experts, tok_rows), 0)
    chosen = [names == ids[k : k + 1, :] for k in range(ids.shape[0])]
    member = functools.reduce(jnp.logical_or, chosen).astype(jnp.bfloat16)
    before = (
        lax.broadcasted_iota(jnp.int32, (tok_rows, tok_rows), 0)
        < lax.broadcasted_iota(jnp.int32, (tok_rows, tok_rows), 1)
    ).astype(jnp.bfloat16)
    rank = f32_dot(member, before).astype(jnp.int32)
    place = names * (PAIR * capacity) + rank
    return [jnp.sum(jnp.where(pick, place, 0), axis=0, keepdims=True) for pick in chosen]


def hits_at(rows, places):
    at = lax.broadcasted_iota(jnp.int32, (rows, places[0].shape[1]), 0)
    return [at == place for place in places]


def either(hits):
    return functools.reduce(jnp.logical_or, hits).astype(jnp.bfloat16)


def started(pairs, sems):
    copies = [pltpu.make_async_copy(*pair, sems.at[i]) for i, pair in enumerate(pairs)]
    for copy in copies:
        copy.start()
    return copies


def dispatch_kernel(capacity, *refs):
    sources, out_ref, held, sems = refs[:4], refs[4], refs[5:9], refs[9]
    ids_copy, gates_copy, tokens_copy, grad_copy = started(zip(sources, held), sems)
    ids_ref, gates_ref, tokens_ref, grad_ref = held
    rows = out_ref.shape[0]
    ids_copy.wait()
    places = row_places(ids_ref[...], rows // (PAIR * capacity), capacity)
    token_hits = hits_at(rows, places)
    grad_hits = hits_at(rows, [place + capacity for place in places])
    gates_copy.wait()
    scales = [jnp.where(hit, gates_ref[k : k + 1, :], 0.0) for k, hit in enumerate(grad_hits)]
    scale = jnp.sum(sum(scales), axis=1, keepdims=True)
    tokens_copy.wait()
    grad_copy.wait()
    value = f32_dot(either(token_hits), tokens_ref[...]) + scale * f32_dot(either(grad_hits), grad_ref[...])
    out_ref[...] = value.astype(jnp.bfloat16)


def paired_rows(number, capacity):
    owner = jnp.floor((number.astype(jnp.float32) + 0.5) * (1.0 / capacity)).astype(jnp.int32)
    return number + owner * ((PAIR - 1) * capacity)


def group_size(peers, capacity):
    size = 1
    while peers % (2 * size) == 0 and size * PAIR * capacity < 192:
        size *= 2
    return size


def take_rows(landed_ref, j, capacity, rows_ref):
    size = group_size(landed_ref.shape[0] // (PAIR * capacity), capacity)
    slots, rows = size * capacity, size * PAIR * capacity
    at = lax.broadcasted_iota(jnp.int32, (slots, rows), 1)
    source = paired_rows(lax.broadcasted_iota(jnp.int32, (slots, 1), 0), capacity) + j * capacity
    mover = (at == source).astype(jnp.bfloat16)
    for i in range(rows_ref.shape[0] // slots):
        taken = f32_dot(mover, landed_ref[i * rows : (i + 1) * rows, :])
        rows_ref[i * slots : (i + 1) * slots, :] = taken.astype(jnp.bfloat16)


def fold_rows(plain_ref, capacity, folded_ref):
    size = group_size(plain_ref.shape[0] // capacity, capacity)
    slots, rows = size * capacity, size * PAIR * capacity
    width = folded_ref.shape[1]
    at = lax.broadcasted_iota(jnp.int32, (rows, slots), 0)
    target = paired_rows(lax.broadcasted_iota(jnp.int32, (1, slots), 1), capacity)
    movers = [(at == target + j * capacity).astype(jnp.bfloat16) for j in range(PAIR)]
    for i in range(plain_ref.shape[0] // slots):
        plain = plain_ref[i * slots : (i + 1) * slots, :].astype(jnp.bfloat16)
        parts = [f32_dot(mover, plain[:, j * width : (j + 1) * width]) for j, mover in enumerate(movers)]
        folded_ref[i * rows : (i + 1) * rows, :] = sum(parts).astype(jnp.bfloat16)


def expert_kernel(capacity, landed_ref, up_ref, down_ref, hidden_out, grads_out, back_out, *scratch):
    landed, up, down, rows, grads, hidden, total, back, weight_sems, hidden_sems, sems = scratch
    steps = weight_sems.shape[1]
    tile = up.shape[1] // steps

    def tile_at(i):
        return pl.ds(pl.multiple_of(i * tile, tile), tile)

    def up_copy(i):
        return pltpu.make_async_copy(up_ref.at[:, tile_at(i)], up.at[:, tile_at(i)], weight_sems.at[0, i])

    def down_copy(i):
        return pltpu.make_async_copy(down_ref.at[tile_at(i)], down.at[tile_at(i)], weight_sems.at[1, i])

    def hidden_copy(i):
        return pltpu.make_async_copy(hidden.at[:, tile_at(i)], hidden_out.at[:, tile_at(i)], hidden_sems.at[i])

    arrival = pltpu.make_async_copy(landed_ref, landed, sems.at[0])
    arrival.start()
    for i in range(min(AHEAD, steps)):
        up_copy(i).start()
        down_copy(i).start()
    total[...] = jnp.zeros_like(total)
    arrival.wait()
    take_rows(landed, 0, capacity, rows)
    take_rows(landed, 1, capacity, grads)
    departure = pltpu.make_async_copy(grads, grads_out, sems.at[1])
    departure.start()

    def step(i, carry):
        @pl.when(i + AHEAD < steps)
        def _():
            up_copy(i + AHEAD).start()
            down_copy(i + AHEAD).start()

        at = tile_at(i)
        up_copy(i).wait()
        preact = f32_dot(rows[...], up[:, at])
        hidden[:, at] = jnp.maximum(preact, 0.0).astype(jnp.bfloat16)
        hidden_copy(i).start()
        down_copy(i).wait()
        hidden_grad = f32_dot(grads[...], down[at, :], ((1,), (1,)))
        preact_grad = jnp.where(preact > 0, hidden_grad, 0.0).astype(jnp.bfloat16)
        total[...] += f32_dot(preact_grad, up[:, at], ((1,), (1,)))
        return carry

    lax.fori_loop(0, steps, step, 0)
    fold_rows(total, capacity, back)
    last = pltpu.make_async_copy(back, back_out, sems.at[2])
    last.start()
    departure.wait()
    for i in range(steps):
        hidden_copy(i).wait()
    last.wait()


def down_grad_kernel(grads_ref, hidden_ref, out_ref):
    out_ref[...] = f32_dot(hidden_ref[...], grads_ref[...], ((0,), (0,))).astype(jnp.bfloat16)


def pick_kernel(capacity, ids_ref, returned_ref, out_ref):
    rows, width = returned_ref.shape
    places = row_places(ids_ref[...], rows // (PAIR * capacity), capacity)
    for j in range(PAIR):
        chosen = either(hits_at(rows, [place + j * capacity for place in places]))
        total = f32_dot(chosen, returned_ref[...], ((0,), (0,)))
        out_ref[:, j * width : (j + 1) * width] = total.astype(jnp.bfloat16)


def exchange(rows):
    axes = ("row", "col")
    peers = lax.axis_size(axes)
    cut = rows.reshape(peers, rows.shape[0] // peers, rows.shape[1])
    return lax.all_to_all(cut, axes, split_axis=0, concat_axis=0, tiled=True).reshape(rows.shape)


def in_hbm(array):
    return pltpu.with_memory_space_constraint(array, pltpu.HBM)


def held(rows, columns, kind=jnp.bfloat16):
    return pltpu.VMEM((rows, columns), kind)


def shards(tokens, out_grad, expert_ids, gates, up_weight, down_weight):
    tok_rows, features = tokens.shape
    top_count = expert_ids.shape[1]
    units = up_weight.shape[2]
    peers = lax.axis_size(("row", "col"))
    capacity = 3 * tok_rows * top_count // (2 * peers)
    slots, rows, width = peers * capacity, peers * PAIR * capacity, features // PAIR
    tile = min(units, TILE)
    steps = units // tile
    bf16, f32 = jnp.bfloat16, jnp.float32
    shape = jax.ShapeDtypeStruct
    dma = pltpu.SemaphoreType.DMA
    flops = 2 * slots * features * units
    weight_bytes = 2 * features * units

    def cost(matmuls, weights):
        return pl.CostEstimate(flops=matmuls * flops, bytes_accessed=weights * weight_bytes, transcendentals=0)

    ids = expert_ids.T
    hbm = pl.BlockSpec(memory_space=pltpu.HBM)
    anywhere = pl.BlockSpec(memory_space=pl.ANY)

    sent = pl.pallas_call(
        functools.partial(dispatch_kernel, capacity),
        out_shape=shape((rows, features), bf16),
        in_specs=[hbm, hbm, hbm, hbm],
        scratch_shapes=[
            held(top_count, tok_rows, jnp.int32),
            held(top_count, tok_rows, f32),
            held(tok_rows, features),
            held(tok_rows, features),
            dma((4,)),
        ],
        compiler_params=params(),
        name="dispatch",
    )(*[in_hbm(array) for array in (ids, gates.T, tokens, out_grad)])
    landed = exchange(sent)

    hidden, grads, back = pl.pallas_call(
        functools.partial(expert_kernel, capacity),
        out_shape=(
            pltpu.HBM((slots, units), bf16),
            pltpu.HBM((slots, features), bf16),
            pltpu.HBM((rows, width), bf16),
        ),
        in_specs=[anywhere, hbm, hbm],
        out_specs=(hbm, hbm, hbm),
        scratch_shapes=[
            held(rows, features),
            held(features, units),
            held(units, features),
            held(slots, features),
            held(slots, features),
            held(slots, units),
            held(slots, features, f32),
            held(rows, width),
            dma((2, steps)),
            dma((steps,)),
            dma((3,)),
        ],
        compiler_params=params(),
        cost_estimate=cost(3, 2),
        name="expert",
    )(landed, in_hbm(up_weight[0]), in_hbm(down_weight[0]))
    returned = exchange(back)

    down_grad = pl.pallas_call(
        down_grad_kernel,
        out_shape=shape((1, units, features), bf16),
        grid=(steps,),
        in_specs=[pl.BlockSpec((slots, features), lambda i: (0, 0)), pl.BlockSpec((slots, tile), lambda i: (0, i))],
        out_specs=pl.BlockSpec((None, tile, features), lambda i: (0, i, 0)),
        compiler_params=params(),
        cost_estimate=cost(1, 1),
        name="down_grad",
    )(in_hbm(grads), in_hbm(hidden))

    input_grad = pl.pallas_call(
        functools.partial(pick_kernel, capacity),
        out_shape=shape((tok_rows, features), bf16),
        compiler_params=params(),
        name="pick",
    )(ids, returned)
    return input_grad, down_grad


def pooled_shards(tokens, out_grad, expert_ids, gates, up_weight, down_weight):
    tok_rows = tokens.shape[0]
    top_count = expert_ids.shape[1]
    features = tokens.shape[1]
    groups = lax.axis_size("row")
    col_count = lax.axis_size("col")
    experts = groups * col_count
    capacity = 3 * tok_rows * top_count // (2 * experts)
    flat_ids = expert_ids.reshape(-1)
    onehot = (flat_ids[:, None] == jnp.arange(experts, dtype=jnp.int32)[None, :]).astype(jnp.int32)
    earlier = jnp.cumsum(onehot, axis=0) - onehot
    slot_index = jnp.sum(earlier * onehot, axis=1)
    target = flat_ids * capacity + slot_index
    placer = (jnp.arange(experts * capacity, dtype=jnp.int32)[:, None] == target[None, :]).astype(
        jnp.bfloat16
    )
    token_rows = jnp.repeat(tokens, top_count, axis=0)
    weighted = (
        gates.reshape(-1)[:, None] * jnp.repeat(out_grad, top_count, axis=0).astype(jnp.float32)
    ).astype(jnp.bfloat16)
    send_inputs = jnp.dot(placer, token_rows, preferred_element_type=jnp.float32).astype(
        jnp.bfloat16
    )
    send_grads = jnp.dot(placer, weighted, preferred_element_type=jnp.float32).astype(jnp.bfloat16)
    landed_inputs, landed_grads = (
        lax.all_to_all(
            send_inputs.reshape(experts, capacity, features),
            ("row", "col"),
            split_axis=0,
            concat_axis=0,
            tiled=True,
        ),
        lax.all_to_all(
            send_grads.reshape(experts, capacity, features),
            ("row", "col"),
            split_axis=0,
            concat_axis=0,
            tiled=True,
        ),
    )
    pooled_inputs, pooled_grads = (
        lax.all_gather(landed_inputs, "rep", axis=0, tiled=True),
        lax.all_gather(landed_grads, "rep", axis=0, tiled=True),
    )
    slot_rows = pooled_inputs.shape[0] * capacity
    input_rows = pooled_inputs.reshape(slot_rows, features)
    grad_rows = pooled_grads.reshape(slot_rows, features)
    up_block = up_weight[0]
    down_block = down_weight[0]
    preact = jnp.dot(input_rows, up_block, preferred_element_type=jnp.float32)
    hidden = jnp.maximum(preact, 0.0).astype(jnp.bfloat16)
    hidden_grad = lax.dot_general(
        grad_rows, down_block, (((1,), (1,)), ((), ())), preferred_element_type=jnp.float32
    )
    preact_grad = jnp.where(preact > 0, hidden_grad, 0.0).astype(jnp.bfloat16)
    weight_grad = lax.dot_general(
        hidden, grad_rows, (((0,), (0,)), ((), ())), preferred_element_type=jnp.float32
    )
    down_grad = weight_grad.astype(jnp.bfloat16)[None]
    summed_rows = lax.psum_scatter(
        lax.dot_general(
            preact_grad, up_block, (((1,), (1,)), ((), ())), preferred_element_type=jnp.float32
        ).astype(jnp.bfloat16),
        "rep",
        scatter_dimension=0,
        tiled=True,
    )
    returned = lax.all_to_all(
        summed_rows.reshape(experts, capacity, features),
        ("row", "col"),
        split_axis=0,
        concat_axis=0,
        tiled=True,
    )
    returned = returned.reshape(experts * capacity, features)
    picked = lax.dot_general(
        placer, returned, (((0,), (0,)), ((), ())), preferred_element_type=jnp.float32
    )
    input_grad = jnp.sum(picked.reshape(tok_rows, top_count, features), axis=1).astype(jnp.bfloat16)
    return (input_grad, down_grad)


def solution(mesh):
    by_token = P(("rep", "row", "col"), None)
    by_expert = (P(("row", "col"), None, "rep"), P(("row", "col"), "rep", None))
    return jax.shard_map(
        shards if mesh.shape["rep"] == 1 else pooled_shards,
        mesh=mesh,
        in_specs=(by_token,) * 4 + by_expert,
        out_specs=(by_token, by_expert[1]),
        check_vma=False,
    )
```

```python
import functools

import jax
import jax.numpy as jnp
from jax import lax
from jax.experimental import pallas as pl
from jax.experimental.pallas import tpu as pltpu
from jax.sharding import Mesh, PartitionSpec as P

VMEM_LIMIT = 40 * 1024 * 1024
PAIR = 2
TILE = 512
AHEAD = 3
NOWHERE = -(1 << 20)


def f32_dot(lhs, rhs, contract=((1,), (0,))):
    return lax.dot_general(lhs, rhs, (contract, ((), ())), preferred_element_type=jnp.float32)


def params():
    return pltpu.CompilerParams(vmem_limit_bytes=VMEM_LIMIT)


def row_places(ids, names, capacity):
    tok_rows = ids.shape[1]
    index = lax.broadcasted_iota(jnp.int32, names.shape, 0)
    chosen = [names == ids[k : k + 1, :] for k in range(ids.shape[0])]
    member = functools.reduce(jnp.logical_or, chosen).astype(jnp.bfloat16)
    before = (
        lax.broadcasted_iota(jnp.int32, (tok_rows, tok_rows), 0)
        < lax.broadcasted_iota(jnp.int32, (tok_rows, tok_rows), 1)
    ).astype(jnp.bfloat16)
    rank = f32_dot(member, before).astype(jnp.int32)
    place = index * (PAIR * capacity) + rank - NOWHERE
    return [jnp.sum(jnp.where(pick, place, 0), axis=0, keepdims=True) + NOWHERE for pick in chosen]


def hits_at(rows, places):
    at = lax.broadcasted_iota(jnp.int32, (rows, places[0].shape[1]), 0)
    return [at == place for place in places]


def either(hits):
    return functools.reduce(jnp.logical_or, hits).astype(jnp.bfloat16)


def started(pairs, sems):
    copies = [pltpu.make_async_copy(*pair, sems.at[i]) for i, pair in enumerate(pairs)]
    for copy in copies:
        copy.start()
    return copies


def dispatch_kernel(capacity, columns, far, half_ref, ids_ref, gates_ref, *refs):
    sources, out_ref, held, sems = refs[:2], refs[2], refs[3:5], refs[5]
    half = half_ref[0]
    tokens_ref, grad_ref = held
    tok_rows = tokens_ref.shape[0]
    if far:
        block = pl.ds(pl.multiple_of((1 - half) * tok_rows, tok_rows), tok_rows)
        sources = [source.at[block] for source in sources]
    tokens_copy, grad_copy = started(zip(sources, held), sems)
    rows = out_ref.shape[0]
    index = lax.broadcasted_iota(jnp.int32, (rows // (PAIR * capacity), tok_rows), 0)
    group = jnp.floor((index.astype(jnp.float32) + 0.5) * (1.0 / columns)).astype(jnp.int32)
    places = row_places(ids_ref[...], index + (group + half) * columns, capacity)
    token_hits = hits_at(rows, places)
    grad_hits = hits_at(rows, [place + capacity for place in places])
    scales = [jnp.where(hit, gates_ref[k : k + 1, :], 0.0) for k, hit in enumerate(grad_hits)]
    scale = jnp.sum(sum(scales), axis=1, keepdims=True)
    tokens_copy.wait()
    grad_copy.wait()
    value = f32_dot(either(token_hits), tokens_ref[...]) + scale * f32_dot(either(grad_hits), grad_ref[...])
    out_ref[...] = value.astype(jnp.bfloat16)


def paired_rows(number, capacity):
    owner = jnp.floor((number.astype(jnp.float32) + 0.5) * (1.0 / capacity)).astype(jnp.int32)
    return number + owner * ((PAIR - 1) * capacity)


def group_size(peers, capacity):
    size = 1
    while peers % (2 * size) == 0 and size * PAIR * capacity < 192:
        size *= 2
    return size


def take_rows(landed_ref, j, capacity, rows_ref):
    size = group_size(landed_ref.shape[0] // (PAIR * capacity), capacity)
    slots, rows = size * capacity, size * PAIR * capacity
    at = lax.broadcasted_iota(jnp.int32, (slots, rows), 1)
    source = paired_rows(lax.broadcasted_iota(jnp.int32, (slots, 1), 0), capacity) + j * capacity
    mover = (at == source).astype(jnp.bfloat16)
    for i in range(rows_ref.shape[0] // slots):
        taken = f32_dot(mover, landed_ref[i * rows : (i + 1) * rows, :])
        rows_ref[i * slots : (i + 1) * slots, :] = taken.astype(jnp.bfloat16)


def fold_rows(plain_ref, capacity, folded_ref):
    size = group_size(plain_ref.shape[0] // capacity, capacity)
    slots, rows = size * capacity, size * PAIR * capacity
    width = folded_ref.shape[1]
    at = lax.broadcasted_iota(jnp.int32, (rows, slots), 0)
    target = paired_rows(lax.broadcasted_iota(jnp.int32, (1, slots), 1), capacity)
    movers = [(at == target + j * capacity).astype(jnp.bfloat16) for j in range(PAIR)]
    for i in range(plain_ref.shape[0] // slots):
        plain = plain_ref[i * slots : (i + 1) * slots, :].astype(jnp.bfloat16)
        parts = [f32_dot(mover, plain[:, j * width : (j + 1) * width]) for j, mover in enumerate(movers)]
        folded_ref[i * rows : (i + 1) * rows, :] = sum(parts).astype(jnp.bfloat16)


def expert(capacity, landed_ref, up_ref, down_ref, hidden_out, grads_out, back, scratch):
    landed, up, down, rows, grads, hidden, total, weight_sems, hidden_sems, sems = scratch
    steps = weight_sems.shape[1]
    tile = up.shape[1] // steps

    def tile_at(i):
        return pl.ds(pl.multiple_of(i * tile, tile), tile)

    def up_copy(i):
        return pltpu.make_async_copy(up_ref.at[:, tile_at(i)], up.at[:, tile_at(i)], weight_sems.at[0, i])

    def down_copy(i):
        return pltpu.make_async_copy(down_ref.at[tile_at(i)], down.at[tile_at(i)], weight_sems.at[1, i])

    def hidden_copy(i):
        return pltpu.make_async_copy(hidden.at[:, tile_at(i)], hidden_out.at[:, tile_at(i)], hidden_sems.at[i])

    arrival = pltpu.make_async_copy(landed_ref, landed, sems.at[0])
    arrival.start()
    for i in range(min(AHEAD, steps)):
        up_copy(i).start()
        down_copy(i).start()
    total[...] = jnp.zeros_like(total)
    arrival.wait()
    take_rows(landed, 0, capacity, rows)
    take_rows(landed, 1, capacity, grads)
    departure = pltpu.make_async_copy(grads, grads_out, sems.at[1])
    departure.start()

    def step(i, carry):
        @pl.when(i + AHEAD < steps)
        def _():
            up_copy(i + AHEAD).start()
            down_copy(i + AHEAD).start()

        at = tile_at(i)
        up_copy(i).wait()
        preact = f32_dot(rows[...], up[:, at])
        hidden[:, at] = jnp.maximum(preact, 0.0).astype(jnp.bfloat16)
        hidden_copy(i).start()
        down_copy(i).wait()
        hidden_grad = f32_dot(grads[...], down[at, :], ((1,), (1,)))
        preact_grad = jnp.where(preact > 0, hidden_grad, 0.0).astype(jnp.bfloat16)
        total[...] += f32_dot(preact_grad, up[:, at], ((1,), (1,)))
        return carry

    lax.fori_loop(0, steps, step, 0)
    fold_rows(total, capacity, back)
    departure.wait()
    for i in range(steps):
        hidden_copy(i).wait()


def own_expert_kernel(capacity, landed_ref, up_ref, down_ref, hidden_out, grads_out, back_ref, *scratch):
    expert(capacity, landed_ref, up_ref, down_ref, hidden_out, grads_out, back_ref, scratch)


def far_expert_kernel(capacity, columns, half_ref, own_ref, landed_ref, up_ref, down_ref, *refs):
    hidden_out, grads_out, both_out, both_ref, own_held, far_held, sems = refs[:7]
    arrival = pltpu.make_async_copy(own_ref, own_held, sems.at[0])
    arrival.start()
    expert(capacity, landed_ref, up_ref, down_ref, hidden_out, grads_out, far_held, refs[7:])
    arrival.wait()
    size = columns * PAIR * capacity
    for source, half in ((own_held, half_ref[0]), (far_held, 1 - half_ref[0])):
        for group in range(source.shape[0] // size):
            target = pl.multiple_of((2 * group + half) * size, size)
            both_ref[pl.ds(target, size), :] = source[group * size : (group + 1) * size, :]
    departure = pltpu.make_async_copy(both_ref, both_out, sems.at[1])
    departure.start()
    departure.wait()


def down_grad_kernel(own_grads_ref, far_grads_ref, own_hidden_ref, far_hidden_ref, out_ref):
    own = f32_dot(own_hidden_ref[...], own_grads_ref[...], ((0,), (0,)))
    far = f32_dot(far_hidden_ref[...], far_grads_ref[...], ((0,), (0,)))
    out_ref[...] = (own + far).astype(jnp.bfloat16)


def pick_kernel(capacity, ids_ref, returned_ref, out_ref):
    rows, width = returned_ref.shape
    ids = ids_ref[...]
    names = lax.broadcasted_iota(jnp.int32, (rows // (PAIR * capacity), ids.shape[1]), 0)
    places = row_places(ids, names, capacity)
    for j in range(PAIR):
        chosen = either(hits_at(rows, [place + j * capacity for place in places]))
        total = f32_dot(chosen, returned_ref[...], ((0,), (0,)))
        out_ref[:, j * width : (j + 1) * width] = total.astype(jnp.bfloat16)


def exchange(rows, axes):
    peers = lax.axis_size(axes)
    cut = rows.reshape(peers, rows.shape[0] // peers, rows.shape[1])
    return lax.all_to_all(cut, axes, split_axis=0, concat_axis=0, tiled=True).reshape(rows.shape)


def swap(block):
    return lax.ppermute(block, "half", [(0, 1), (1, 0)])


def in_hbm(array):
    return pltpu.with_memory_space_constraint(array, pltpu.HBM)


def held(rows, columns, kind=jnp.bfloat16):
    return pltpu.VMEM((rows, columns), kind)


def shards(tokens, out_grad, expert_ids, gates, up_weight, down_weight):
    tok_rows, features = tokens.shape
    top_count = expert_ids.shape[1]
    units = up_weight.shape[2]
    columns = lax.axis_size("col")
    peers = lax.axis_size(("row", "col"))
    capacity = 3 * tok_rows * top_count // (4 * peers)
    slots, rows, width = peers * capacity, peers * PAIR * capacity, features // PAIR
    tile = min(units, TILE)
    steps = units // tile
    bf16, f32 = jnp.bfloat16, jnp.float32
    shape = jax.ShapeDtypeStruct
    dma = pltpu.SemaphoreType.DMA
    flops = 2 * slots * features * units
    weight_bytes = 2 * features * units

    def cost(matmuls, weights):
        return pl.CostEstimate(flops=matmuls * flops, bytes_accessed=weights * weight_bytes, transcendentals=0)

    smem = pl.BlockSpec(memory_space=pltpu.SMEM)
    vmem = pl.BlockSpec(memory_space=pltpu.VMEM)
    hbm = pl.BlockSpec(memory_space=pltpu.HBM)
    anywhere = pl.BlockSpec(memory_space=pl.ANY)
    ids, own_gates = expert_ids.T, gates.T
    far_ids, far_gates = swap(ids), swap(own_gates)
    pair_tokens = lax.all_gather(tokens, "half", axis=0, tiled=True)
    pair_grads = lax.all_gather(out_grad, "half", axis=0, tiled=True)
    half = lax.axis_index("half").astype(jnp.int32).reshape(1)

    def dispatch(far, matmuls, ids, gates, *blocks):
        sent = pl.pallas_call(
            functools.partial(dispatch_kernel, capacity, columns, far),
            out_shape=shape((rows, features), bf16),
            in_specs=[smem, vmem, vmem, hbm, hbm],
            scratch_shapes=[held(tok_rows, features), held(tok_rows, features), dma((2,))],
            compiler_params=params(),
            cost_estimate=cost(matmuls, 0),
            name="far_dispatch" if far else "own_dispatch",
        )(half, ids, gates, *[in_hbm(block) for block in blocks])
        return exchange(sent, ("row", "col"))

    landed_own = dispatch(False, 1, ids, own_gates, tokens, out_grad)
    landed_far = dispatch(True, 64, far_ids, far_gates, pair_tokens, pair_grads)

    weights = in_hbm(up_weight[0]), in_hbm(down_weight[0])
    results = pltpu.HBM((slots, units), bf16), pltpu.HBM((slots, features), bf16)
    scratch = [
        held(rows, features),
        held(features, units),
        held(units, features),
        held(slots, features),
        held(slots, features),
        held(slots, units),
        held(slots, features, f32),
        dma((2, steps)),
        dma((steps,)),
        dma((2,)),
    ]
    own_hidden, own_grads, own_back = pl.pallas_call(
        functools.partial(own_expert_kernel, capacity),
        out_shape=results + (shape((rows, width), bf16),),
        in_specs=[anywhere, hbm, hbm],
        out_specs=(hbm, hbm, vmem),
        scratch_shapes=scratch,
        compiler_params=params(),
        cost_estimate=cost(3, 2),
        name="own_expert",
    )(landed_own, *weights)
    far_hidden, far_grads, back = pl.pallas_call(
        functools.partial(far_expert_kernel, capacity, columns),
        out_shape=results + (pltpu.HBM((2 * rows, width), bf16),),
        in_specs=[smem, anywhere, anywhere, hbm, hbm],
        out_specs=(hbm, hbm, hbm),
        scratch_shapes=[held(2 * rows, width), held(rows, width), held(rows, width), dma((2,))] + scratch,
        compiler_params=params(),
        cost_estimate=cost(3, 2),
        name="far_expert",
    )(half, own_back, landed_far, *weights)
    returned = exchange(back, ("row", "half", "col"))

    grads_spec = pl.BlockSpec((slots, features), lambda i: (0, 0))
    hidden_spec = pl.BlockSpec((slots, tile), lambda i: (0, i))
    down_grad = pl.pallas_call(
        down_grad_kernel,
        out_shape=shape((1, units, features), bf16),
        grid=(steps,),
        in_specs=[grads_spec, grads_spec, hidden_spec, hidden_spec],
        out_specs=pl.BlockSpec((None, tile, features), lambda i: (0, i, 0)),
        compiler_params=params(),
        cost_estimate=cost(2, 1),
        name="down_grad",
    )(*[in_hbm(array) for array in (own_grads, far_grads, own_hidden, far_hidden)])

    input_grad = pl.pallas_call(
        functools.partial(pick_kernel, capacity),
        out_shape=shape((tok_rows, features), bf16),
        compiler_params=params(),
        name="pick",
    )(ids, returned)
    return input_grad, down_grad


def pooled_shards(tokens, out_grad, expert_ids, gates, up_weight, down_weight):
    tok_rows = tokens.shape[0]
    top_count = expert_ids.shape[1]
    features = tokens.shape[1]
    groups = lax.axis_size("row")
    col_count = lax.axis_size("col")
    experts = groups * col_count
    capacity = 3 * tok_rows * top_count // (2 * experts)
    flat_ids = expert_ids.reshape(-1)
    onehot = (flat_ids[:, None] == jnp.arange(experts, dtype=jnp.int32)[None, :]).astype(jnp.int32)
    earlier = jnp.cumsum(onehot, axis=0) - onehot
    slot_index = jnp.sum(earlier * onehot, axis=1)
    target = flat_ids * capacity + slot_index
    placer = (jnp.arange(experts * capacity, dtype=jnp.int32)[:, None] == target[None, :]).astype(
        jnp.bfloat16
    )
    token_rows = jnp.repeat(tokens, top_count, axis=0)
    weighted = (
        gates.reshape(-1)[:, None] * jnp.repeat(out_grad, top_count, axis=0).astype(jnp.float32)
    ).astype(jnp.bfloat16)
    send_inputs = jnp.dot(placer, token_rows, preferred_element_type=jnp.float32).astype(
        jnp.bfloat16
    )
    send_grads = jnp.dot(placer, weighted, preferred_element_type=jnp.float32).astype(jnp.bfloat16)
    landed_inputs, landed_grads = (
        lax.all_to_all(
            send_inputs.reshape(experts, capacity, features),
            ("row", "col"),
            split_axis=0,
            concat_axis=0,
            tiled=True,
        ),
        lax.all_to_all(
            send_grads.reshape(experts, capacity, features),
            ("row", "col"),
            split_axis=0,
            concat_axis=0,
            tiled=True,
        ),
    )
    pooled_inputs, pooled_grads = (
        lax.all_gather(landed_inputs, "rep", axis=0, tiled=True),
        lax.all_gather(landed_grads, "rep", axis=0, tiled=True),
    )
    slot_rows = pooled_inputs.shape[0] * capacity
    input_rows = pooled_inputs.reshape(slot_rows, features)
    grad_rows = pooled_grads.reshape(slot_rows, features)
    up_block = up_weight[0]
    down_block = down_weight[0]
    preact = jnp.dot(input_rows, up_block, preferred_element_type=jnp.float32)
    hidden = jnp.maximum(preact, 0.0).astype(jnp.bfloat16)
    hidden_grad = lax.dot_general(
        grad_rows, down_block, (((1,), (1,)), ((), ())), preferred_element_type=jnp.float32
    )
    preact_grad = jnp.where(preact > 0, hidden_grad, 0.0).astype(jnp.bfloat16)
    weight_grad = lax.dot_general(
        hidden, grad_rows, (((0,), (0,)), ((), ())), preferred_element_type=jnp.float32
    )
    down_grad = weight_grad.astype(jnp.bfloat16)[None]
    summed_rows = lax.psum_scatter(
        lax.dot_general(
            preact_grad, up_block, (((1,), (1,)), ((), ())), preferred_element_type=jnp.float32
        ).astype(jnp.bfloat16),
        "rep",
        scatter_dimension=0,
        tiled=True,
    )
    returned = lax.all_to_all(
        summed_rows.reshape(experts, capacity, features),
        ("row", "col"),
        split_axis=0,
        concat_axis=0,
        tiled=True,
    )
    returned = returned.reshape(experts * capacity, features)
    picked = lax.dot_general(
        placer, returned, (((0,), (0,)), ((), ())), preferred_element_type=jnp.float32
    )
    input_grad = jnp.sum(picked.reshape(tok_rows, top_count, features), axis=1).astype(jnp.bfloat16)
    return (input_grad, down_grad)


def solution(mesh):
    sizes = dict(mesh.shape)
    body, axes, owner = pooled_shards, mesh, ("row", "col")
    if sizes["rep"] == 1:
        cut = mesh.devices.reshape(1, sizes["row"], 2, sizes["col"] // 2)
        body, axes, owner = shards, Mesh(cut, ("rep", "row", "half", "col")), ("row", "half", "col")
    by_token = P(("rep",) + owner, None)
    by_expert = (P(owner, None, "rep"), P(owner, "rep", None))
    return jax.shard_map(
        body,
        mesh=axes,
        in_specs=(by_token,) * 4 + by_expert,
        out_specs=(by_token, by_expert[1]),
        check_vma=False,
    )
```

```python
import functools

import jax
import jax.numpy as jnp
from jax import lax
from jax.experimental import pallas as pl
from jax.experimental.pallas import tpu as pltpu
from jax.sharding import PartitionSpec as P

VMEM_LIMIT = 50 * 1024 * 1024
PAIR = 2
TILE = 512
UNITS_STEP = 1024
AHEAD = 2
NOWHERE = -(1 << 20)


def f32_dot(lhs, rhs, contract=((1,), (0,))):
    return lax.dot_general(lhs, rhs, (contract, ((), ())), preferred_element_type=jnp.float32)


def params():
    return pltpu.CompilerParams(vmem_limit_bytes=VMEM_LIMIT)


def row_places(ids, experts, capacity):
    tok_rows = ids.shape[1]
    names = lax.broadcasted_iota(jnp.int32, (experts, tok_rows), 0)
    chosen = [names == ids[k : k + 1, :] for k in range(ids.shape[0])]
    member = functools.reduce(jnp.logical_or, chosen).astype(jnp.bfloat16)
    before = (
        lax.broadcasted_iota(jnp.int32, (tok_rows, tok_rows), 0)
        < lax.broadcasted_iota(jnp.int32, (tok_rows, tok_rows), 1)
    ).astype(jnp.bfloat16)
    rank = f32_dot(member, before).astype(jnp.int32)
    place = names * (PAIR * capacity) + rank
    return [jnp.sum(jnp.where(pick, place, 0), axis=0, keepdims=True) for pick in chosen]


def hits_at(rows, places):
    at = lax.broadcasted_iota(jnp.int32, (rows, places[0].shape[1]), 0)
    return [at == place for place in places]


def either(hits):
    return functools.reduce(jnp.logical_or, hits).astype(jnp.bfloat16)


def started(pairs, sems):
    copies = [pltpu.make_async_copy(*pair, sems.at[i]) for i, pair in enumerate(pairs)]
    for copy in copies:
        copy.start()
    return copies


def dispatch_kernel(capacity, *refs):
    sources, out_ref, held, held_out, sems = refs[:4], refs[4], refs[5:9], refs[9], refs[10]
    ids_copy, gates_copy, tokens_copy, grad_copy = started(zip(sources, held), sems)
    ids_ref, gates_ref, tokens_ref, grad_ref = held
    rows = out_ref.shape[0]
    ids_copy.wait()
    places = row_places(ids_ref[...], rows // (PAIR * capacity), capacity)
    token_hits = hits_at(rows, places)
    grad_hits = hits_at(rows, [place + capacity for place in places])
    gates_copy.wait()
    scales = [jnp.where(hit, gates_ref[k : k + 1, :], 0.0) for k, hit in enumerate(grad_hits)]
    scale = jnp.sum(sum(scales), axis=1, keepdims=True)
    gathers = either(token_hits), either(grad_hits)
    tokens_copy.wait()
    grad_copy.wait()
    size = rows // (sems.shape[0] - 4)
    copies = []
    for i in range(rows // size):
        part = slice(i * size, (i + 1) * size)
        value = f32_dot(gathers[0][part], tokens_ref[...]) + scale[part] * f32_dot(gathers[1][part], grad_ref[...])
        held_out[part, :] = value.astype(jnp.bfloat16)
        copies.append(pltpu.make_async_copy(held_out.at[part], out_ref.at[part], sems.at[4 + i]))
        copies[-1].start()
    for copy in copies:
        copy.wait()


def paired_rows(number, capacity):
    owner = jnp.floor((number.astype(jnp.float32) + 0.5) * (1.0 / capacity)).astype(jnp.int32)
    return number + owner * ((PAIR - 1) * capacity)


def group_size(peers, capacity):
    size = 1
    while peers % (2 * size) == 0 and size * PAIR * capacity < 192:
        size *= 2
    return size


def take_rows(landed_ref, j, capacity, rows_ref):
    size = group_size(landed_ref.shape[0] // (PAIR * capacity), capacity)
    slots, rows = size * capacity, size * PAIR * capacity
    at = lax.broadcasted_iota(jnp.int32, (slots, rows), 1)
    source = paired_rows(lax.broadcasted_iota(jnp.int32, (slots, 1), 0), capacity) + j * capacity
    mover = (at == source).astype(jnp.bfloat16)
    for i in range(rows_ref.shape[0] // slots):
        taken = f32_dot(mover, landed_ref[i * rows : (i + 1) * rows, :])
        rows_ref[i * slots : (i + 1) * slots, :] = taken.astype(jnp.bfloat16)


def fold_rows(plain_ref, capacity, folded_ref, out_ref, sems):
    size = group_size(plain_ref.shape[0] // capacity, capacity)
    slots, rows = size * capacity, size * PAIR * capacity
    width = folded_ref.shape[1]
    at = lax.broadcasted_iota(jnp.int32, (rows, slots), 0)
    target = paired_rows(lax.broadcasted_iota(jnp.int32, (1, slots), 1), capacity)
    movers = [(at == target + j * capacity).astype(jnp.bfloat16) for j in range(PAIR)]
    copies = []
    for i in range(plain_ref.shape[0] // slots):
        plain = plain_ref[i * slots : (i + 1) * slots, :].astype(jnp.bfloat16)
        parts = [f32_dot(mover, plain[:, j * width : (j + 1) * width]) for j, mover in enumerate(movers)]
        part = slice(i * rows, (i + 1) * rows)
        folded_ref[part, :] = sum(parts).astype(jnp.bfloat16)
        copies.append(pltpu.make_async_copy(folded_ref.at[part], out_ref.at[part], sems.at[i]))
        copies[-1].start()
    return copies


def expert_kernel(capacity, landed_ref, up_ref, down_ref, hidden_out, grads_out, back_out, *scratch):
    landed, up, down, rows, grads, hidden, masked, total, back, weight_sems, hidden_sems, sems, back_sems = scratch
    steps = weight_sems.shape[1]
    tile = up.shape[1] // steps

    def tile_at(i):
        return pl.ds(i * tile, tile)

    def up_copy(i):
        return pltpu.make_async_copy(up_ref.at[:, tile_at(i)], up.at[:, tile_at(i)], weight_sems.at[0, i])

    def down_copy(i):
        return pltpu.make_async_copy(down_ref.at[tile_at(i)], down.at[tile_at(i)], weight_sems.at[1, i])

    def hidden_copy(i):
        return pltpu.make_async_copy(hidden.at[:, tile_at(i)], hidden_out.at[:, tile_at(i)], hidden_sems.at[i])

    def add_row_grad(i):
        part = f32_dot(masked[i % 2], up[:, tile_at(i)], ((1,), (1,)))
        total[...] = part if i == 0 else total[...] + part

    arrival = pltpu.make_async_copy(landed_ref, landed, sems.at[0])
    arrival.start()
    for i in range(min(AHEAD, steps)):
        up_copy(i).start()
        down_copy(i).start()
    arrival.wait()
    take_rows(landed, 0, capacity, rows)
    take_rows(landed, 1, capacity, grads)
    departure = pltpu.make_async_copy(grads, grads_out, sems.at[1])
    departure.start()
    for i in range(steps):
        if i + AHEAD < steps:
            up_copy(i + AHEAD).start()
            down_copy(i + AHEAD).start()
        up_copy(i).wait()
        down_copy(i).wait()
        preact = f32_dot(rows[...], up[:, tile_at(i)])
        hidden_grad = f32_dot(grads[...], down[tile_at(i), :], ((1,), (1,)))
        if i:
            add_row_grad(i - 1)
        hidden[:, tile_at(i)] = jnp.maximum(preact, 0.0).astype(jnp.bfloat16)
        masked[i % 2] = jnp.where(preact > 0, hidden_grad, 0.0).astype(jnp.bfloat16)
        hidden_copy(i).start()
    add_row_grad(steps - 1)
    last = fold_rows(total, capacity, back, back_out, back_sems)
    departure.wait()
    for i in range(steps):
        hidden_copy(i).wait()
    for copy in last:
        copy.wait()


def down_grad_kernel(grads_ref, hidden_ref, out_ref):
    out_ref[...] = f32_dot(hidden_ref[...], grads_ref[...], ((0,), (0,))).astype(jnp.bfloat16)


def pick_kernel(capacity, ids_ref, returned_ref, out_ref):
    rows, width = returned_ref.shape
    places = row_places(ids_ref[...], rows // (PAIR * capacity), capacity)
    for j in range(PAIR):
        chosen = either(hits_at(rows, [place + j * capacity for place in places]))
        total = f32_dot(chosen, returned_ref[...], ((0,), (0,)))
        out_ref[:, j * width : (j + 1) * width] = total.astype(jnp.bfloat16)


def exchange(rows):
    axes = ("row", "col")
    peers = lax.axis_size(axes)
    cut = rows.reshape(peers, rows.shape[0] // peers, rows.shape[1])
    return lax.all_to_all(cut, axes, split_axis=0, concat_axis=0, tiled=True).reshape(rows.shape)


def in_hbm(array):
    return pltpu.with_memory_space_constraint(array, pltpu.HBM)


def held(rows, columns, kind=jnp.bfloat16):
    return pltpu.VMEM((rows, columns), kind)


def shards(tokens, out_grad, expert_ids, gates, up_weight, down_weight):
    tok_rows, features = tokens.shape
    top_count = expert_ids.shape[1]
    units = up_weight.shape[2]
    peers = lax.axis_size(("row", "col"))
    capacity = 3 * tok_rows * top_count // (2 * peers)
    slots, rows, width = peers * capacity, peers * PAIR * capacity, features // PAIR
    tile = min(units, TILE)
    steps = units // tile
    step = min(units, UNITS_STEP)
    parts = peers // group_size(peers, capacity)
    bf16, f32 = jnp.bfloat16, jnp.float32
    shape = jax.ShapeDtypeStruct
    dma = pltpu.SemaphoreType.DMA
    flops = 2 * slots * features * units
    weight_bytes = 2 * features * units

    def cost(matmuls, weights):
        return pl.CostEstimate(flops=matmuls * flops, bytes_accessed=weights * weight_bytes, transcendentals=0)

    ids = expert_ids.T
    hbm = pl.BlockSpec(memory_space=pltpu.HBM)
    anywhere = pl.BlockSpec(memory_space=pl.ANY)

    sent = pl.pallas_call(
        functools.partial(dispatch_kernel, capacity),
        out_shape=pltpu.HBM((rows, features), bf16),
        in_specs=[hbm, hbm, hbm, hbm],
        out_specs=hbm,
        scratch_shapes=[
            held(top_count, tok_rows, jnp.int32),
            held(top_count, tok_rows, f32),
            held(tok_rows, features),
            held(tok_rows, features),
            held(rows, features),
            dma((4 + parts,)),
        ],
        compiler_params=params(),
        name="dispatch",
    )(*[in_hbm(array) for array in (ids, gates.T, tokens, out_grad)])
    landed = exchange(sent)

    hidden, grads, back = pl.pallas_call(
        functools.partial(expert_kernel, capacity),
        out_shape=(
            pltpu.HBM((slots, units), bf16),
            pltpu.HBM((slots, features), bf16),
            pltpu.HBM((rows, width), bf16),
        ),
        in_specs=[anywhere, hbm, hbm],
        out_specs=(hbm, hbm, hbm),
        scratch_shapes=[
            held(rows, features),
            held(features, units),
            held(units, features),
            held(slots, features),
            held(slots, features),
            held(slots, units),
            pltpu.VMEM((2, slots, step), bf16),
            held(slots, features, f32),
            held(rows, width),
            dma((2, units // step)),
            dma((units // step,)),
            dma((2,)),
            dma((parts,)),
        ],
        compiler_params=params(),
        cost_estimate=cost(3, 2),
        name="expert",
    )(landed, in_hbm(up_weight[0]), in_hbm(down_weight[0]))
    returned = exchange(back)

    down_grad = pl.pallas_call(
        down_grad_kernel,
        out_shape=shape((1, units, features), bf16),
        grid=(steps,),
        in_specs=[pl.BlockSpec((slots, features), lambda i: (0, 0)), pl.BlockSpec((slots, tile), lambda i: (0, i))],
        out_specs=pl.BlockSpec((None, tile, features), lambda i: (0, i, 0)),
        compiler_params=params(),
        cost_estimate=cost(1, 1),
        name="down_grad",
    )(in_hbm(grads), in_hbm(hidden))

    input_grad = pl.pallas_call(
        functools.partial(pick_kernel, capacity),
        out_shape=shape((tok_rows, features), bf16),
        compiler_params=params(),
        name="pick",
    )(ids, returned)
    return input_grad, down_grad


def pooled_shards(tokens, out_grad, expert_ids, gates, up_weight, down_weight):
    tok_rows = tokens.shape[0]
    top_count = expert_ids.shape[1]
    features = tokens.shape[1]
    groups = lax.axis_size("row")
    col_count = lax.axis_size("col")
    experts = groups * col_count
    capacity = 3 * tok_rows * top_count // (2 * experts)
    flat_ids = expert_ids.reshape(-1)
    onehot = (flat_ids[:, None] == jnp.arange(experts, dtype=jnp.int32)[None, :]).astype(jnp.int32)
    earlier = jnp.cumsum(onehot, axis=0) - onehot
    slot_index = jnp.sum(earlier * onehot, axis=1)
    target = flat_ids * capacity + slot_index
    placer = (jnp.arange(experts * capacity, dtype=jnp.int32)[:, None] == target[None, :]).astype(
        jnp.bfloat16
    )
    token_rows = jnp.repeat(tokens, top_count, axis=0)
    weighted = (
        gates.reshape(-1)[:, None] * jnp.repeat(out_grad, top_count, axis=0).astype(jnp.float32)
    ).astype(jnp.bfloat16)
    send_inputs = jnp.dot(placer, token_rows, preferred_element_type=jnp.float32).astype(
        jnp.bfloat16
    )
    send_grads = jnp.dot(placer, weighted, preferred_element_type=jnp.float32).astype(jnp.bfloat16)
    landed_inputs, landed_grads = (
        lax.all_to_all(
            send_inputs.reshape(experts, capacity, features),
            ("row", "col"),
            split_axis=0,
            concat_axis=0,
            tiled=True,
        ),
        lax.all_to_all(
            send_grads.reshape(experts, capacity, features),
            ("row", "col"),
            split_axis=0,
            concat_axis=0,
            tiled=True,
        ),
    )
    pooled_inputs, pooled_grads = (
        lax.all_gather(landed_inputs, "rep", axis=0, tiled=True),
        lax.all_gather(landed_grads, "rep", axis=0, tiled=True),
    )
    slot_rows = pooled_inputs.shape[0] * capacity
    input_rows = pooled_inputs.reshape(slot_rows, features)
    grad_rows = pooled_grads.reshape(slot_rows, features)
    up_block = up_weight[0]
    down_block = down_weight[0]
    preact = jnp.dot(input_rows, up_block, preferred_element_type=jnp.float32)
    hidden = jnp.maximum(preact, 0.0).astype(jnp.bfloat16)
    hidden_grad = lax.dot_general(
        grad_rows, down_block, (((1,), (1,)), ((), ())), preferred_element_type=jnp.float32
    )
    preact_grad = jnp.where(preact > 0, hidden_grad, 0.0).astype(jnp.bfloat16)
    weight_grad = lax.dot_general(
        hidden, grad_rows, (((0,), (0,)), ((), ())), preferred_element_type=jnp.float32
    )
    down_grad = weight_grad.astype(jnp.bfloat16)[None]
    summed_rows = lax.psum_scatter(
        lax.dot_general(
            preact_grad, up_block, (((1,), (1,)), ((), ())), preferred_element_type=jnp.float32
        ).astype(jnp.bfloat16),
        "rep",
        scatter_dimension=0,
        tiled=True,
    )
    returned = lax.all_to_all(
        summed_rows.reshape(experts, capacity, features),
        ("row", "col"),
        split_axis=0,
        concat_axis=0,
        tiled=True,
    )
    returned = returned.reshape(experts * capacity, features)
    picked = lax.dot_general(
        placer, returned, (((0,), (0,)), ((), ())), preferred_element_type=jnp.float32
    )
    input_grad = jnp.sum(picked.reshape(tok_rows, top_count, features), axis=1).astype(jnp.bfloat16)
    return (input_grad, down_grad)


def solution(mesh):
    by_token = P(("rep", "row", "col"), None)
    by_expert = (P(("row", "col"), None, "rep"), P(("row", "col"), "rep", None))
    return jax.shard_map(
        shards if mesh.shape["rep"] == 1 else pooled_shards,
        mesh=mesh,
        in_specs=(by_token,) * 4 + by_expert,
        out_specs=(by_token, by_expert[1]),
        check_vma=False,
    )
```

```python
import functools

import jax
import jax.numpy as jnp
from jax import lax
from jax.experimental import pallas as pl
from jax.experimental.pallas import tpu as pltpu
from jax.sharding import PartitionSpec as P

VMEM_LIMIT = 48 * 1024 * 1024
PAIR = 2
TILE = 512
PIECES = 4
NOWHERE = -(1 << 20)


def f32_dot(lhs, rhs, contract=((1,), (0,))):
    return lax.dot_general(lhs, rhs, (contract, ((), ())), preferred_element_type=jnp.float32)


def params():
    return pltpu.CompilerParams(vmem_limit_bytes=VMEM_LIMIT)


def row_places(ids, experts, capacity):
    tok_rows = ids.shape[1]
    names = lax.broadcasted_iota(jnp.int32, (experts, tok_rows), 0)
    chosen = [names == ids[k : k + 1, :] for k in range(ids.shape[0])]
    member = functools.reduce(jnp.logical_or, chosen).astype(jnp.bfloat16)
    before = (
        lax.broadcasted_iota(jnp.int32, (tok_rows, tok_rows), 0)
        < lax.broadcasted_iota(jnp.int32, (tok_rows, tok_rows), 1)
    ).astype(jnp.bfloat16)
    rank = f32_dot(member, before).astype(jnp.int32)
    place = names * (PAIR * capacity) + rank
    return [jnp.sum(jnp.where(pick, place, 0), axis=0, keepdims=True) for pick in chosen]


def hits_at(rows, places):
    at = lax.broadcasted_iota(jnp.int32, (rows, places[0].shape[1]), 0)
    return [at == place for place in places]


def either(hits):
    return functools.reduce(jnp.logical_or, hits).astype(jnp.bfloat16)


def started(pairs, sems):
    copies = [pltpu.make_async_copy(*pair, sems.at[i]) for i, pair in enumerate(pairs)]
    for copy in copies:
        copy.start()
    return copies


def dispatch_kernel(capacity, *refs):
    sources, out_ref, held, sems = refs[:4], refs[4], refs[5:9], refs[9]
    ids_copy, gates_copy, tokens_copy, grad_copy = started(zip(sources, held), sems)
    ids_ref, gates_ref, tokens_ref, grad_ref = held
    rows = out_ref.shape[0]
    ids_copy.wait()
    places = row_places(ids_ref[...], rows // (PAIR * capacity), capacity)
    token_hits = hits_at(rows, places)
    grad_hits = hits_at(rows, [place + capacity for place in places])
    gates_copy.wait()
    scales = [jnp.where(hit, gates_ref[k : k + 1, :], 0.0) for k, hit in enumerate(grad_hits)]
    scale = jnp.sum(sum(scales), axis=1, keepdims=True)
    tokens_copy.wait()
    grad_copy.wait()
    value = f32_dot(either(token_hits), tokens_ref[...]) + scale * f32_dot(either(grad_hits), grad_ref[...])
    out_ref[...] = value.astype(jnp.bfloat16)


def paired_rows(number, capacity):
    owner = jnp.floor((number.astype(jnp.float32) + 0.5) * (1.0 / capacity)).astype(jnp.int32)
    return number + owner * ((PAIR - 1) * capacity)


def group_size(peers, capacity):
    size = 1
    while peers % (2 * size) == 0 and size * PAIR * capacity < 192:
        size *= 2
    return size


def take_apart(landed_ref, capacity, rows_ref, grads_ref):
    size = group_size(landed_ref.shape[0] // (PAIR * capacity), capacity)
    slots, rows = size * capacity, size * PAIR * capacity
    at = lax.broadcasted_iota(jnp.int32, (slots, rows), 1)
    source = paired_rows(lax.broadcasted_iota(jnp.int32, (slots, 1), 0), capacity)
    mover = jnp.concatenate([(at == source + j * capacity).astype(jnp.bfloat16) for j in range(PAIR)], axis=0)
    for i in range(rows_ref.shape[0] // slots):
        taken = f32_dot(mover, landed_ref[i * rows : (i + 1) * rows, :]).astype(jnp.bfloat16)
        rows_ref[i * slots : (i + 1) * slots, :] = taken[:slots]
        grads_ref[i * slots : (i + 1) * slots, :] = taken[slots:]


def fold_rows(plain_ref, capacity, folded_ref, out_ref, sems):
    size = group_size(plain_ref.shape[0] // capacity, capacity)
    slots, rows = size * capacity, size * PAIR * capacity
    width = folded_ref.shape[1]
    at = lax.broadcasted_iota(jnp.int32, (rows, slots), 0)
    target = paired_rows(lax.broadcasted_iota(jnp.int32, (1, slots), 1), capacity)
    movers = [(at == target + j * capacity).astype(jnp.bfloat16) for j in range(PAIR)]
    copies = []
    for i in range(plain_ref.shape[0] // slots):
        plain = plain_ref[i * slots : (i + 1) * slots, :].astype(jnp.bfloat16)
        parts = [f32_dot(mover, plain[:, j * width : (j + 1) * width]) for j, mover in enumerate(movers)]
        part = slice(i * rows, (i + 1) * rows)
        folded_ref[part, :] = sum(parts).astype(jnp.bfloat16)
        copies.append(pltpu.make_async_copy(folded_ref.at[part], out_ref.at[part], sems.at[i]))
        copies[-1].start()
    return copies


def unit_tiles(units):
    sizes = [TILE, TILE] if units % (2 * TILE) == 0 else []
    while sum(sizes) < units:
        sizes.append(2 * TILE if sizes else units)
    return [(sum(sizes[:i]), size) for i, size in enumerate(sizes)]


def expert_kernel(capacity, landed_ref, up_ref, down_ref, hidden_out, grads_out, back_out, *scratch):
    up, down, rows, grads, hidden, masked, total, back, weight_sems, hidden_sems, grads_sem, back_sems = scratch
    tiles = unit_tiles(up.shape[1])
    features = up.shape[0]

    def weight_copies(i):
        start, size = tiles[i]
        copies = []
        for n in range(PIECES):
            part = pl.ds(n * (features // PIECES), features // PIECES), pl.ds(start, size)
            copies.append(pltpu.make_async_copy(up_ref.at[part], up.at[part], weight_sems.at[0, i, n]))
        for n in range(PIECES):
            part = pl.ds(start + n * (size // PIECES), size // PIECES)
            copies.append(pltpu.make_async_copy(down_ref.at[part], down.at[part], weight_sems.at[1, i, n]))
        return copies

    def start_weights(i):
        if i < len(tiles):
            arriving[i] = weight_copies(i)
            for copy in arriving[i]:
                copy.start()

    def add_row_grad(i):
        start, size = tiles[i]
        part = f32_dot(masked[i % 2, :, :size], up[:, start : start + size], ((1,), (1,)))
        total[...] = part if i == 0 else total[...] + part

    arriving, leaving = {}, []
    start_weights(0)
    take_apart(landed_ref, capacity, rows, grads)
    leaving.append(pltpu.make_async_copy(grads, grads_out, grads_sem.at[0]))
    leaving[-1].start()
    start_weights(1)
    for i, (start, size) in enumerate(tiles):
        here = slice(start, start + size)
        for copy in arriving[i]:
            copy.wait()
        start_weights(i + 2)
        preact = f32_dot(rows[...], up[:, here])
        hidden_grad = f32_dot(grads[...], down[here, :], ((1,), (1,)))
        if i:
            add_row_grad(i - 1)
        hidden[:, here] = jnp.maximum(preact, 0.0).astype(jnp.bfloat16)
        masked[i % 2, :, :size] = jnp.where(preact > 0, hidden_grad, 0.0).astype(jnp.bfloat16)
        leaving.append(pltpu.make_async_copy(hidden.at[:, here], hidden_out.at[:, here], hidden_sems.at[i]))
        leaving[-1].start()
    add_row_grad(len(tiles) - 1)
    for copy in leaving + fold_rows(total, capacity, back, back_out, back_sems):
        copy.wait()


def down_grad_kernel(grads_ref, hidden_ref, out_ref):
    out_ref[...] = f32_dot(hidden_ref[...], grads_ref[...], ((0,), (0,))).astype(jnp.bfloat16)


def pick_map_kernel(capacity, ids_ref, after_ref, out_ref):
    tok_rows, rows = ids_ref.shape[1], out_ref.shape[1]
    places = row_places(ids_ref[...], rows // (PAIR * capacity), capacity)
    for j in range(PAIR):
        chosen = either(hits_at(rows, [place + j * capacity for place in places]))
        out_ref[j * tok_rows : (j + 1) * tok_rows, :] = chosen.T


def pick_kernel(map_ref, returned_ref, out_ref):
    tok_rows, width = out_ref.shape[0], returned_ref.shape[1]
    picked = f32_dot(map_ref[...], returned_ref[...]).astype(jnp.bfloat16)
    for j in range(PAIR):
        out_ref[:, j * width : (j + 1) * width] = picked[j * tok_rows : (j + 1) * tok_rows]


def exchange(rows):
    axes = ("row", "col")
    peers = lax.axis_size(axes)
    cut = rows.reshape(peers, rows.shape[0] // peers, rows.shape[1])
    return lax.all_to_all(cut, axes, split_axis=0, concat_axis=0, tiled=True).reshape(rows.shape)


def in_hbm(array):
    return pltpu.with_memory_space_constraint(array, pltpu.HBM)


def held(rows, columns, kind=jnp.bfloat16):
    return pltpu.VMEM((rows, columns), kind)


def shards(tokens, out_grad, expert_ids, gates, up_weight, down_weight):
    tok_rows, features = tokens.shape
    top_count = expert_ids.shape[1]
    units = up_weight.shape[2]
    peers = lax.axis_size(("row", "col"))
    capacity = 3 * tok_rows * top_count // (2 * peers)
    slots, rows, width = peers * capacity, peers * PAIR * capacity, features // PAIR
    tile = min(units, TILE)
    steps = units // tile
    bf16, f32 = jnp.bfloat16, jnp.float32
    shape = jax.ShapeDtypeStruct
    dma = pltpu.SemaphoreType.DMA
    flops = 2 * slots * features * units
    weight_bytes = 2 * features * units

    def cost(matmuls, weights):
        return pl.CostEstimate(flops=matmuls * flops, bytes_accessed=weights * weight_bytes, transcendentals=0)

    ids = expert_ids.T
    hbm = pl.BlockSpec(memory_space=pltpu.HBM)
    vmem = pl.BlockSpec(memory_space=pltpu.VMEM)
    anywhere = pl.BlockSpec(memory_space=pl.ANY)
    tiles = unit_tiles(units)
    largest = max(size for _, size in tiles)

    sent = pl.pallas_call(
        functools.partial(dispatch_kernel, capacity),
        out_shape=shape((rows, features), bf16),
        in_specs=[hbm, hbm, hbm, hbm],
        scratch_shapes=[
            held(top_count, tok_rows, jnp.int32),
            held(top_count, tok_rows, f32),
            held(tok_rows, features),
            held(tok_rows, features),
            dma((4,)),
        ],
        compiler_params=params(),
        name="dispatch",
    )(*[in_hbm(array) for array in (ids, gates.T, tokens, out_grad)])
    landed = exchange(sent)

    hidden, grads, back = pl.pallas_call(
        functools.partial(expert_kernel, capacity),
        out_shape=(
            pltpu.HBM((slots, units), bf16),
            pltpu.HBM((slots, features), bf16),
            pltpu.HBM((rows, width), bf16),
        ),
        in_specs=[vmem, hbm, hbm],
        out_specs=(hbm, hbm, hbm),
        scratch_shapes=[
            held(features, units),
            held(units, features),
            held(slots, features),
            held(slots, features),
            held(slots, units),
            pltpu.VMEM((2, slots, largest), bf16),
            held(slots, features, f32),
            held(rows, width),
            dma((2, len(tiles), PIECES)),
            dma((len(tiles),)),
            dma((1,)),
            dma((peers // group_size(peers, capacity),)),
        ],
        compiler_params=params(),
        cost_estimate=cost(3, 2),
        name="expert",
    )(landed, in_hbm(up_weight[0]), in_hbm(down_weight[0]))
    returned = exchange(back)

    down_grad = pl.pallas_call(
        down_grad_kernel,
        out_shape=shape((1, units, features), bf16),
        grid=(steps,),
        in_specs=[pl.BlockSpec((slots, features), lambda i: (0, 0)), pl.BlockSpec((slots, tile), lambda i: (0, i))],
        out_specs=pl.BlockSpec((None, tile, features), lambda i: (0, i, 0)),
        compiler_params=params(),
        cost_estimate=cost(1, 1),
        name="down_grad",
    )(in_hbm(grads), in_hbm(hidden))

    pick_map = pl.pallas_call(
        functools.partial(pick_map_kernel, capacity),
        out_shape=shape((PAIR * tok_rows, rows), bf16),
        in_specs=[vmem, anywhere],
        compiler_params=params(),
        name="pick_map",
    )(ids, in_hbm(grads))
    input_grad = pl.pallas_call(
        pick_kernel,
        out_shape=shape((tok_rows, features), bf16),
        compiler_params=params(),
        name="pick",
    )(pick_map, returned)
    return input_grad, down_grad


def pooled_shards(tokens, out_grad, expert_ids, gates, up_weight, down_weight):
    tok_rows = tokens.shape[0]
    top_count = expert_ids.shape[1]
    features = tokens.shape[1]
    groups = lax.axis_size("row")
    col_count = lax.axis_size("col")
    experts = groups * col_count
    capacity = 3 * tok_rows * top_count // (2 * experts)
    flat_ids = expert_ids.reshape(-1)
    onehot = (flat_ids[:, None] == jnp.arange(experts, dtype=jnp.int32)[None, :]).astype(jnp.int32)
    earlier = jnp.cumsum(onehot, axis=0) - onehot
    slot_index = jnp.sum(earlier * onehot, axis=1)
    target = flat_ids * capacity + slot_index
    placer = (jnp.arange(experts * capacity, dtype=jnp.int32)[:, None] == target[None, :]).astype(
        jnp.bfloat16
    )
    token_rows = jnp.repeat(tokens, top_count, axis=0)
    weighted = (
        gates.reshape(-1)[:, None] * jnp.repeat(out_grad, top_count, axis=0).astype(jnp.float32)
    ).astype(jnp.bfloat16)
    send_inputs = jnp.dot(placer, token_rows, preferred_element_type=jnp.float32).astype(
        jnp.bfloat16
    )
    send_grads = jnp.dot(placer, weighted, preferred_element_type=jnp.float32).astype(jnp.bfloat16)
    landed_inputs, landed_grads = (
        lax.all_to_all(
            send_inputs.reshape(experts, capacity, features),
            ("row", "col"),
            split_axis=0,
            concat_axis=0,
            tiled=True,
        ),
        lax.all_to_all(
            send_grads.reshape(experts, capacity, features),
            ("row", "col"),
            split_axis=0,
            concat_axis=0,
            tiled=True,
        ),
    )
    pooled_inputs, pooled_grads = (
        lax.all_gather(landed_inputs, "rep", axis=0, tiled=True),
        lax.all_gather(landed_grads, "rep", axis=0, tiled=True),
    )
    slot_rows = pooled_inputs.shape[0] * capacity
    input_rows = pooled_inputs.reshape(slot_rows, features)
    grad_rows = pooled_grads.reshape(slot_rows, features)
    up_block = up_weight[0]
    down_block = down_weight[0]
    preact = jnp.dot(input_rows, up_block, preferred_element_type=jnp.float32)
    hidden = jnp.maximum(preact, 0.0).astype(jnp.bfloat16)
    hidden_grad = lax.dot_general(
        grad_rows, down_block, (((1,), (1,)), ((), ())), preferred_element_type=jnp.float32
    )
    preact_grad = jnp.where(preact > 0, hidden_grad, 0.0).astype(jnp.bfloat16)
    weight_grad = lax.dot_general(
        hidden, grad_rows, (((0,), (0,)), ((), ())), preferred_element_type=jnp.float32
    )
    down_grad = weight_grad.astype(jnp.bfloat16)[None]
    summed_rows = lax.psum_scatter(
        lax.dot_general(
            preact_grad, up_block, (((1,), (1,)), ((), ())), preferred_element_type=jnp.float32
        ).astype(jnp.bfloat16),
        "rep",
        scatter_dimension=0,
        tiled=True,
    )
    returned = lax.all_to_all(
        summed_rows.reshape(experts, capacity, features),
        ("row", "col"),
        split_axis=0,
        concat_axis=0,
        tiled=True,
    )
    returned = returned.reshape(experts * capacity, features)
    picked = lax.dot_general(
        placer, returned, (((0,), (0,)), ((), ())), preferred_element_type=jnp.float32
    )
    input_grad = jnp.sum(picked.reshape(tok_rows, top_count, features), axis=1).astype(jnp.bfloat16)
    return (input_grad, down_grad)


def solution(mesh):
    by_token = P(("rep", "row", "col"), None)
    by_expert = (P(("row", "col"), None, "rep"), P(("row", "col"), "rep", None))
    return jax.shard_map(
        shards if mesh.shape["rep"] == 1 else pooled_shards,
        mesh=mesh,
        in_specs=(by_token,) * 4 + by_expert,
        out_specs=(by_token, by_expert[1]),
        check_vma=False,
    )
```

```python
import functools

import jax
import jax.numpy as jnp
from jax import lax
from jax.experimental import pallas as pl
from jax.experimental.pallas import tpu as pltpu
from jax.sharding import PartitionSpec as P

VMEM_LIMIT = 48 * 1024 * 1024
PAIR = 2
TILE = 512
PIECES = 4
AHEAD = 2
NOWHERE = -(1 << 20)


def f32_dot(lhs, rhs, contract=((1,), (0,))):
    return lax.dot_general(lhs, rhs, (contract, ((), ())), preferred_element_type=jnp.float32)


def params():
    return pltpu.CompilerParams(vmem_limit_bytes=VMEM_LIMIT)


def row_places(ids, experts, capacity):
    tok_rows = ids.shape[1]
    names = lax.broadcasted_iota(jnp.int32, (experts, tok_rows), 0)
    chosen = [names == ids[k : k + 1, :] for k in range(ids.shape[0])]
    member = functools.reduce(jnp.logical_or, chosen).astype(jnp.bfloat16)
    before = (
        lax.broadcasted_iota(jnp.int32, (tok_rows, tok_rows), 0)
        < lax.broadcasted_iota(jnp.int32, (tok_rows, tok_rows), 1)
    ).astype(jnp.bfloat16)
    rank = f32_dot(member, before).astype(jnp.int32)
    place = names * (PAIR * capacity) + rank
    return [jnp.sum(jnp.where(pick, place, 0), axis=0, keepdims=True) for pick in chosen]


def hits_at(rows, places):
    at = lax.broadcasted_iota(jnp.int32, (rows, places[0].shape[1]), 0)
    return [at == place for place in places]


def either(hits):
    return functools.reduce(jnp.logical_or, hits).astype(jnp.bfloat16)


def started(pairs, sems):
    copies = [pltpu.make_async_copy(*pair, sems.at[i]) for i, pair in enumerate(pairs)]
    for copy in copies:
        copy.start()
    return copies


def dispatch_kernel(capacity, *refs):
    sources, out_ref, held, sems = refs[:4], refs[4], refs[5:9], refs[9]
    ids_copy, gates_copy, tokens_copy, grad_copy = started(zip(sources, held), sems)
    ids_ref, gates_ref, tokens_ref, grad_ref = held
    rows = out_ref.shape[0]
    ids_copy.wait()
    places = row_places(ids_ref[...], rows // (PAIR * capacity), capacity)
    token_hits = hits_at(rows, places)
    grad_hits = hits_at(rows, [place + capacity for place in places])
    gates_copy.wait()
    scales = [jnp.where(hit, gates_ref[k : k + 1, :], 0.0) for k, hit in enumerate(grad_hits)]
    scale = jnp.sum(sum(scales), axis=1, keepdims=True)
    tokens_copy.wait()
    grad_copy.wait()
    value = f32_dot(either(token_hits), tokens_ref[...]) + scale * f32_dot(either(grad_hits), grad_ref[...])
    out_ref[...] = value.astype(jnp.bfloat16)


def paired_rows(number, capacity):
    owner = jnp.floor((number.astype(jnp.float32) + 0.5) * (1.0 / capacity)).astype(jnp.int32)
    return number + owner * ((PAIR - 1) * capacity)


def group_size(peers, capacity):
    size = 1
    while peers % (2 * size) == 0 and size * PAIR * capacity < 192:
        size *= 2
    return size


def take_apart(landed_ref, capacity, rows_ref, grads_ref):
    size = group_size(landed_ref.shape[0] // (PAIR * capacity), capacity)
    slots, rows = size * capacity, size * PAIR * capacity
    at = lax.broadcasted_iota(jnp.int32, (slots, rows), 1)
    source = paired_rows(lax.broadcasted_iota(jnp.int32, (slots, 1), 0), capacity)
    mover = jnp.concatenate([(at == source + j * capacity).astype(jnp.bfloat16) for j in range(PAIR)], axis=0)
    for i in range(rows_ref.shape[0] // slots):
        taken = f32_dot(mover, landed_ref[i * rows : (i + 1) * rows, :]).astype(jnp.bfloat16)
        rows_ref[i * slots : (i + 1) * slots, :] = taken[:slots]
        grads_ref[i * slots : (i + 1) * slots, :] = taken[slots:]


def fold_rows(plain_ref, capacity, folded_ref, out_ref, sems):
    size = group_size(plain_ref.shape[0] // capacity, capacity)
    slots, rows = size * capacity, size * PAIR * capacity
    width = folded_ref.shape[1]
    at = lax.broadcasted_iota(jnp.int32, (rows, slots), 0)
    target = paired_rows(lax.broadcasted_iota(jnp.int32, (1, slots), 1), capacity)
    movers = [(at == target + j * capacity).astype(jnp.bfloat16) for j in range(PAIR)]
    copies = []
    for i in range(plain_ref.shape[0] // slots):
        plain = plain_ref[i * slots : (i + 1) * slots, :].astype(jnp.bfloat16)
        parts = [f32_dot(mover, plain[:, j * width : (j + 1) * width]) for j, mover in enumerate(movers)]
        part = slice(i * rows, (i + 1) * rows)
        folded_ref[part, :] = sum(parts).astype(jnp.bfloat16)
        copies.append(pltpu.make_async_copy(folded_ref.at[part], out_ref.at[part], sems.at[i]))
        copies[-1].start()
    return copies


def expert_kernel(capacity, landed_ref, up_ref, down_ref, hidden_out, grads_out, back_out, *scratch):
    up, down, rows, grads, hidden, masked, total, back, weight_sems, hidden_sems, grads_sem, back_sems = scratch
    features, units = up.shape
    tile = masked.shape[2]
    steps = units // tile

    def tile_at(i, part=0, parts=1):
        size = tile // parts
        return pl.ds(pl.multiple_of(i * tile + part * size, size), size)

    def weight_copies(i):
        copies = []
        for n in range(PIECES):
            part = pl.ds(n * (features // PIECES), features // PIECES), tile_at(i)
            copies.append(pltpu.make_async_copy(up_ref.at[part], up.at[part], weight_sems.at[0, i, n]))
        for n in range(PIECES):
            part = tile_at(i, n, PIECES)
            copies.append(pltpu.make_async_copy(down_ref.at[part], down.at[part], weight_sems.at[1, i, n]))
        return copies

    def start_weights(i):
        for copy in weight_copies(i):
            copy.start()

    def hidden_copy(i):
        return pltpu.make_async_copy(hidden.at[:, tile_at(i)], hidden_out.at[:, tile_at(i)], hidden_sems.at[i])

    def row_grad(i):
        return f32_dot(masked[i % 2], up[:, tile_at(i)], ((1,), (1,)))

    def activate(i, preact, hidden_grad):
        hidden[:, tile_at(i)] = jnp.maximum(preact, 0.0).astype(jnp.bfloat16)
        masked[i % 2] = jnp.where(preact > 0, hidden_grad, 0.0).astype(jnp.bfloat16)
        hidden_copy(i).start()

    def products(i):
        for copy in weight_copies(i):
            copy.wait()
        preact = f32_dot(rows[...], up[:, tile_at(i)])
        return preact, f32_dot(grads[...], down[tile_at(i), :], ((1,), (1,)))

    start_weights(0)
    take_apart(landed_ref, capacity, rows, grads)
    grads_copy = pltpu.make_async_copy(grads, grads_out, grads_sem.at[0])
    grads_copy.start()
    for i in range(1, min(1 + AHEAD, steps)):
        start_weights(i)
    total[...] = jnp.zeros_like(total)
    activate(0, *products(0))

    def step(i, carry):
        @pl.when(i + AHEAD < steps)
        def _():
            start_weights(i + AHEAD)

        preact, hidden_grad = products(i)
        total[...] += row_grad(i - 1)
        activate(i, preact, hidden_grad)
        return carry

    lax.fori_loop(1, steps, step, 0)
    total[...] += row_grad(steps - 1)
    leaving = fold_rows(total, capacity, back, back_out, back_sems)
    grads_copy.wait()
    for i in range(steps):
        hidden_copy(i).wait()
    for copy in leaving:
        copy.wait()


def down_grad_kernel(grads_ref, hidden_ref, out_ref):
    out_ref[...] = f32_dot(hidden_ref[...], grads_ref[...], ((0,), (0,))).astype(jnp.bfloat16)


def pick_map_kernel(capacity, ids_ref, after_ref, out_ref):
    tok_rows, rows = ids_ref.shape[1], out_ref.shape[1]
    places = row_places(ids_ref[...], rows // (PAIR * capacity), capacity)
    for j in range(PAIR):
        chosen = either(hits_at(rows, [place + j * capacity for place in places]))
        out_ref[j * tok_rows : (j + 1) * tok_rows, :] = chosen.T


def pick_kernel(map_ref, returned_ref, out_ref):
    tok_rows, width = out_ref.shape[0], returned_ref.shape[1]
    picked = f32_dot(map_ref[...], returned_ref[...]).astype(jnp.bfloat16)
    for j in range(PAIR):
        out_ref[:, j * width : (j + 1) * width] = picked[j * tok_rows : (j + 1) * tok_rows]


def exchange(rows):
    axes = ("row", "col")
    peers = lax.axis_size(axes)
    cut = rows.reshape(peers, rows.shape[0] // peers, rows.shape[1])
    return lax.all_to_all(cut, axes, split_axis=0, concat_axis=0, tiled=True).reshape(rows.shape)


def in_hbm(array):
    return pltpu.with_memory_space_constraint(array, pltpu.HBM)


def held(rows, columns, kind=jnp.bfloat16):
    return pltpu.VMEM((rows, columns), kind)


def shards(tokens, out_grad, expert_ids, gates, up_weight, down_weight):
    tok_rows, features = tokens.shape
    top_count = expert_ids.shape[1]
    units = up_weight.shape[2]
    peers = lax.axis_size(("row", "col"))
    capacity = 3 * tok_rows * top_count // (2 * peers)
    slots, rows, width = peers * capacity, peers * PAIR * capacity, features // PAIR
    tile = min(units, TILE)
    steps = units // tile
    bf16, f32 = jnp.bfloat16, jnp.float32
    shape = jax.ShapeDtypeStruct
    dma = pltpu.SemaphoreType.DMA
    flops = 2 * slots * features * units
    weight_bytes = 2 * features * units

    def cost(matmuls, weights):
        return pl.CostEstimate(flops=matmuls * flops, bytes_accessed=weights * weight_bytes, transcendentals=0)

    ids = expert_ids.T
    hbm = pl.BlockSpec(memory_space=pltpu.HBM)
    vmem = pl.BlockSpec(memory_space=pltpu.VMEM)
    anywhere = pl.BlockSpec(memory_space=pl.ANY)

    sent = pl.pallas_call(
        functools.partial(dispatch_kernel, capacity),
        out_shape=shape((rows, features), bf16),
        in_specs=[hbm, hbm, hbm, hbm],
        scratch_shapes=[
            held(top_count, tok_rows, jnp.int32),
            held(top_count, tok_rows, f32),
            held(tok_rows, features),
            held(tok_rows, features),
            dma((4,)),
        ],
        compiler_params=params(),
        name="dispatch",
    )(*[in_hbm(array) for array in (ids, gates.T, tokens, out_grad)])
    landed = exchange(sent)

    hidden, grads, back = pl.pallas_call(
        functools.partial(expert_kernel, capacity),
        out_shape=(
            pltpu.HBM((slots, units), bf16),
            pltpu.HBM((slots, features), bf16),
            pltpu.HBM((rows, width), bf16),
        ),
        in_specs=[vmem, hbm, hbm],
        out_specs=(hbm, hbm, hbm),
        scratch_shapes=[
            held(features, units),
            held(units, features),
            held(slots, features),
            held(slots, features),
            held(slots, units),
            pltpu.VMEM((2, slots, tile), bf16),
            held(slots, features, f32),
            held(rows, width),
            dma((2, steps, PIECES)),
            dma((steps,)),
            dma((1,)),
            dma((peers // group_size(peers, capacity),)),
        ],
        compiler_params=params(),
        cost_estimate=cost(3, 2),
        name="expert",
    )(landed, in_hbm(up_weight[0]), in_hbm(down_weight[0]))
    returned = exchange(back)

    down_grad = pl.pallas_call(
        down_grad_kernel,
        out_shape=shape((1, units, features), bf16),
        grid=(steps,),
        in_specs=[pl.BlockSpec((slots, features), lambda i: (0, 0)), pl.BlockSpec((slots, tile), lambda i: (0, i))],
        out_specs=pl.BlockSpec((None, tile, features), lambda i: (0, i, 0)),
        compiler_params=params(),
        cost_estimate=cost(1, 1),
        name="down_grad",
    )(in_hbm(grads), in_hbm(hidden))

    pick_map = pl.pallas_call(
        functools.partial(pick_map_kernel, capacity),
        out_shape=shape((PAIR * tok_rows, rows), bf16),
        in_specs=[vmem, anywhere],
        compiler_params=params(),
        name="pick_map",
    )(ids, in_hbm(grads))
    input_grad = pl.pallas_call(
        pick_kernel,
        out_shape=shape((tok_rows, features), bf16),
        compiler_params=params(),
        name="pick",
    )(pick_map, returned)
    return input_grad, down_grad


def pooled_shards(tokens, out_grad, expert_ids, gates, up_weight, down_weight):
    tok_rows = tokens.shape[0]
    top_count = expert_ids.shape[1]
    features = tokens.shape[1]
    groups = lax.axis_size("row")
    col_count = lax.axis_size("col")
    experts = groups * col_count
    capacity = 3 * tok_rows * top_count // (2 * experts)
    flat_ids = expert_ids.reshape(-1)
    onehot = (flat_ids[:, None] == jnp.arange(experts, dtype=jnp.int32)[None, :]).astype(jnp.int32)
    earlier = jnp.cumsum(onehot, axis=0) - onehot
    slot_index = jnp.sum(earlier * onehot, axis=1)
    target = flat_ids * capacity + slot_index
    placer = (jnp.arange(experts * capacity, dtype=jnp.int32)[:, None] == target[None, :]).astype(
        jnp.bfloat16
    )
    token_rows = jnp.repeat(tokens, top_count, axis=0)
    weighted = (
        gates.reshape(-1)[:, None] * jnp.repeat(out_grad, top_count, axis=0).astype(jnp.float32)
    ).astype(jnp.bfloat16)
    send_inputs = jnp.dot(placer, token_rows, preferred_element_type=jnp.float32).astype(
        jnp.bfloat16
    )
    send_grads = jnp.dot(placer, weighted, preferred_element_type=jnp.float32).astype(jnp.bfloat16)
    landed_inputs, landed_grads = (
        lax.all_to_all(
            send_inputs.reshape(experts, capacity, features),
            ("row", "col"),
            split_axis=0,
            concat_axis=0,
            tiled=True,
        ),
        lax.all_to_all(
            send_grads.reshape(experts, capacity, features),
            ("row", "col"),
            split_axis=0,
            concat_axis=0,
            tiled=True,
        ),
    )
    pooled_inputs, pooled_grads = (
        lax.all_gather(landed_inputs, "rep", axis=0, tiled=True),
        lax.all_gather(landed_grads, "rep", axis=0, tiled=True),
    )
    slot_rows = pooled_inputs.shape[0] * capacity
    input_rows = pooled_inputs.reshape(slot_rows, features)
    grad_rows = pooled_grads.reshape(slot_rows, features)
    up_block = up_weight[0]
    down_block = down_weight[0]
    preact = jnp.dot(input_rows, up_block, preferred_element_type=jnp.float32)
    hidden = jnp.maximum(preact, 0.0).astype(jnp.bfloat16)
    hidden_grad = lax.dot_general(
        grad_rows, down_block, (((1,), (1,)), ((), ())), preferred_element_type=jnp.float32
    )
    preact_grad = jnp.where(preact > 0, hidden_grad, 0.0).astype(jnp.bfloat16)
    weight_grad = lax.dot_general(
        hidden, grad_rows, (((0,), (0,)), ((), ())), preferred_element_type=jnp.float32
    )
    down_grad = weight_grad.astype(jnp.bfloat16)[None]
    summed_rows = lax.psum_scatter(
        lax.dot_general(
            preact_grad, up_block, (((1,), (1,)), ((), ())), preferred_element_type=jnp.float32
        ).astype(jnp.bfloat16),
        "rep",
        scatter_dimension=0,
        tiled=True,
    )
    returned = lax.all_to_all(
        summed_rows.reshape(experts, capacity, features),
        ("row", "col"),
        split_axis=0,
        concat_axis=0,
        tiled=True,
    )
    returned = returned.reshape(experts * capacity, features)
    picked = lax.dot_general(
        placer, returned, (((0,), (0,)), ((), ())), preferred_element_type=jnp.float32
    )
    input_grad = jnp.sum(picked.reshape(tok_rows, top_count, features), axis=1).astype(jnp.bfloat16)
    return (input_grad, down_grad)


def solution(mesh):
    by_token = P(("rep", "row", "col"), None)
    by_expert = (P(("row", "col"), None, "rep"), P(("row", "col"), "rep", None))
    return jax.shard_map(
        shards if mesh.shape["rep"] == 1 else pooled_shards,
        mesh=mesh,
        in_specs=(by_token,) * 4 + by_expert,
        out_specs=(by_token, by_expert[1]),
        check_vma=False,
    )
```

```python
import functools

import jax
import jax.numpy as jnp
from jax import lax
from jax.experimental import pallas as pl
from jax.experimental.pallas import tpu as pltpu
from jax.sharding import PartitionSpec as P

VMEM_LIMIT = 48 * 1024 * 1024
PAIR = 2
TILE = 1024
PIECES = 4
NOWHERE = -(1 << 20)


def f32_dot(lhs, rhs, contract=((1,), (0,))):
    return lax.dot_general(lhs, rhs, (contract, ((), ())), preferred_element_type=jnp.float32)


def params():
    return pltpu.CompilerParams(vmem_limit_bytes=VMEM_LIMIT)


def row_places(ids, experts, capacity):
    tok_rows = ids.shape[1]
    names = lax.broadcasted_iota(jnp.int32, (experts, tok_rows), 0)
    chosen = [names == ids[k : k + 1, :] for k in range(ids.shape[0])]
    member = functools.reduce(jnp.logical_or, chosen).astype(jnp.bfloat16)
    before = (
        lax.broadcasted_iota(jnp.int32, (tok_rows, tok_rows), 0)
        < lax.broadcasted_iota(jnp.int32, (tok_rows, tok_rows), 1)
    ).astype(jnp.bfloat16)
    rank = f32_dot(member, before).astype(jnp.int32)
    place = names * (PAIR * capacity) + rank
    return [jnp.sum(jnp.where(pick, place, 0), axis=0, keepdims=True) for pick in chosen]


def hits_at(rows, places):
    at = lax.broadcasted_iota(jnp.int32, (rows, places[0].shape[1]), 0)
    return [at == place for place in places]


def either(hits):
    return functools.reduce(jnp.logical_or, hits).astype(jnp.bfloat16)


def started(pairs, sems):
    copies = [pltpu.make_async_copy(*pair, sems.at[i]) for i, pair in enumerate(pairs)]
    for copy in copies:
        copy.start()
    return copies


def dispatch_kernel(capacity, *refs):
    sources, (out_ref, ids_ref, gates_ref, both_ref, sems) = refs[:4], refs[4:]
    tok_rows = both_ref.shape[0] // 2
    targets = ids_ref, gates_ref, both_ref.at[pl.ds(0, tok_rows)], both_ref.at[pl.ds(tok_rows, tok_rows)]
    ids_copy, gates_copy, tokens_copy, grad_copy = started(zip(sources, targets), sems)
    rows = out_ref.shape[0]
    ids_copy.wait()
    places = row_places(ids_ref[...], rows // (PAIR * capacity), capacity)
    token_hits = hits_at(rows, places)
    grad_hits = hits_at(rows, [place + capacity for place in places])
    gates_copy.wait()
    scales = [jnp.where(hit, 1.0, 0.0) for hit in token_hits]
    scales += [jnp.where(hit, gates_ref[k : k + 1, :], 0.0) for k, hit in enumerate(grad_hits)]
    scale = jnp.sum(sum(scales), axis=1, keepdims=True)
    gather = jnp.concatenate([either(token_hits), either(grad_hits)], axis=1)
    tokens_copy.wait()
    grad_copy.wait()
    out_ref[...] = (scale * f32_dot(gather, both_ref[...])).astype(jnp.bfloat16)


def paired_rows(number, capacity):
    owner = jnp.floor((number.astype(jnp.float32) + 0.5) * (1.0 / capacity)).astype(jnp.int32)
    return number + owner * ((PAIR - 1) * capacity)


def group_size(peers, capacity):
    size = 1
    while peers % (2 * size) == 0 and size * PAIR * capacity < 192:
        size *= 2
    return size


def take_apart(landed_ref, capacity, rows_ref, grads_ref):
    size = group_size(landed_ref.shape[0] // (PAIR * capacity), capacity)
    slots, rows = size * capacity, size * PAIR * capacity
    at = lax.broadcasted_iota(jnp.int32, (slots, rows), 1)
    source = paired_rows(lax.broadcasted_iota(jnp.int32, (slots, 1), 0), capacity)
    mover = jnp.concatenate([(at == source + j * capacity).astype(jnp.bfloat16) for j in range(PAIR)], axis=0)
    for i in range(rows_ref.shape[0] // slots):
        taken = f32_dot(mover, landed_ref[i * rows : (i + 1) * rows, :]).astype(jnp.bfloat16)
        rows_ref[i * slots : (i + 1) * slots, :] = taken[:slots]
        grads_ref[i * slots : (i + 1) * slots, :] = taken[slots:]


def fold_rows(plain_ref, capacity, folded_ref, out_ref, sems):
    size = group_size(plain_ref.shape[0] // capacity, capacity)
    slots, rows = size * capacity, size * PAIR * capacity
    width = folded_ref.shape[1]
    at = lax.broadcasted_iota(jnp.int32, (rows, slots), 0)
    target = paired_rows(lax.broadcasted_iota(jnp.int32, (1, slots), 1), capacity)
    mover = jnp.concatenate([(at == target + j * capacity).astype(jnp.bfloat16) for j in range(PAIR)], axis=1)
    copies = []
    for i in range(plain_ref.shape[0] // slots):
        plain = plain_ref[i * slots : (i + 1) * slots, :].astype(jnp.bfloat16)
        halves = jnp.concatenate([plain[:, j * width : (j + 1) * width] for j in range(PAIR)], axis=0)
        part = slice(i * rows, (i + 1) * rows)
        folded_ref[part, :] = f32_dot(mover, halves).astype(jnp.bfloat16)
        copies.append(pltpu.make_async_copy(folded_ref.at[part], out_ref.at[part], sems.at[i]))
        copies[-1].start()
    return copies


def unit_tiles(units):
    size = min(units, TILE)
    return [(start, size) for start in range(0, units, size)]


def expert_kernel(capacity, landed_ref, up_ref, down_ref, hidden_out, grads_out, back_out, *scratch):
    up, down, rows, grads, hidden, masked, total, back, weight_sems, hidden_sems, grads_sem, back_sems = scratch
    tiles = unit_tiles(up.shape[1])
    features = up.shape[0]

    def weight_copies(i):
        start, size = tiles[i]
        copies = []
        for n in range(PIECES):
            part = pl.ds(n * (features // PIECES), features // PIECES), pl.ds(start, size)
            copies.append(pltpu.make_async_copy(up_ref.at[part], up.at[part], weight_sems.at[0, i, n]))
        for n in range(PIECES):
            part = pl.ds(start + n * (size // PIECES), size // PIECES)
            copies.append(pltpu.make_async_copy(down_ref.at[part], down.at[part], weight_sems.at[1, i, n]))
        return copies

    def start_weights(i):
        if i < len(tiles):
            arriving[i] = weight_copies(i)
            for copy in arriving[i]:
                copy.start()

    def add_row_grad(i):
        start, size = tiles[i]
        part = f32_dot(masked[i % 2, :, :size], up[:, start : start + size], ((1,), (1,)))
        total[...] = part if i == 0 else total[...] + part

    arriving, leaving = {}, []
    start_weights(0)
    take_apart(landed_ref, capacity, rows, grads)
    leaving.append(pltpu.make_async_copy(grads, grads_out, grads_sem.at[0]))
    leaving[-1].start()
    start_weights(1)
    for i, (start, size) in enumerate(tiles):
        here = slice(start, start + size)
        for copy in arriving[i]:
            copy.wait()
        start_weights(i + 2)
        preact = f32_dot(rows[...], up[:, here])
        hidden_grad = f32_dot(grads[...], down[here, :], ((1,), (1,)))
        if i:
            add_row_grad(i - 1)
        hidden[:, here] = jnp.maximum(preact, 0.0).astype(jnp.bfloat16)
        masked[i % 2, :, :size] = jnp.where(preact > 0, hidden_grad, 0.0).astype(jnp.bfloat16)
        leaving.append(pltpu.make_async_copy(hidden.at[:, here], hidden_out.at[:, here], hidden_sems.at[i]))
        leaving[-1].start()
    add_row_grad(len(tiles) - 1)
    for copy in leaving + fold_rows(total, capacity, back, back_out, back_sems):
        copy.wait()


def down_grad_kernel(grads_ref, hidden_ref, out_ref):
    out_ref[...] = f32_dot(hidden_ref[...], grads_ref[...], ((0,), (0,))).astype(jnp.bfloat16)


def pick_map_kernel(capacity, ids_ref, after_ref, out_ref):
    tok_rows, rows = ids_ref.shape[1], out_ref.shape[1]
    places = row_places(ids_ref[...], rows // (PAIR * capacity), capacity)
    for j in range(PAIR):
        chosen = either(hits_at(rows, [place + j * capacity for place in places]))
        out_ref[j * tok_rows : (j + 1) * tok_rows, :] = chosen.T


def pick_kernel(map_ref, returned_ref, out_ref):
    tok_rows, width = out_ref.shape[0], returned_ref.shape[1]
    picked = f32_dot(map_ref[...], returned_ref[...]).astype(jnp.bfloat16)
    for j in range(PAIR):
        out_ref[:, j * width : (j + 1) * width] = picked[j * tok_rows : (j + 1) * tok_rows]


def exchange(rows):
    axes = ("row", "col")
    peers = lax.axis_size(axes)
    cut = rows.reshape(peers, rows.shape[0] // peers, rows.shape[1])
    return lax.all_to_all(cut, axes, split_axis=0, concat_axis=0, tiled=True).reshape(rows.shape)


def in_hbm(array):
    return pltpu.with_memory_space_constraint(array, pltpu.HBM)


def held(rows, columns, kind=jnp.bfloat16):
    return pltpu.VMEM((rows, columns), kind)


def shards(tokens, out_grad, expert_ids, gates, up_weight, down_weight):
    tok_rows, features = tokens.shape
    top_count = expert_ids.shape[1]
    units = up_weight.shape[2]
    peers = lax.axis_size(("row", "col"))
    capacity = 3 * tok_rows * top_count // (2 * peers)
    slots, rows, width = peers * capacity, peers * PAIR * capacity, features // PAIR
    tile = min(units, TILE // 2)
    steps = units // tile
    bf16, f32 = jnp.bfloat16, jnp.float32
    shape = jax.ShapeDtypeStruct
    dma = pltpu.SemaphoreType.DMA
    flops = 2 * slots * features * units
    weight_bytes = 2 * features * units

    def cost(matmuls, weights):
        return pl.CostEstimate(flops=matmuls * flops, bytes_accessed=weights * weight_bytes, transcendentals=0)

    ids = expert_ids.T
    hbm = pl.BlockSpec(memory_space=pltpu.HBM)
    vmem = pl.BlockSpec(memory_space=pltpu.VMEM)
    anywhere = pl.BlockSpec(memory_space=pl.ANY)
    tiles = unit_tiles(units)

    sent = pl.pallas_call(
        functools.partial(dispatch_kernel, capacity),
        out_shape=shape((rows, features), bf16),
        in_specs=[hbm, hbm, hbm, hbm],
        scratch_shapes=[
            held(top_count, tok_rows, jnp.int32),
            held(top_count, tok_rows, f32),
            held(2 * tok_rows, features),
            dma((4,)),
        ],
        compiler_params=params(),
        name="dispatch",
    )(*[in_hbm(array) for array in (ids, gates.T, tokens, out_grad)])
    landed = exchange(sent)

    hidden, grads, back = pl.pallas_call(
        functools.partial(expert_kernel, capacity),
        out_shape=(
            pltpu.HBM((slots, units), bf16),
            pltpu.HBM((slots, features), bf16),
            pltpu.HBM((rows, width), bf16),
        ),
        in_specs=[vmem, hbm, hbm],
        out_specs=(hbm, hbm, hbm),
        scratch_shapes=[
            held(features, units),
            held(units, features),
            held(slots, features),
            held(slots, features),
            held(slots, units),
            pltpu.VMEM((2, slots, tiles[0][1]), bf16),
            held(slots, features, f32),
            held(rows, width),
            dma((2, len(tiles), PIECES)),
            dma((len(tiles),)),
            dma((1,)),
            dma((peers // group_size(peers, capacity),)),
        ],
        compiler_params=params(),
        cost_estimate=cost(3, 2),
        name="expert",
    )(landed, in_hbm(up_weight[0]), in_hbm(down_weight[0]))
    returned = exchange(back)

    down_grad = pl.pallas_call(
        down_grad_kernel,
        out_shape=shape((1, units, features), bf16),
        grid=(steps,),
        in_specs=[pl.BlockSpec((slots, features), lambda i: (0, 0)), pl.BlockSpec((slots, tile), lambda i: (0, i))],
        out_specs=pl.BlockSpec((None, tile, features), lambda i: (0, i, 0)),
        compiler_params=params(),
        cost_estimate=cost(1, 1),
        name="down_grad",
    )(in_hbm(grads), in_hbm(hidden))

    pick_map = pl.pallas_call(
        functools.partial(pick_map_kernel, capacity),
        out_shape=shape((PAIR * tok_rows, rows), bf16),
        in_specs=[vmem, anywhere],
        compiler_params=params(),
        name="pick_map",
    )(ids, in_hbm(grads))
    input_grad = pl.pallas_call(
        pick_kernel,
        out_shape=shape((tok_rows, features), bf16),
        compiler_params=params(),
        name="pick",
    )(pick_map, returned)
    return input_grad, down_grad


def pooled_shards(tokens, out_grad, expert_ids, gates, up_weight, down_weight):
    tok_rows = tokens.shape[0]
    top_count = expert_ids.shape[1]
    features = tokens.shape[1]
    groups = lax.axis_size("row")
    col_count = lax.axis_size("col")
    experts = groups * col_count
    capacity = 3 * tok_rows * top_count // (2 * experts)
    flat_ids = expert_ids.reshape(-1)
    onehot = (flat_ids[:, None] == jnp.arange(experts, dtype=jnp.int32)[None, :]).astype(jnp.int32)
    earlier = jnp.cumsum(onehot, axis=0) - onehot
    slot_index = jnp.sum(earlier * onehot, axis=1)
    target = flat_ids * capacity + slot_index
    placer = (jnp.arange(experts * capacity, dtype=jnp.int32)[:, None] == target[None, :]).astype(
        jnp.bfloat16
    )
    token_rows = jnp.repeat(tokens, top_count, axis=0)
    weighted = (
        gates.reshape(-1)[:, None] * jnp.repeat(out_grad, top_count, axis=0).astype(jnp.float32)
    ).astype(jnp.bfloat16)
    send_inputs = jnp.dot(placer, token_rows, preferred_element_type=jnp.float32).astype(
        jnp.bfloat16
    )
    send_grads = jnp.dot(placer, weighted, preferred_element_type=jnp.float32).astype(jnp.bfloat16)
    landed_inputs, landed_grads = (
        lax.all_to_all(
            send_inputs.reshape(experts, capacity, features),
            ("row", "col"),
            split_axis=0,
            concat_axis=0,
            tiled=True,
        ),
        lax.all_to_all(
            send_grads.reshape(experts, capacity, features),
            ("row", "col"),
            split_axis=0,
            concat_axis=0,
            tiled=True,
        ),
    )
    pooled_inputs, pooled_grads = (
        lax.all_gather(landed_inputs, "rep", axis=0, tiled=True),
        lax.all_gather(landed_grads, "rep", axis=0, tiled=True),
    )
    slot_rows = pooled_inputs.shape[0] * capacity
    input_rows = pooled_inputs.reshape(slot_rows, features)
    grad_rows = pooled_grads.reshape(slot_rows, features)
    up_block = up_weight[0]
    down_block = down_weight[0]
    preact = jnp.dot(input_rows, up_block, preferred_element_type=jnp.float32)
    hidden = jnp.maximum(preact, 0.0).astype(jnp.bfloat16)
    hidden_grad = lax.dot_general(
        grad_rows, down_block, (((1,), (1,)), ((), ())), preferred_element_type=jnp.float32
    )
    preact_grad = jnp.where(preact > 0, hidden_grad, 0.0).astype(jnp.bfloat16)
    weight_grad = lax.dot_general(
        hidden, grad_rows, (((0,), (0,)), ((), ())), preferred_element_type=jnp.float32
    )
    down_grad = weight_grad.astype(jnp.bfloat16)[None]
    summed_rows = lax.psum_scatter(
        lax.dot_general(
            preact_grad, up_block, (((1,), (1,)), ((), ())), preferred_element_type=jnp.float32
        ).astype(jnp.bfloat16),
        "rep",
        scatter_dimension=0,
        tiled=True,
    )
    returned = lax.all_to_all(
        summed_rows.reshape(experts, capacity, features),
        ("row", "col"),
        split_axis=0,
        concat_axis=0,
        tiled=True,
    )
    returned = returned.reshape(experts * capacity, features)
    picked = lax.dot_general(
        placer, returned, (((0,), (0,)), ((), ())), preferred_element_type=jnp.float32
    )
    input_grad = jnp.sum(picked.reshape(tok_rows, top_count, features), axis=1).astype(jnp.bfloat16)
    return (input_grad, down_grad)


def solution(mesh):
    by_token = P(("rep", "row", "col"), None)
    by_expert = (P(("row", "col"), None, "rep"), P(("row", "col"), "rep", None))
    return jax.shard_map(
        shards if mesh.shape["rep"] == 1 else pooled_shards,
        mesh=mesh,
        in_specs=(by_token,) * 4 + by_expert,
        out_specs=(by_token, by_expert[1]),
        check_vma=False,
    )
```

```python
import functools

import jax
import jax.numpy as jnp
from jax import lax
from jax.experimental import pallas as pl
from jax.experimental.pallas import tpu as pltpu
from jax.sharding import PartitionSpec as P

VMEM_LIMIT = 54 * 1024 * 1024
PAIR = 2
TILE = 1024
PIECES = 4
NOWHERE = -(1 << 20)


def f32_dot(lhs, rhs, contract=((1,), (0,))):
    return lax.dot_general(lhs, rhs, (contract, ((), ())), preferred_element_type=jnp.float32)


def params():
    return pltpu.CompilerParams(vmem_limit_bytes=VMEM_LIMIT)


def row_places(ids, experts, capacity):
    tok_rows = ids.shape[1]
    names = lax.broadcasted_iota(jnp.int32, (experts, tok_rows), 0)
    chosen = [names == ids[k : k + 1, :] for k in range(ids.shape[0])]
    member = functools.reduce(jnp.logical_or, chosen).astype(jnp.bfloat16)
    before = (
        lax.broadcasted_iota(jnp.int32, (tok_rows, tok_rows), 0)
        < lax.broadcasted_iota(jnp.int32, (tok_rows, tok_rows), 1)
    ).astype(jnp.bfloat16)
    rank = f32_dot(member, before).astype(jnp.int32)
    place = names * (PAIR * capacity) + rank
    return [jnp.sum(jnp.where(pick, place, 0), axis=0, keepdims=True) for pick in chosen]


def hits_at(rows, places):
    at = lax.broadcasted_iota(jnp.int32, (rows, places[0].shape[1]), 0)
    return [at == place for place in places]


def either(hits):
    return functools.reduce(jnp.logical_or, hits).astype(jnp.bfloat16)


def started(pairs, sems):
    copies = [pltpu.make_async_copy(*pair, sems.at[i]) for i, pair in enumerate(pairs)]
    for copy in copies:
        copy.start()
    return copies


def dispatch_kernel(capacity, *refs):
    sources, (out_ref, ids_ref, gates_ref, both_ref, sems) = refs[:4], refs[4:]
    tok_rows = both_ref.shape[0] // 2
    targets = ids_ref, gates_ref, both_ref.at[pl.ds(0, tok_rows)], both_ref.at[pl.ds(tok_rows, tok_rows)]
    ids_copy, gates_copy, tokens_copy, grad_copy = started(zip(sources, targets), sems)
    rows = out_ref.shape[0]
    ids_copy.wait()
    places = row_places(ids_ref[...], rows // (PAIR * capacity), capacity)
    token_hits = hits_at(rows, places)
    grad_hits = hits_at(rows, [place + capacity for place in places])
    gates_copy.wait()
    scales = [jnp.where(hit, 1.0, 0.0) for hit in token_hits]
    scales += [jnp.where(hit, gates_ref[k : k + 1, :], 0.0) for k, hit in enumerate(grad_hits)]
    scale = jnp.sum(sum(scales), axis=1, keepdims=True)
    gather = jnp.concatenate([either(token_hits), either(grad_hits)], axis=1)
    tokens_copy.wait()
    grad_copy.wait()
    out_ref[...] = (scale * f32_dot(gather, both_ref[...])).astype(jnp.bfloat16)


def paired_rows(number, capacity):
    owner = jnp.floor((number.astype(jnp.float32) + 0.5) * (1.0 / capacity)).astype(jnp.int32)
    return number + owner * ((PAIR - 1) * capacity)


def group_size(peers, capacity):
    size = 1
    while peers % (2 * size) == 0 and size * PAIR * capacity < 192:
        size *= 2
    return size


def take_apart(landed_ref, capacity, rows_ref, grads_ref):
    size = group_size(landed_ref.shape[0] // (PAIR * capacity), capacity)
    slots, rows = size * capacity, size * PAIR * capacity
    at = lax.broadcasted_iota(jnp.int32, (slots, rows), 1)
    source = paired_rows(lax.broadcasted_iota(jnp.int32, (slots, 1), 0), capacity)
    mover = jnp.concatenate([(at == source + j * capacity).astype(jnp.bfloat16) for j in range(PAIR)], axis=0)
    for i in range(rows_ref.shape[0] // slots):
        taken = f32_dot(mover, landed_ref[i * rows : (i + 1) * rows, :]).astype(jnp.bfloat16)
        rows_ref[i * slots : (i + 1) * slots, :] = taken[:slots]
        grads_ref[i * slots : (i + 1) * slots, :] = taken[slots:]


def fold_rows(plain_ref, capacity, folded_ref, out_ref, sems):
    size = group_size(plain_ref.shape[0] // capacity, capacity)
    slots, rows = size * capacity, size * PAIR * capacity
    width = folded_ref.shape[1]
    at = lax.broadcasted_iota(jnp.int32, (rows, slots), 0)
    target = paired_rows(lax.broadcasted_iota(jnp.int32, (1, slots), 1), capacity)
    mover = jnp.concatenate([(at == target + j * capacity).astype(jnp.bfloat16) for j in range(PAIR)], axis=1)
    copies = []
    for i in range(plain_ref.shape[0] // slots):
        plain = plain_ref[i * slots : (i + 1) * slots, :].astype(jnp.bfloat16)
        halves = jnp.concatenate([plain[:, j * width : (j + 1) * width] for j in range(PAIR)], axis=0)
        part = slice(i * rows, (i + 1) * rows)
        folded_ref[part, :] = f32_dot(mover, halves).astype(jnp.bfloat16)
        copies.append(pltpu.make_async_copy(folded_ref.at[part], out_ref.at[part], sems.at[i]))
        copies[-1].start()
    return copies


def unit_tiles(units):
    size = min(units, TILE)
    return [(start, size) for start in range(0, units, size)]


def turn_kernel(up_ref, down_ref, after_ref, up_out, down_out):
    up_out[...] = up_ref[...].T
    down_out[...] = down_ref[...].T


def expert_kernel(
    capacity, landed_ref, up_ref, up_turned_ref, down_turned_ref, hidden_out, grads_out, back_out, *scratch
):
    up, up_turned, down_turned, rows, grads, hidden, masked, total, back, weight_sems, hidden_sems, grads_sem, back_sems = scratch
    tiles = unit_tiles(up.shape[1])
    features = up.shape[0]

    def weight_copies(i):
        start, size = tiles[i]
        copies = []
        for n in range(PIECES):
            part = pl.ds(n * (features // PIECES), features // PIECES), pl.ds(start, size)
            copies.append(pltpu.make_async_copy(up_ref.at[part], up.at[part], weight_sems.at[0, i, n]))
        for n in range(PIECES):
            part = pl.ds(n * (features // PIECES), features // PIECES), pl.ds(start, size)
            copies.append(
                pltpu.make_async_copy(down_turned_ref.at[part], down_turned.at[part], weight_sems.at[1, i, n])
            )
        for n in range(PIECES):
            part = pl.ds(start + n * (size // PIECES), size // PIECES)
            copies.append(pltpu.make_async_copy(up_turned_ref.at[part], up_turned.at[part], weight_sems.at[2, i, n]))
        return copies

    def start_weights(i):
        if i < len(tiles):
            arriving[i] = weight_copies(i)
            for copy in arriving[i]:
                copy.start()

    def add_row_grad(i):
        start, size = tiles[i]
        part = f32_dot(masked[i % 2, :, :size], up_turned[start : start + size, :])
        total[...] = part if i == 0 else total[...] + part

    arriving, leaving = {}, []
    start_weights(0)
    take_apart(landed_ref, capacity, rows, grads)
    leaving.append(pltpu.make_async_copy(grads, grads_out, grads_sem.at[0]))
    leaving[-1].start()
    start_weights(1)
    for i, (start, size) in enumerate(tiles):
        here = slice(start, start + size)
        for copy in arriving[i]:
            copy.wait()
        start_weights(i + 2)
        preact = f32_dot(rows[...], up[:, here])
        hidden_grad = f32_dot(grads[...], down_turned[:, here])
        if i:
            add_row_grad(i - 1)
        hidden[:, here] = jnp.maximum(preact, 0.0).astype(jnp.bfloat16)
        masked[i % 2, :, :size] = jnp.where(preact > 0, hidden_grad, 0.0).astype(jnp.bfloat16)
        leaving.append(pltpu.make_async_copy(hidden.at[:, here], hidden_out.at[:, here], hidden_sems.at[i]))
        leaving[-1].start()
    add_row_grad(len(tiles) - 1)
    for copy in leaving + fold_rows(total, capacity, back, back_out, back_sems):
        copy.wait()


def down_grad_kernel(grads_ref, hidden_ref, out_ref):
    out_ref[...] = f32_dot(hidden_ref[...], grads_ref[...], ((0,), (0,))).astype(jnp.bfloat16)


def pick_map_kernel(capacity, ids_ref, after_ref, out_ref):
    tok_rows, rows = ids_ref.shape[1], out_ref.shape[1]
    places = row_places(ids_ref[...], rows // (PAIR * capacity), capacity)
    for j in range(PAIR):
        chosen = either(hits_at(rows, [place + j * capacity for place in places]))
        out_ref[j * tok_rows : (j + 1) * tok_rows, :] = chosen.T


def pick_kernel(map_ref, returned_ref, out_ref):
    tok_rows, width = out_ref.shape[0], returned_ref.shape[1]
    picked = f32_dot(map_ref[...], returned_ref[...]).astype(jnp.bfloat16)
    for j in range(PAIR):
        out_ref[:, j * width : (j + 1) * width] = picked[j * tok_rows : (j + 1) * tok_rows]


def exchange(rows):
    axes = ("row", "col")
    peers = lax.axis_size(axes)
    cut = rows.reshape(peers, rows.shape[0] // peers, rows.shape[1])
    return lax.all_to_all(cut, axes, split_axis=0, concat_axis=0, tiled=True).reshape(rows.shape)


def in_hbm(array):
    return pltpu.with_memory_space_constraint(array, pltpu.HBM)


def held(rows, columns, kind=jnp.bfloat16):
    return pltpu.VMEM((rows, columns), kind)


def shards(tokens, out_grad, expert_ids, gates, up_weight, down_weight):
    tok_rows, features = tokens.shape
    top_count = expert_ids.shape[1]
    units = up_weight.shape[2]
    peers = lax.axis_size(("row", "col"))
    capacity = 3 * tok_rows * top_count // (2 * peers)
    slots, rows, width = peers * capacity, peers * PAIR * capacity, features // PAIR
    tile = min(units, TILE // 2)
    steps = units // tile
    bf16, f32 = jnp.bfloat16, jnp.float32
    shape = jax.ShapeDtypeStruct
    dma = pltpu.SemaphoreType.DMA
    flops = 2 * slots * features * units
    weight_bytes = 2 * features * units

    def cost(matmuls, weights):
        return pl.CostEstimate(flops=matmuls * flops, bytes_accessed=weights * weight_bytes, transcendentals=0)

    ids = expert_ids.T
    hbm = pl.BlockSpec(memory_space=pltpu.HBM)
    vmem = pl.BlockSpec(memory_space=pltpu.VMEM)
    anywhere = pl.BlockSpec(memory_space=pl.ANY)
    tiles = unit_tiles(units)

    sent = pl.pallas_call(
        functools.partial(dispatch_kernel, capacity),
        out_shape=shape((rows, features), bf16),
        in_specs=[hbm, hbm, hbm, hbm],
        scratch_shapes=[
            held(top_count, tok_rows, jnp.int32),
            held(top_count, tok_rows, f32),
            held(2 * tok_rows, features),
            dma((4,)),
        ],
        compiler_params=params(),
        name="dispatch",
    )(*[in_hbm(array) for array in (ids, gates.T, tokens, out_grad)])
    landed = exchange(sent)

    turned_up, turned_down = pl.pallas_call(
        turn_kernel,
        out_shape=(shape((units, features), bf16), shape((features, units), bf16)),
        grid=(steps,),
        in_specs=[
            pl.BlockSpec((None, features, tile), lambda i: (0, 0, i)),
            pl.BlockSpec((None, tile, features), lambda i: (0, i, 0)),
            anywhere,
        ],
        out_specs=(
            pl.BlockSpec((tile, features), lambda i: (i, 0)),
            pl.BlockSpec((features, tile), lambda i: (0, i)),
        ),
        compiler_params=params(),
        cost_estimate=cost(0, 4),
        name="turn",
    )(up_weight, down_weight, sent)

    hidden, grads, back = pl.pallas_call(
        functools.partial(expert_kernel, capacity),
        out_shape=(
            pltpu.HBM((slots, units), bf16),
            pltpu.HBM((slots, features), bf16),
            pltpu.HBM((rows, width), bf16),
        ),
        in_specs=[vmem, hbm, hbm, hbm],
        out_specs=(hbm, hbm, hbm),
        scratch_shapes=[
            held(features, units),
            held(units, features),
            held(features, units),
            held(slots, features),
            held(slots, features),
            held(slots, units),
            pltpu.VMEM((2, slots, tiles[0][1]), bf16),
            held(slots, features, f32),
            held(rows, width),
            dma((3, len(tiles), PIECES)),
            dma((len(tiles),)),
            dma((1,)),
            dma((peers // group_size(peers, capacity),)),
        ],
        compiler_params=params(),
        cost_estimate=cost(3, 2),
        name="expert",
    )(landed, *[in_hbm(weight) for weight in (up_weight[0], turned_up, turned_down)])
    returned = exchange(back)

    down_grad = pl.pallas_call(
        down_grad_kernel,
        out_shape=shape((1, units, features), bf16),
        grid=(steps,),
        in_specs=[pl.BlockSpec((slots, features), lambda i: (0, 0)), pl.BlockSpec((slots, tile), lambda i: (0, i))],
        out_specs=pl.BlockSpec((None, tile, features), lambda i: (0, i, 0)),
        compiler_params=params(),
        cost_estimate=cost(1, 1),
        name="down_grad",
    )(in_hbm(grads), in_hbm(hidden))

    pick_map = pl.pallas_call(
        functools.partial(pick_map_kernel, capacity),
        out_shape=shape((PAIR * tok_rows, rows), bf16),
        in_specs=[vmem, anywhere],
        compiler_params=params(),
        name="pick_map",
    )(ids, in_hbm(grads))
    input_grad = pl.pallas_call(
        pick_kernel,
        out_shape=shape((tok_rows, features), bf16),
        compiler_params=params(),
        name="pick",
    )(pick_map, returned)
    return input_grad, down_grad


def pooled_shards(tokens, out_grad, expert_ids, gates, up_weight, down_weight):
    tok_rows = tokens.shape[0]
    top_count = expert_ids.shape[1]
    features = tokens.shape[1]
    groups = lax.axis_size("row")
    col_count = lax.axis_size("col")
    experts = groups * col_count
    capacity = 3 * tok_rows * top_count // (2 * experts)
    flat_ids = expert_ids.reshape(-1)
    onehot = (flat_ids[:, None] == jnp.arange(experts, dtype=jnp.int32)[None, :]).astype(jnp.int32)
    earlier = jnp.cumsum(onehot, axis=0) - onehot
    slot_index = jnp.sum(earlier * onehot, axis=1)
    target = flat_ids * capacity + slot_index
    placer = (jnp.arange(experts * capacity, dtype=jnp.int32)[:, None] == target[None, :]).astype(
        jnp.bfloat16
    )
    token_rows = jnp.repeat(tokens, top_count, axis=0)
    weighted = (
        gates.reshape(-1)[:, None] * jnp.repeat(out_grad, top_count, axis=0).astype(jnp.float32)
    ).astype(jnp.bfloat16)
    send_inputs = jnp.dot(placer, token_rows, preferred_element_type=jnp.float32).astype(
        jnp.bfloat16
    )
    send_grads = jnp.dot(placer, weighted, preferred_element_type=jnp.float32).astype(jnp.bfloat16)
    landed_inputs, landed_grads = (
        lax.all_to_all(
            send_inputs.reshape(experts, capacity, features),
            ("row", "col"),
            split_axis=0,
            concat_axis=0,
            tiled=True,
        ),
        lax.all_to_all(
            send_grads.reshape(experts, capacity, features),
            ("row", "col"),
            split_axis=0,
            concat_axis=0,
            tiled=True,
        ),
    )
    pooled_inputs, pooled_grads = (
        lax.all_gather(landed_inputs, "rep", axis=0, tiled=True),
        lax.all_gather(landed_grads, "rep", axis=0, tiled=True),
    )
    slot_rows = pooled_inputs.shape[0] * capacity
    input_rows = pooled_inputs.reshape(slot_rows, features)
    grad_rows = pooled_grads.reshape(slot_rows, features)
    up_block = up_weight[0]
    down_block = down_weight[0]
    preact = jnp.dot(input_rows, up_block, preferred_element_type=jnp.float32)
    hidden = jnp.maximum(preact, 0.0).astype(jnp.bfloat16)
    hidden_grad = lax.dot_general(
        grad_rows, down_block, (((1,), (1,)), ((), ())), preferred_element_type=jnp.float32
    )
    preact_grad = jnp.where(preact > 0, hidden_grad, 0.0).astype(jnp.bfloat16)
    weight_grad = lax.dot_general(
        hidden, grad_rows, (((0,), (0,)), ((), ())), preferred_element_type=jnp.float32
    )
    down_grad = weight_grad.astype(jnp.bfloat16)[None]
    summed_rows = lax.psum_scatter(
        lax.dot_general(
            preact_grad, up_block, (((1,), (1,)), ((), ())), preferred_element_type=jnp.float32
        ).astype(jnp.bfloat16),
        "rep",
        scatter_dimension=0,
        tiled=True,
    )
    returned = lax.all_to_all(
        summed_rows.reshape(experts, capacity, features),
        ("row", "col"),
        split_axis=0,
        concat_axis=0,
        tiled=True,
    )
    returned = returned.reshape(experts * capacity, features)
    picked = lax.dot_general(
        placer, returned, (((0,), (0,)), ((), ())), preferred_element_type=jnp.float32
    )
    input_grad = jnp.sum(picked.reshape(tok_rows, top_count, features), axis=1).astype(jnp.bfloat16)
    return (input_grad, down_grad)


def solution(mesh):
    by_token = P(("rep", "row", "col"), None)
    by_expert = (P(("row", "col"), None, "rep"), P(("row", "col"), "rep", None))
    return jax.shard_map(
        shards if mesh.shape["rep"] == 1 else pooled_shards,
        mesh=mesh,
        in_specs=(by_token,) * 4 + by_expert,
        out_specs=(by_token, by_expert[1]),
        check_vma=False,
    )
```

```python
import functools

import jax
import jax.numpy as jnp
from jax import lax
from jax.experimental import pallas as pl
from jax.experimental.pallas import tpu as pltpu
from jax.sharding import PartitionSpec as P

VMEM_LIMIT = 54 * 1024 * 1024
PAIR = 2
TILE = 1024
PIECES = 4
NOWHERE = -(1 << 20)


def f32_dot(lhs, rhs, contract=((1,), (0,))):
    return lax.dot_general(lhs, rhs, (contract, ((), ())), preferred_element_type=jnp.float32)


def params():
    return pltpu.CompilerParams(vmem_limit_bytes=VMEM_LIMIT)


def row_places(ids, experts, capacity):
    tok_rows = ids.shape[1]
    names = lax.broadcasted_iota(jnp.int32, (experts, tok_rows), 0)
    chosen = [names == ids[k : k + 1, :] for k in range(ids.shape[0])]
    member = functools.reduce(jnp.logical_or, chosen).astype(jnp.bfloat16)
    before = (
        lax.broadcasted_iota(jnp.int32, (tok_rows, tok_rows), 0)
        < lax.broadcasted_iota(jnp.int32, (tok_rows, tok_rows), 1)
    ).astype(jnp.bfloat16)
    rank = f32_dot(member, before).astype(jnp.int32)
    place = names * (PAIR * capacity) + rank
    return [jnp.sum(jnp.where(pick, place, 0), axis=0, keepdims=True) for pick in chosen]


def hits_at(rows, places):
    at = lax.broadcasted_iota(jnp.int32, (rows, places[0].shape[1]), 0)
    return [at == place for place in places]


def either(hits):
    return functools.reduce(jnp.logical_or, hits).astype(jnp.bfloat16)


def started(pairs, sems):
    copies = [pltpu.make_async_copy(*pair, sems.at[i]) for i, pair in enumerate(pairs)]
    for copy in copies:
        copy.start()
    return copies


def dispatch_kernel(capacity, *refs):
    sources, (out_ref, ids_ref, gates_ref, both_ref, sems) = refs[:4], refs[4:]
    tok_rows = both_ref.shape[0] // 2
    targets = ids_ref, gates_ref, both_ref.at[pl.ds(0, tok_rows)], both_ref.at[pl.ds(tok_rows, tok_rows)]
    ids_copy, gates_copy, tokens_copy, grad_copy = started(zip(sources, targets), sems)
    rows = out_ref.shape[0]
    ids_copy.wait()
    places = row_places(ids_ref[...], rows // (PAIR * capacity), capacity)
    token_hits = hits_at(rows, places)
    grad_hits = hits_at(rows, [place + capacity for place in places])
    gates_copy.wait()
    scales = [jnp.where(hit, 1.0, 0.0) for hit in token_hits]
    scales += [jnp.where(hit, gates_ref[k : k + 1, :], 0.0) for k, hit in enumerate(grad_hits)]
    scale = jnp.sum(sum(scales), axis=1, keepdims=True)
    gather = jnp.concatenate([either(token_hits), either(grad_hits)], axis=1)
    tokens_copy.wait()
    grad_copy.wait()
    out_ref[...] = (scale * f32_dot(gather, both_ref[...])).astype(jnp.bfloat16)


def paired_rows(number, capacity):
    owner = jnp.floor((number.astype(jnp.float32) + 0.5) * (1.0 / capacity)).astype(jnp.int32)
    return number + owner * ((PAIR - 1) * capacity)


def group_size(peers, capacity):
    size = 1
    while peers % (2 * size) == 0 and size * PAIR * capacity < 192:
        size *= 2
    return size


def take_apart(landed_ref, capacity, rows_ref, grads_ref):
    size = group_size(landed_ref.shape[0] // (PAIR * capacity), capacity)
    slots, rows = size * capacity, size * PAIR * capacity
    at = lax.broadcasted_iota(jnp.int32, (slots, rows), 1)
    source = paired_rows(lax.broadcasted_iota(jnp.int32, (slots, 1), 0), capacity)
    mover = jnp.concatenate([(at == source + j * capacity).astype(jnp.bfloat16) for j in range(PAIR)], axis=0)
    for i in range(rows_ref.shape[0] // slots):
        taken = f32_dot(mover, landed_ref[i * rows : (i + 1) * rows, :]).astype(jnp.bfloat16)
        rows_ref[i * slots : (i + 1) * slots, :] = taken[:slots]
        grads_ref[i * slots : (i + 1) * slots, :] = taken[slots:]


def fold_rows(plain_ref, capacity, folded_ref, out_ref, sems):
    size = group_size(plain_ref.shape[0] // capacity, capacity)
    slots, rows = size * capacity, size * PAIR * capacity
    width = folded_ref.shape[1]
    at = lax.broadcasted_iota(jnp.int32, (rows, slots), 0)
    target = paired_rows(lax.broadcasted_iota(jnp.int32, (1, slots), 1), capacity)
    mover = jnp.concatenate([(at == target + j * capacity).astype(jnp.bfloat16) for j in range(PAIR)], axis=1)
    copies = []
    for i in range(plain_ref.shape[0] // slots):
        plain = plain_ref[i * slots : (i + 1) * slots, :].astype(jnp.bfloat16)
        halves = jnp.concatenate([plain[:, j * width : (j + 1) * width] for j in range(PAIR)], axis=0)
        part = slice(i * rows, (i + 1) * rows)
        folded_ref[part, :] = f32_dot(mover, halves).astype(jnp.bfloat16)
        copies.append(pltpu.make_async_copy(folded_ref.at[part], out_ref.at[part], sems.at[i]))
        copies[-1].start()
    return copies


def unit_tiles(units):
    if units % (4 * TILE):
        return [(0, units)]
    sizes = [units // 4, units * 3 // 8, units * 3 // 8]
    return [(sum(sizes[:i]), size) for i, size in enumerate(sizes)]


def expert_kernel(capacity, landed_ref, up_ref, down_ref, hidden_out, grads_out, back_out, *scratch):
    up, down, rows, grads, hidden, masked, total, back, weight_sems, hidden_sems, grads_sem, back_sems = scratch
    tiles = unit_tiles(up.shape[1])
    features = up.shape[0]

    def weight_copies(m):
        start, size = tiles[m // 2]
        copies = []
        for n in range(PIECES):
            if m % 2 == 0:
                source, target = up_ref, up
                part = pl.ds(n * (features // PIECES), features // PIECES), pl.ds(start, size)
            else:
                source, target = down_ref, down
                part = pl.ds(start + n * (size // PIECES), size // PIECES)
            copies.append(pltpu.make_async_copy(source.at[part], target.at[part], weight_sems.at[m, n]))
        return copies

    def start_weights(m):
        if m < 2 * len(tiles):
            arriving[m] = weight_copies(m)
            for copy in arriving[m]:
                copy.start()

    def wait_weights(m):
        for copy in arriving[m]:
            copy.wait()
        start_weights(m + 2)

    def add_row_grad(i):
        start, size = tiles[i]
        part = f32_dot(masked[i % 2, :, :size], up[:, start : start + size], ((1,), (1,)))
        total[...] = part if i == 0 else total[...] + part

    arriving, leaving = {}, []
    start_weights(0)
    take_apart(landed_ref, capacity, rows, grads)
    leaving.append(pltpu.make_async_copy(grads, grads_out, grads_sem.at[0]))
    leaving[-1].start()
    start_weights(1)
    for i, (start, size) in enumerate(tiles):
        here = slice(start, start + size)
        wait_weights(2 * i)
        preact = f32_dot(rows[...], up[:, here])
        wait_weights(2 * i + 1)
        hidden_grad = f32_dot(grads[...], down[here, :], ((1,), (1,)))
        if i:
            add_row_grad(i - 1)
        hidden[:, here] = jnp.maximum(preact, 0.0).astype(jnp.bfloat16)
        masked[i % 2, :, :size] = jnp.where(preact > 0, hidden_grad, 0.0).astype(jnp.bfloat16)
        leaving.append(pltpu.make_async_copy(hidden.at[:, here], hidden_out.at[:, here], hidden_sems.at[i]))
        leaving[-1].start()
    add_row_grad(len(tiles) - 1)
    for copy in leaving + fold_rows(total, capacity, back, back_out, back_sems):
        copy.wait()


def down_grad_kernel(grads_ref, hidden_ref, out_ref):
    out_ref[...] = f32_dot(hidden_ref[...], grads_ref[...], ((0,), (0,))).astype(jnp.bfloat16)


def pick_map_kernel(capacity, ids_ref, after_ref, out_ref):
    tok_rows, rows = ids_ref.shape[1], out_ref.shape[1]
    places = row_places(ids_ref[...], rows // (PAIR * capacity), capacity)
    for j in range(PAIR):
        chosen = either(hits_at(rows, [place + j * capacity for place in places]))
        out_ref[j * tok_rows : (j + 1) * tok_rows, :] = chosen.T


def pick_kernel(map_ref, returned_ref, out_ref):
    tok_rows, width = out_ref.shape[0], returned_ref.shape[1]
    picked = f32_dot(map_ref[...], returned_ref[...]).astype(jnp.bfloat16)
    for j in range(PAIR):
        out_ref[:, j * width : (j + 1) * width] = picked[j * tok_rows : (j + 1) * tok_rows]


def exchange(rows):
    axes = ("row", "col")
    peers = lax.axis_size(axes)
    cut = rows.reshape(peers, rows.shape[0] // peers, rows.shape[1])
    return lax.all_to_all(cut, axes, split_axis=0, concat_axis=0, tiled=True).reshape(rows.shape)


def in_hbm(array):
    return pltpu.with_memory_space_constraint(array, pltpu.HBM)


def held(rows, columns, kind=jnp.bfloat16):
    return pltpu.VMEM((rows, columns), kind)


def shards(tokens, out_grad, expert_ids, gates, up_weight, down_weight):
    tok_rows, features = tokens.shape
    top_count = expert_ids.shape[1]
    units = up_weight.shape[2]
    peers = lax.axis_size(("row", "col"))
    capacity = 3 * tok_rows * top_count // (2 * peers)
    slots, rows, width = peers * capacity, peers * PAIR * capacity, features // PAIR
    tile = min(units, TILE // 2)
    steps = units // tile
    bf16, f32 = jnp.bfloat16, jnp.float32
    shape = jax.ShapeDtypeStruct
    dma = pltpu.SemaphoreType.DMA
    flops = 2 * slots * features * units
    weight_bytes = 2 * features * units

    def cost(matmuls, weights):
        return pl.CostEstimate(flops=matmuls * flops, bytes_accessed=weights * weight_bytes, transcendentals=0)

    ids = expert_ids.T
    hbm = pl.BlockSpec(memory_space=pltpu.HBM)
    vmem = pl.BlockSpec(memory_space=pltpu.VMEM)
    anywhere = pl.BlockSpec(memory_space=pl.ANY)
    tiles = unit_tiles(units)

    sent = pl.pallas_call(
        functools.partial(dispatch_kernel, capacity),
        out_shape=shape((rows, features), bf16),
        in_specs=[hbm, hbm, hbm, hbm],
        scratch_shapes=[
            held(top_count, tok_rows, jnp.int32),
            held(top_count, tok_rows, f32),
            held(2 * tok_rows, features),
            dma((4,)),
        ],
        compiler_params=params(),
        name="dispatch",
    )(*[in_hbm(array) for array in (ids, gates.T, tokens, out_grad)])
    landed = exchange(sent)

    hidden, grads, back = pl.pallas_call(
        functools.partial(expert_kernel, capacity),
        out_shape=(
            pltpu.HBM((slots, units), bf16),
            pltpu.HBM((slots, features), bf16),
            pltpu.HBM((rows, width), bf16),
        ),
        in_specs=[vmem, hbm, hbm],
        out_specs=(hbm, hbm, hbm),
        scratch_shapes=[
            held(features, units),
            held(units, features),
            held(slots, features),
            held(slots, features),
            held(slots, units),
            pltpu.VMEM((2, slots, tiles[-1][1]), bf16),
            held(slots, features, f32),
            held(rows, width),
            dma((2 * len(tiles), PIECES)),
            dma((len(tiles),)),
            dma((1,)),
            dma((peers // group_size(peers, capacity),)),
        ],
        compiler_params=params(),
        cost_estimate=cost(3, 2),
        name="expert",
    )(landed, in_hbm(up_weight[0]), in_hbm(down_weight[0]))
    returned = exchange(back)

    down_grad = pl.pallas_call(
        down_grad_kernel,
        out_shape=shape((1, units, features), bf16),
        grid=(steps,),
        in_specs=[pl.BlockSpec((slots, features), lambda i: (0, 0)), pl.BlockSpec((slots, tile), lambda i: (0, i))],
        out_specs=pl.BlockSpec((None, tile, features), lambda i: (0, i, 0)),
        compiler_params=params(),
        cost_estimate=cost(1, 1),
        name="down_grad",
    )(in_hbm(grads), in_hbm(hidden))

    pick_map = pl.pallas_call(
        functools.partial(pick_map_kernel, capacity),
        out_shape=shape((PAIR * tok_rows, rows), bf16),
        in_specs=[vmem, anywhere],
        compiler_params=params(),
        name="pick_map",
    )(ids, in_hbm(grads))
    input_grad = pl.pallas_call(
        pick_kernel,
        out_shape=shape((tok_rows, features), bf16),
        compiler_params=params(),
        name="pick",
    )(pick_map, returned)
    return input_grad, down_grad


def pooled_shards(tokens, out_grad, expert_ids, gates, up_weight, down_weight):
    tok_rows = tokens.shape[0]
    top_count = expert_ids.shape[1]
    features = tokens.shape[1]
    groups = lax.axis_size("row")
    col_count = lax.axis_size("col")
    experts = groups * col_count
    capacity = 3 * tok_rows * top_count // (2 * experts)
    flat_ids = expert_ids.reshape(-1)
    onehot = (flat_ids[:, None] == jnp.arange(experts, dtype=jnp.int32)[None, :]).astype(jnp.int32)
    earlier = jnp.cumsum(onehot, axis=0) - onehot
    slot_index = jnp.sum(earlier * onehot, axis=1)
    target = flat_ids * capacity + slot_index
    placer = (jnp.arange(experts * capacity, dtype=jnp.int32)[:, None] == target[None, :]).astype(
        jnp.bfloat16
    )
    token_rows = jnp.repeat(tokens, top_count, axis=0)
    weighted = (
        gates.reshape(-1)[:, None] * jnp.repeat(out_grad, top_count, axis=0).astype(jnp.float32)
    ).astype(jnp.bfloat16)
    send_inputs = jnp.dot(placer, token_rows, preferred_element_type=jnp.float32).astype(
        jnp.bfloat16
    )
    send_grads = jnp.dot(placer, weighted, preferred_element_type=jnp.float32).astype(jnp.bfloat16)
    landed_inputs, landed_grads = (
        lax.all_to_all(
            send_inputs.reshape(experts, capacity, features),
            ("row", "col"),
            split_axis=0,
            concat_axis=0,
            tiled=True,
        ),
        lax.all_to_all(
            send_grads.reshape(experts, capacity, features),
            ("row", "col"),
            split_axis=0,
            concat_axis=0,
            tiled=True,
        ),
    )
    pooled_inputs, pooled_grads = (
        lax.all_gather(landed_inputs, "rep", axis=0, tiled=True),
        lax.all_gather(landed_grads, "rep", axis=0, tiled=True),
    )
    slot_rows = pooled_inputs.shape[0] * capacity
    input_rows = pooled_inputs.reshape(slot_rows, features)
    grad_rows = pooled_grads.reshape(slot_rows, features)
    up_block = up_weight[0]
    down_block = down_weight[0]
    preact = jnp.dot(input_rows, up_block, preferred_element_type=jnp.float32)
    hidden = jnp.maximum(preact, 0.0).astype(jnp.bfloat16)
    hidden_grad = lax.dot_general(
        grad_rows, down_block, (((1,), (1,)), ((), ())), preferred_element_type=jnp.float32
    )
    preact_grad = jnp.where(preact > 0, hidden_grad, 0.0).astype(jnp.bfloat16)
    weight_grad = lax.dot_general(
        hidden, grad_rows, (((0,), (0,)), ((), ())), preferred_element_type=jnp.float32
    )
    down_grad = weight_grad.astype(jnp.bfloat16)[None]
    summed_rows = lax.psum_scatter(
        lax.dot_general(
            preact_grad, up_block, (((1,), (1,)), ((), ())), preferred_element_type=jnp.float32
        ).astype(jnp.bfloat16),
        "rep",
        scatter_dimension=0,
        tiled=True,
    )
    returned = lax.all_to_all(
        summed_rows.reshape(experts, capacity, features),
        ("row", "col"),
        split_axis=0,
        concat_axis=0,
        tiled=True,
    )
    returned = returned.reshape(experts * capacity, features)
    picked = lax.dot_general(
        placer, returned, (((0,), (0,)), ((), ())), preferred_element_type=jnp.float32
    )
    input_grad = jnp.sum(picked.reshape(tok_rows, top_count, features), axis=1).astype(jnp.bfloat16)
    return (input_grad, down_grad)


def solution(mesh):
    by_token = P(("rep", "row", "col"), None)
    by_expert = (P(("row", "col"), None, "rep"), P(("row", "col"), "rep", None))
    return jax.shard_map(
        shards if mesh.shape["rep"] == 1 else pooled_shards,
        mesh=mesh,
        in_specs=(by_token,) * 4 + by_expert,
        out_specs=(by_token, by_expert[1]),
        check_vma=False,
    )
```

```python
import functools

import jax
import jax.numpy as jnp
from jax import lax
from jax.experimental import pallas as pl
from jax.experimental.pallas import tpu as pltpu
from jax.sharding import PartitionSpec as P

VMEM_LIMIT = 48 * 1024 * 1024
PAIR = 2
TILE = 1024
AHEAD = 2
NOWHERE = -(1 << 20)


def f32_dot(lhs, rhs, contract=((1,), (0,))):
    return lax.dot_general(lhs, rhs, (contract, ((), ())), preferred_element_type=jnp.float32)


def params():
    return pltpu.CompilerParams(vmem_limit_bytes=VMEM_LIMIT)


def row_places(ids, experts, capacity):
    tok_rows = ids.shape[1]
    names = lax.broadcasted_iota(jnp.int32, (experts, tok_rows), 0)
    chosen = [names == ids[k : k + 1, :] for k in range(ids.shape[0])]
    member = functools.reduce(jnp.logical_or, chosen).astype(jnp.bfloat16)
    before = (
        lax.broadcasted_iota(jnp.int32, (tok_rows, tok_rows), 0)
        < lax.broadcasted_iota(jnp.int32, (tok_rows, tok_rows), 1)
    ).astype(jnp.bfloat16)
    rank = f32_dot(member, before).astype(jnp.int32)
    place = names * (PAIR * capacity) + rank
    return [jnp.sum(jnp.where(pick, place, 0), axis=0, keepdims=True) for pick in chosen]


def hits_at(rows, places):
    at = lax.broadcasted_iota(jnp.int32, (rows, places[0].shape[1]), 0)
    return [at == place for place in places]


def either(hits):
    return functools.reduce(jnp.logical_or, hits).astype(jnp.bfloat16)


def started(pairs, sems):
    copies = [pltpu.make_async_copy(*pair, sems.at[i]) for i, pair in enumerate(pairs)]
    for copy in copies:
        copy.start()
    return copies


def dispatch_kernel(capacity, *refs):
    sources, (out_ref, ids_ref, gates_ref, both_ref, sems) = refs[:4], refs[4:]
    tok_rows = both_ref.shape[0] // 2
    targets = ids_ref, gates_ref, both_ref.at[pl.ds(0, tok_rows)], both_ref.at[pl.ds(tok_rows, tok_rows)]
    ids_copy, gates_copy, tokens_copy, grad_copy = started(zip(sources, targets), sems)
    rows = out_ref.shape[0]
    ids_copy.wait()
    places = row_places(ids_ref[...], rows // (PAIR * capacity), capacity)
    token_hits = hits_at(rows, places)
    grad_hits = hits_at(rows, [place + capacity for place in places])
    gates_copy.wait()
    scales = [jnp.where(hit, 1.0, 0.0) for hit in token_hits]
    scales += [jnp.where(hit, gates_ref[k : k + 1, :], 0.0) for k, hit in enumerate(grad_hits)]
    scale = jnp.sum(sum(scales), axis=1, keepdims=True)
    gather = jnp.concatenate([either(token_hits), either(grad_hits)], axis=1)
    tokens_copy.wait()
    grad_copy.wait()
    out_ref[...] = (scale * f32_dot(gather, both_ref[...])).astype(jnp.bfloat16)


def paired_rows(number, capacity):
    owner = jnp.floor((number.astype(jnp.float32) + 0.5) * (1.0 / capacity)).astype(jnp.int32)
    return number + owner * ((PAIR - 1) * capacity)


def group_size(peers, capacity):
    size = 1
    while peers % (2 * size) == 0 and size * PAIR * capacity < 192:
        size *= 2
    return size


def take_apart(landed_ref, capacity, rows_ref, grads_ref):
    size = group_size(landed_ref.shape[0] // (PAIR * capacity), capacity)
    slots, rows = size * capacity, size * PAIR * capacity
    at = lax.broadcasted_iota(jnp.int32, (slots, rows), 1)
    source = paired_rows(lax.broadcasted_iota(jnp.int32, (slots, 1), 0), capacity)
    mover = jnp.concatenate([(at == source + j * capacity).astype(jnp.bfloat16) for j in range(PAIR)], axis=0)
    for i in range(rows_ref.shape[0] // slots):
        taken = f32_dot(mover, landed_ref[i * rows : (i + 1) * rows, :]).astype(jnp.bfloat16)
        rows_ref[i * slots : (i + 1) * slots, :] = taken[:slots]
        grads_ref[i * slots : (i + 1) * slots, :] = taken[slots:]


def fold_rows(plain_ref, capacity, folded_ref, out_ref, sems):
    size = group_size(plain_ref.shape[0] // capacity, capacity)
    slots, rows = size * capacity, size * PAIR * capacity
    width = folded_ref.shape[1]
    at = lax.broadcasted_iota(jnp.int32, (rows, slots), 0)
    target = paired_rows(lax.broadcasted_iota(jnp.int32, (1, slots), 1), capacity)
    mover = jnp.concatenate([(at == target + j * capacity).astype(jnp.bfloat16) for j in range(PAIR)], axis=1)
    copies = []
    for i in range(plain_ref.shape[0] // slots):
        plain = plain_ref[i * slots : (i + 1) * slots, :].astype(jnp.bfloat16)
        halves = jnp.concatenate([plain[:, j * width : (j + 1) * width] for j in range(PAIR)], axis=0)
        part = slice(i * rows, (i + 1) * rows)
        folded_ref[part, :] = f32_dot(mover, halves).astype(jnp.bfloat16)
        copies.append(pltpu.make_async_copy(folded_ref.at[part], out_ref.at[part], sems.at[i]))
        copies[-1].start()
    return copies


def unit_tiles(units):
    size = min(units, TILE)
    return [(start, size) for start in range(0, units, size)]


def expert_kernel(capacity, landed_ref, up_ref, down_ref, hidden_out, grads_out, back_out, *scratch):
    up, down, rows, grads, hidden, masked, total, back, weight_sems, hidden_sems, grads_sem, back_sems = scratch
    tiles = unit_tiles(up.shape[1])

    def weight_copies(i):
        at = pl.ds(*tiles[i])
        return [
            pltpu.make_async_copy(up_ref.at[:, at], up.at[:, at], weight_sems.at[0, i]),
            pltpu.make_async_copy(down_ref.at[at], down.at[at], weight_sems.at[1, i]),
        ]

    def start_weights(i):
        if i < len(tiles):
            arriving[i] = weight_copies(i)
            for copy in arriving[i]:
                copy.start()

    def add_row_grad(i):
        start, size = tiles[i]
        part = f32_dot(masked[i % 2, :, :size], up[:, start : start + size], ((1,), (1,)))
        total[...] = part if i == 0 else total[...] + part

    arriving, leaving = {}, []
    for i in range(AHEAD):
        start_weights(i)
    take_apart(landed_ref, capacity, rows, grads)
    leaving.append(pltpu.make_async_copy(grads, grads_out, grads_sem.at[0]))
    leaving[-1].start()
    for i, (start, size) in enumerate(tiles):
        here = slice(start, start + size)
        start_weights(i + AHEAD)
        for copy in arriving[i]:
            copy.wait()
        preact = f32_dot(rows[...], up[:, here])
        hidden_grad = f32_dot(grads[...], down[here, :], ((1,), (1,)))
        if i:
            add_row_grad(i - 1)
        hidden[:, here] = jnp.maximum(preact, 0.0).astype(jnp.bfloat16)
        masked[i % 2, :, :size] = jnp.where(preact > 0, hidden_grad, 0.0).astype(jnp.bfloat16)
        leaving.append(pltpu.make_async_copy(hidden.at[:, here], hidden_out.at[:, here], hidden_sems.at[i]))
        leaving[-1].start()
    add_row_grad(len(tiles) - 1)
    for copy in leaving + fold_rows(total, capacity, back, back_out, back_sems):
        copy.wait()


def down_grad_kernel(grads_ref, hidden_ref, out_ref):
    out_ref[...] = f32_dot(hidden_ref[...], grads_ref[...], ((0,), (0,))).astype(jnp.bfloat16)


def pick_map_kernel(capacity, ids_ref, after_ref, out_ref):
    tok_rows, rows = ids_ref.shape[1], out_ref.shape[1]
    places = row_places(ids_ref[...], rows // (PAIR * capacity), capacity)
    for j in range(PAIR):
        chosen = either(hits_at(rows, [place + j * capacity for place in places]))
        out_ref[j * tok_rows : (j + 1) * tok_rows, :] = chosen.T


def pick_kernel(map_ref, returned_ref, out_ref):
    tok_rows, width = out_ref.shape[0], returned_ref.shape[1]
    picked = f32_dot(map_ref[...], returned_ref[...]).astype(jnp.bfloat16)
    for j in range(PAIR):
        out_ref[:, j * width : (j + 1) * width] = picked[j * tok_rows : (j + 1) * tok_rows]


def exchange(rows):
    axes = ("row", "col")
    peers = lax.axis_size(axes)
    cut = rows.reshape(peers, rows.shape[0] // peers, rows.shape[1])
    return lax.all_to_all(cut, axes, split_axis=0, concat_axis=0, tiled=True).reshape(rows.shape)


def in_hbm(array):
    return pltpu.with_memory_space_constraint(array, pltpu.HBM)


def held(rows, columns, kind=jnp.bfloat16):
    return pltpu.VMEM((rows, columns), kind)


def shards(tokens, out_grad, expert_ids, gates, up_weight, down_weight):
    tok_rows, features = tokens.shape
    top_count = expert_ids.shape[1]
    units = up_weight.shape[2]
    peers = lax.axis_size(("row", "col"))
    capacity = 3 * tok_rows * top_count // (2 * peers)
    slots, rows, width = peers * capacity, peers * PAIR * capacity, features // PAIR
    tile = min(units, TILE // 2)
    steps = units // tile
    bf16, f32 = jnp.bfloat16, jnp.float32
    shape = jax.ShapeDtypeStruct
    dma = pltpu.SemaphoreType.DMA
    flops = 2 * slots * features * units
    weight_bytes = 2 * features * units

    def cost(matmuls, weights):
        return pl.CostEstimate(flops=matmuls * flops, bytes_accessed=weights * weight_bytes, transcendentals=0)

    ids = expert_ids.T
    hbm = pl.BlockSpec(memory_space=pltpu.HBM)
    vmem = pl.BlockSpec(memory_space=pltpu.VMEM)
    anywhere = pl.BlockSpec(memory_space=pl.ANY)
    tiles = unit_tiles(units)

    sent = pl.pallas_call(
        functools.partial(dispatch_kernel, capacity),
        out_shape=shape((rows, features), bf16),
        in_specs=[hbm, hbm, hbm, hbm],
        scratch_shapes=[
            held(top_count, tok_rows, jnp.int32),
            held(top_count, tok_rows, f32),
            held(2 * tok_rows, features),
            dma((4,)),
        ],
        compiler_params=params(),
        name="dispatch",
    )(*[in_hbm(array) for array in (ids, gates.T, tokens, out_grad)])
    landed = exchange(sent)

    hidden, grads, back = pl.pallas_call(
        functools.partial(expert_kernel, capacity),
        out_shape=(
            pltpu.HBM((slots, units), bf16),
            pltpu.HBM((slots, features), bf16),
            pltpu.HBM((rows, width), bf16),
        ),
        in_specs=[vmem, hbm, hbm],
        out_specs=(hbm, hbm, hbm),
        scratch_shapes=[
            held(features, units),
            held(units, features),
            held(slots, features),
            held(slots, features),
            held(slots, units),
            pltpu.VMEM((2, slots, tiles[0][1]), bf16),
            held(slots, features, f32),
            held(rows, width),
            dma((2, len(tiles))),
            dma((len(tiles),)),
            dma((1,)),
            dma((peers // group_size(peers, capacity),)),
        ],
        compiler_params=params(),
        cost_estimate=cost(3, 2),
        name="expert",
    )(landed, in_hbm(up_weight[0]), in_hbm(down_weight[0]))
    returned = exchange(back)

    down_grad = pl.pallas_call(
        down_grad_kernel,
        out_shape=shape((1, units, features), bf16),
        grid=(steps,),
        in_specs=[pl.BlockSpec((slots, features), lambda i: (0, 0)), pl.BlockSpec((slots, tile), lambda i: (0, i))],
        out_specs=pl.BlockSpec((None, tile, features), lambda i: (0, i, 0)),
        compiler_params=params(),
        cost_estimate=cost(1, 1),
        name="down_grad",
    )(in_hbm(grads), in_hbm(hidden))

    pick_map = pl.pallas_call(
        functools.partial(pick_map_kernel, capacity),
        out_shape=shape((PAIR * tok_rows, rows), bf16),
        in_specs=[vmem, anywhere],
        compiler_params=params(),
        name="pick_map",
    )(ids, in_hbm(grads))
    input_grad = pl.pallas_call(
        pick_kernel,
        out_shape=shape((tok_rows, features), bf16),
        compiler_params=params(),
        name="pick",
    )(pick_map, returned)
    return input_grad, down_grad


def pooled_shards(tokens, out_grad, expert_ids, gates, up_weight, down_weight):
    tok_rows = tokens.shape[0]
    top_count = expert_ids.shape[1]
    features = tokens.shape[1]
    groups = lax.axis_size("row")
    col_count = lax.axis_size("col")
    experts = groups * col_count
    capacity = 3 * tok_rows * top_count // (2 * experts)
    flat_ids = expert_ids.reshape(-1)
    onehot = (flat_ids[:, None] == jnp.arange(experts, dtype=jnp.int32)[None, :]).astype(jnp.int32)
    earlier = jnp.cumsum(onehot, axis=0) - onehot
    slot_index = jnp.sum(earlier * onehot, axis=1)
    target = flat_ids * capacity + slot_index
    placer = (jnp.arange(experts * capacity, dtype=jnp.int32)[:, None] == target[None, :]).astype(
        jnp.bfloat16
    )
    token_rows = jnp.repeat(tokens, top_count, axis=0)
    weighted = (
        gates.reshape(-1)[:, None] * jnp.repeat(out_grad, top_count, axis=0).astype(jnp.float32)
    ).astype(jnp.bfloat16)
    send_inputs = jnp.dot(placer, token_rows, preferred_element_type=jnp.float32).astype(
        jnp.bfloat16
    )
    send_grads = jnp.dot(placer, weighted, preferred_element_type=jnp.float32).astype(jnp.bfloat16)
    landed_inputs, landed_grads = (
        lax.all_to_all(
            send_inputs.reshape(experts, capacity, features),
            ("row", "col"),
            split_axis=0,
            concat_axis=0,
            tiled=True,
        ),
        lax.all_to_all(
            send_grads.reshape(experts, capacity, features),
            ("row", "col"),
            split_axis=0,
            concat_axis=0,
            tiled=True,
        ),
    )
    pooled_inputs, pooled_grads = (
        lax.all_gather(landed_inputs, "rep", axis=0, tiled=True),
        lax.all_gather(landed_grads, "rep", axis=0, tiled=True),
    )
    slot_rows = pooled_inputs.shape[0] * capacity
    input_rows = pooled_inputs.reshape(slot_rows, features)
    grad_rows = pooled_grads.reshape(slot_rows, features)
    up_block = up_weight[0]
    down_block = down_weight[0]
    preact = jnp.dot(input_rows, up_block, preferred_element_type=jnp.float32)
    hidden = jnp.maximum(preact, 0.0).astype(jnp.bfloat16)
    hidden_grad = lax.dot_general(
        grad_rows, down_block, (((1,), (1,)), ((), ())), preferred_element_type=jnp.float32
    )
    preact_grad = jnp.where(preact > 0, hidden_grad, 0.0).astype(jnp.bfloat16)
    weight_grad = lax.dot_general(
        hidden, grad_rows, (((0,), (0,)), ((), ())), preferred_element_type=jnp.float32
    )
    down_grad = weight_grad.astype(jnp.bfloat16)[None]
    summed_rows = lax.psum_scatter(
        lax.dot_general(
            preact_grad, up_block, (((1,), (1,)), ((), ())), preferred_element_type=jnp.float32
        ).astype(jnp.bfloat16),
        "rep",
        scatter_dimension=0,
        tiled=True,
    )
    returned = lax.all_to_all(
        summed_rows.reshape(experts, capacity, features),
        ("row", "col"),
        split_axis=0,
        concat_axis=0,
        tiled=True,
    )
    returned = returned.reshape(experts * capacity, features)
    picked = lax.dot_general(
        placer, returned, (((0,), (0,)), ((), ())), preferred_element_type=jnp.float32
    )
    input_grad = jnp.sum(picked.reshape(tok_rows, top_count, features), axis=1).astype(jnp.bfloat16)
    return (input_grad, down_grad)


def solution(mesh):
    by_token = P(("rep", "row", "col"), None)
    by_expert = (P(("row", "col"), None, "rep"), P(("row", "col"), "rep", None))
    return jax.shard_map(
        shards if mesh.shape["rep"] == 1 else pooled_shards,
        mesh=mesh,
        in_specs=(by_token,) * 4 + by_expert,
        out_specs=(by_token, by_expert[1]),
        check_vma=False,
    )
```

```python
import functools

import jax
import jax.numpy as jnp
from jax import lax
from jax.experimental import pallas as pl
from jax.experimental.pallas import tpu as pltpu
from jax.sharding import PartitionSpec as P

VMEM_LIMIT = 48 * 1024 * 1024
PAIR = 2
TILE = 1024
AHEAD = 2
NOWHERE = -(1 << 20)


def f32_dot(lhs, rhs, contract=((1,), (0,))):
    return lax.dot_general(lhs, rhs, (contract, ((), ())), preferred_element_type=jnp.float32)


def params():
    return pltpu.CompilerParams(vmem_limit_bytes=VMEM_LIMIT)


def row_places(ids, experts, capacity):
    tok_rows = ids.shape[1]
    names = lax.broadcasted_iota(jnp.int32, (experts, tok_rows), 0)
    chosen = [names == ids[k : k + 1, :] for k in range(ids.shape[0])]
    member = functools.reduce(jnp.logical_or, chosen).astype(jnp.bfloat16)
    before = (
        lax.broadcasted_iota(jnp.int32, (tok_rows, tok_rows), 0)
        < lax.broadcasted_iota(jnp.int32, (tok_rows, tok_rows), 1)
    ).astype(jnp.bfloat16)
    rank = f32_dot(member, before).astype(jnp.int32)
    place = names * (PAIR * capacity) + rank
    return [jnp.sum(jnp.where(pick, place, 0), axis=0, keepdims=True) for pick in chosen]


def hits_at(rows, places):
    at = lax.broadcasted_iota(jnp.int32, (rows, places[0].shape[1]), 0)
    return [at == place for place in places]


def either(hits):
    return functools.reduce(jnp.logical_or, hits).astype(jnp.bfloat16)


def started(pairs, sems):
    copies = [pltpu.make_async_copy(*pair, sems.at[i]) for i, pair in enumerate(pairs)]
    for copy in copies:
        copy.start()
    return copies


def dispatch_kernel(capacity, *refs):
    sources, (out_ref, ids_ref, gates_ref, both_ref, sems) = refs[:4], refs[4:]
    tok_rows = both_ref.shape[0] // 2
    targets = ids_ref, gates_ref, both_ref.at[pl.ds(0, tok_rows)], both_ref.at[pl.ds(tok_rows, tok_rows)]
    ids_copy, gates_copy, tokens_copy, grad_copy = started(zip(sources, targets), sems)
    rows = out_ref.shape[0]
    ids_copy.wait()
    places = row_places(ids_ref[...], rows // (PAIR * capacity), capacity)
    token_hits = hits_at(rows, places)
    grad_hits = hits_at(rows, [place + capacity for place in places])
    gates_copy.wait()
    scales = [jnp.where(hit, 1.0, 0.0) for hit in token_hits]
    scales += [jnp.where(hit, gates_ref[k : k + 1, :], 0.0) for k, hit in enumerate(grad_hits)]
    scale = jnp.sum(sum(scales), axis=1, keepdims=True)
    gather = jnp.concatenate([either(token_hits), either(grad_hits)], axis=1)
    tokens_copy.wait()
    grad_copy.wait()
    out_ref[...] = (scale * f32_dot(gather, both_ref[...])).astype(jnp.bfloat16)


def paired_rows(number, capacity):
    owner = jnp.floor((number.astype(jnp.float32) + 0.5) * (1.0 / capacity)).astype(jnp.int32)
    return number + owner * ((PAIR - 1) * capacity)


def group_size(peers, capacity):
    size = 1
    while peers % (2 * size) == 0 and size * PAIR * capacity < 192:
        size *= 2
    return size


def take_apart(landed_ref, capacity, rows_ref, grads_ref):
    size = group_size(landed_ref.shape[0] // (PAIR * capacity), capacity)
    slots, rows = size * capacity, size * PAIR * capacity
    at = lax.broadcasted_iota(jnp.int32, (slots, rows), 1)
    source = paired_rows(lax.broadcasted_iota(jnp.int32, (slots, 1), 0), capacity)
    mover = jnp.concatenate([(at == source + j * capacity).astype(jnp.bfloat16) for j in range(PAIR)], axis=0)
    for i in range(rows_ref.shape[0] // slots):
        taken = f32_dot(mover, landed_ref[i * rows : (i + 1) * rows, :]).astype(jnp.bfloat16)
        rows_ref[i * slots : (i + 1) * slots, :] = taken[:slots]
        grads_ref[i * slots : (i + 1) * slots, :] = taken[slots:]


def fold_rows(plain_ref, capacity, folded_ref, out_ref, sems):
    size = group_size(plain_ref.shape[0] // capacity, capacity)
    slots, rows = size * capacity, size * PAIR * capacity
    width = folded_ref.shape[1]
    at = lax.broadcasted_iota(jnp.int32, (rows, slots), 0)
    target = paired_rows(lax.broadcasted_iota(jnp.int32, (1, slots), 1), capacity)
    mover = jnp.concatenate([(at == target + j * capacity).astype(jnp.bfloat16) for j in range(PAIR)], axis=1)
    copies = []
    for i in range(plain_ref.shape[0] // slots):
        plain = plain_ref[i * slots : (i + 1) * slots, :].astype(jnp.bfloat16)
        halves = jnp.concatenate([plain[:, j * width : (j + 1) * width] for j in range(PAIR)], axis=0)
        part = slice(i * rows, (i + 1) * rows)
        folded_ref[part, :] = f32_dot(mover, halves).astype(jnp.bfloat16)
        copies.append(pltpu.make_async_copy(folded_ref.at[part], out_ref.at[part], sems.at[i]))
        copies[-1].start()
    return copies


def unit_tiles(units):
    size = min(units, TILE)
    return [(start, size) for start in range(0, units, size)]


def expert_kernel(capacity, landed_ref, up_ref, down_ref, hidden_out, grads_out, back_out, *scratch):
    up, down, rows, grads, hidden, masked, total, back, weight_sems, hidden_sems, grads_sem, back_sems = scratch
    tile = masked.shape[2]
    steps = up.shape[1] // tile

    def tile_at(i):
        return pl.ds(pl.multiple_of(i * tile, tile), tile)

    def up_copy(i):
        return pltpu.make_async_copy(up_ref.at[:, tile_at(i)], up.at[:, tile_at(i)], weight_sems.at[0, i])

    def down_copy(i):
        return pltpu.make_async_copy(down_ref.at[tile_at(i)], down.at[tile_at(i)], weight_sems.at[1, i])

    def start_weights(i):
        up_copy(i).start()
        down_copy(i).start()

    def hidden_copy(i):
        return pltpu.make_async_copy(hidden.at[:, tile_at(i)], hidden_out.at[:, tile_at(i)], hidden_sems.at[i])

    def row_grad(i):
        return f32_dot(masked[i % 2], up[:, tile_at(i)], ((1,), (1,)))

    def activate(i, preact, hidden_grad):
        hidden[:, tile_at(i)] = jnp.maximum(preact, 0.0).astype(jnp.bfloat16)
        masked[i % 2] = jnp.where(preact > 0, hidden_grad, 0.0).astype(jnp.bfloat16)
        hidden_copy(i).start()

    def products(i):
        up_copy(i).wait()
        down_copy(i).wait()
        preact = f32_dot(rows[...], up[:, tile_at(i)])
        return preact, f32_dot(grads[...], down[tile_at(i), :], ((1,), (1,)))

    for i in range(min(AHEAD, steps)):
        start_weights(i)
    take_apart(landed_ref, capacity, rows, grads)
    grads_copy = pltpu.make_async_copy(grads, grads_out, grads_sem.at[0])
    grads_copy.start()
    if AHEAD < steps:
        start_weights(AHEAD)
    total[...] = jnp.zeros_like(total)
    activate(0, *products(0))

    def step(i, carry):
        @pl.when(i + AHEAD < steps)
        def _():
            start_weights(i + AHEAD)

        preact, hidden_grad = products(i)
        total[...] += row_grad(i - 1)
        activate(i, preact, hidden_grad)
        return carry

    lax.fori_loop(1, steps, step, 0)
    total[...] += row_grad(steps - 1)
    leaving = fold_rows(total, capacity, back, back_out, back_sems)
    grads_copy.wait()
    for i in range(steps):
        hidden_copy(i).wait()
    for copy in leaving:
        copy.wait()


def down_grad_kernel(grads_ref, hidden_ref, out_ref):
    out_ref[...] = f32_dot(hidden_ref[...], grads_ref[...], ((0,), (0,))).astype(jnp.bfloat16)


def pick_map_kernel(capacity, ids_ref, after_ref, out_ref):
    tok_rows, rows = ids_ref.shape[1], out_ref.shape[1]
    places = row_places(ids_ref[...], rows // (PAIR * capacity), capacity)
    for j in range(PAIR):
        chosen = either(hits_at(rows, [place + j * capacity for place in places]))
        out_ref[j * tok_rows : (j + 1) * tok_rows, :] = chosen.T


def pick_kernel(map_ref, returned_ref, out_ref):
    tok_rows, width = out_ref.shape[0], returned_ref.shape[1]
    picked = f32_dot(map_ref[...], returned_ref[...]).astype(jnp.bfloat16)
    for j in range(PAIR):
        out_ref[:, j * width : (j + 1) * width] = picked[j * tok_rows : (j + 1) * tok_rows]


def exchange(rows):
    axes = ("row", "col")
    peers = lax.axis_size(axes)
    cut = rows.reshape(peers, rows.shape[0] // peers, rows.shape[1])
    return lax.all_to_all(cut, axes, split_axis=0, concat_axis=0, tiled=True).reshape(rows.shape)


def in_hbm(array):
    return pltpu.with_memory_space_constraint(array, pltpu.HBM)


def held(rows, columns, kind=jnp.bfloat16):
    return pltpu.VMEM((rows, columns), kind)


def shards(tokens, out_grad, expert_ids, gates, up_weight, down_weight):
    tok_rows, features = tokens.shape
    top_count = expert_ids.shape[1]
    units = up_weight.shape[2]
    peers = lax.axis_size(("row", "col"))
    capacity = 3 * tok_rows * top_count // (2 * peers)
    slots, rows, width = peers * capacity, peers * PAIR * capacity, features // PAIR
    tile = min(units, TILE // 2)
    steps = units // tile
    bf16, f32 = jnp.bfloat16, jnp.float32
    shape = jax.ShapeDtypeStruct
    dma = pltpu.SemaphoreType.DMA
    flops = 2 * slots * features * units
    weight_bytes = 2 * features * units

    def cost(matmuls, weights):
        return pl.CostEstimate(flops=matmuls * flops, bytes_accessed=weights * weight_bytes, transcendentals=0)

    ids = expert_ids.T
    hbm = pl.BlockSpec(memory_space=pltpu.HBM)
    vmem = pl.BlockSpec(memory_space=pltpu.VMEM)
    anywhere = pl.BlockSpec(memory_space=pl.ANY)
    tiles = unit_tiles(units)

    sent = pl.pallas_call(
        functools.partial(dispatch_kernel, capacity),
        out_shape=shape((rows, features), bf16),
        in_specs=[hbm, hbm, hbm, hbm],
        scratch_shapes=[
            held(top_count, tok_rows, jnp.int32),
            held(top_count, tok_rows, f32),
            held(2 * tok_rows, features),
            dma((4,)),
        ],
        compiler_params=params(),
        name="dispatch",
    )(*[in_hbm(array) for array in (ids, gates.T, tokens, out_grad)])
    landed = exchange(sent)

    hidden, grads, back = pl.pallas_call(
        functools.partial(expert_kernel, capacity),
        out_shape=(
            pltpu.HBM((slots, units), bf16),
            pltpu.HBM((slots, features), bf16),
            pltpu.HBM((rows, width), bf16),
        ),
        in_specs=[vmem, hbm, hbm],
        out_specs=(hbm, hbm, hbm),
        scratch_shapes=[
            held(features, units),
            held(units, features),
            held(slots, features),
            held(slots, features),
            held(slots, units),
            pltpu.VMEM((2, slots, tiles[0][1]), bf16),
            held(slots, features, f32),
            held(rows, width),
            dma((2, len(tiles))),
            dma((len(tiles),)),
            dma((1,)),
            dma((peers // group_size(peers, capacity),)),
        ],
        compiler_params=params(),
        cost_estimate=cost(3, 2),
        name="expert",
    )(landed, in_hbm(up_weight[0]), in_hbm(down_weight[0]))
    returned = exchange(back)

    down_grad = pl.pallas_call(
        down_grad_kernel,
        out_shape=shape((1, units, features), bf16),
        grid=(steps,),
        in_specs=[pl.BlockSpec((slots, features), lambda i: (0, 0)), pl.BlockSpec((slots, tile), lambda i: (0, i))],
        out_specs=pl.BlockSpec((None, tile, features), lambda i: (0, i, 0)),
        compiler_params=params(),
        cost_estimate=cost(1, 1),
        name="down_grad",
    )(in_hbm(grads), in_hbm(hidden))

    pick_map = pl.pallas_call(
        functools.partial(pick_map_kernel, capacity),
        out_shape=shape((PAIR * tok_rows, rows), bf16),
        in_specs=[vmem, anywhere],
        compiler_params=params(),
        name="pick_map",
    )(ids, in_hbm(grads))
    input_grad = pl.pallas_call(
        pick_kernel,
        out_shape=shape((tok_rows, features), bf16),
        compiler_params=params(),
        name="pick",
    )(pick_map, returned)
    return input_grad, down_grad


def pooled_shards(tokens, out_grad, expert_ids, gates, up_weight, down_weight):
    tok_rows = tokens.shape[0]
    top_count = expert_ids.shape[1]
    features = tokens.shape[1]
    groups = lax.axis_size("row")
    col_count = lax.axis_size("col")
    experts = groups * col_count
    capacity = 3 * tok_rows * top_count // (2 * experts)
    flat_ids = expert_ids.reshape(-1)
    onehot = (flat_ids[:, None] == jnp.arange(experts, dtype=jnp.int32)[None, :]).astype(jnp.int32)
    earlier = jnp.cumsum(onehot, axis=0) - onehot
    slot_index = jnp.sum(earlier * onehot, axis=1)
    target = flat_ids * capacity + slot_index
    placer = (jnp.arange(experts * capacity, dtype=jnp.int32)[:, None] == target[None, :]).astype(
        jnp.bfloat16
    )
    token_rows = jnp.repeat(tokens, top_count, axis=0)
    weighted = (
        gates.reshape(-1)[:, None] * jnp.repeat(out_grad, top_count, axis=0).astype(jnp.float32)
    ).astype(jnp.bfloat16)
    send_inputs = jnp.dot(placer, token_rows, preferred_element_type=jnp.float32).astype(
        jnp.bfloat16
    )
    send_grads = jnp.dot(placer, weighted, preferred_element_type=jnp.float32).astype(jnp.bfloat16)
    landed_inputs, landed_grads = (
        lax.all_to_all(
            send_inputs.reshape(experts, capacity, features),
            ("row", "col"),
            split_axis=0,
            concat_axis=0,
            tiled=True,
        ),
        lax.all_to_all(
            send_grads.reshape(experts, capacity, features),
            ("row", "col"),
            split_axis=0,
            concat_axis=0,
            tiled=True,
        ),
    )
    pooled_inputs, pooled_grads = (
        lax.all_gather(landed_inputs, "rep", axis=0, tiled=True),
        lax.all_gather(landed_grads, "rep", axis=0, tiled=True),
    )
    slot_rows = pooled_inputs.shape[0] * capacity
    input_rows = pooled_inputs.reshape(slot_rows, features)
    grad_rows = pooled_grads.reshape(slot_rows, features)
    up_block = up_weight[0]
    down_block = down_weight[0]
    preact = jnp.dot(input_rows, up_block, preferred_element_type=jnp.float32)
    hidden = jnp.maximum(preact, 0.0).astype(jnp.bfloat16)
    hidden_grad = lax.dot_general(
        grad_rows, down_block, (((1,), (1,)), ((), ())), preferred_element_type=jnp.float32
    )
    preact_grad = jnp.where(preact > 0, hidden_grad, 0.0).astype(jnp.bfloat16)
    weight_grad = lax.dot_general(
        hidden, grad_rows, (((0,), (0,)), ((), ())), preferred_element_type=jnp.float32
    )
    down_grad = weight_grad.astype(jnp.bfloat16)[None]
    summed_rows = lax.psum_scatter(
        lax.dot_general(
            preact_grad, up_block, (((1,), (1,)), ((), ())), preferred_element_type=jnp.float32
        ).astype(jnp.bfloat16),
        "rep",
        scatter_dimension=0,
        tiled=True,
    )
    returned = lax.all_to_all(
        summed_rows.reshape(experts, capacity, features),
        ("row", "col"),
        split_axis=0,
        concat_axis=0,
        tiled=True,
    )
    returned = returned.reshape(experts * capacity, features)
    picked = lax.dot_general(
        placer, returned, (((0,), (0,)), ((), ())), preferred_element_type=jnp.float32
    )
    input_grad = jnp.sum(picked.reshape(tok_rows, top_count, features), axis=1).astype(jnp.bfloat16)
    return (input_grad, down_grad)


def solution(mesh):
    by_token = P(("rep", "row", "col"), None)
    by_expert = (P(("row", "col"), None, "rep"), P(("row", "col"), "rep", None))
    return jax.shard_map(
        shards if mesh.shape["rep"] == 1 else pooled_shards,
        mesh=mesh,
        in_specs=(by_token,) * 4 + by_expert,
        out_specs=(by_token, by_expert[1]),
        check_vma=False,
    )
```

```python
import functools

import jax
import jax.numpy as jnp
from jax import lax
from jax.experimental import pallas as pl
from jax.experimental.pallas import tpu as pltpu
from jax.sharding import PartitionSpec as P

VMEM_LIMIT = 48 * 1024 * 1024
PAIR = 2
TILE = 1024
AHEAD = 2
NOWHERE = -(1 << 20)


def f32_dot(lhs, rhs, contract=((1,), (0,))):
    return lax.dot_general(lhs, rhs, (contract, ((), ())), preferred_element_type=jnp.float32)


def params():
    return pltpu.CompilerParams(vmem_limit_bytes=VMEM_LIMIT)


def row_places(ids, experts, capacity):
    tok_rows = ids.shape[1]
    names = lax.broadcasted_iota(jnp.int32, (experts, tok_rows), 0)
    chosen = [names == ids[k : k + 1, :] for k in range(ids.shape[0])]
    member = functools.reduce(jnp.logical_or, chosen).astype(jnp.bfloat16)
    before = (
        lax.broadcasted_iota(jnp.int32, (tok_rows, tok_rows), 0)
        < lax.broadcasted_iota(jnp.int32, (tok_rows, tok_rows), 1)
    ).astype(jnp.bfloat16)
    rank = f32_dot(member, before).astype(jnp.int32)
    place = names * (PAIR * capacity) + rank
    return [jnp.sum(jnp.where(pick, place, 0), axis=0, keepdims=True) for pick in chosen]


def hits_at(rows, places):
    at = lax.broadcasted_iota(jnp.int32, (rows, places[0].shape[1]), 0)
    return [at == place for place in places]


def either(hits):
    return functools.reduce(jnp.logical_or, hits).astype(jnp.bfloat16)


def started(pairs, sems):
    copies = [pltpu.make_async_copy(*pair, sems.at[i]) for i, pair in enumerate(pairs)]
    for copy in copies:
        copy.start()
    return copies


def dispatch_kernel(capacity, *refs):
    sources, (out_ref, ids_ref, gates_ref, both_ref, sems) = refs[:4], refs[4:]
    tok_rows = both_ref.shape[0] // 2
    targets = ids_ref, gates_ref, both_ref.at[pl.ds(0, tok_rows)], both_ref.at[pl.ds(tok_rows, tok_rows)]
    ids_copy, gates_copy, tokens_copy, grad_copy = started(zip(sources, targets), sems)
    rows = out_ref.shape[0]
    ids_copy.wait()
    places = row_places(ids_ref[...], rows // (PAIR * capacity), capacity)
    token_hits = hits_at(rows, places)
    grad_hits = hits_at(rows, [place + capacity for place in places])
    gates_copy.wait()
    scales = [jnp.where(hit, 1.0, 0.0) for hit in token_hits]
    scales += [jnp.where(hit, gates_ref[k : k + 1, :], 0.0) for k, hit in enumerate(grad_hits)]
    scale = jnp.sum(sum(scales), axis=1, keepdims=True)
    gather = jnp.concatenate([either(token_hits), either(grad_hits)], axis=1)
    tokens_copy.wait()
    grad_copy.wait()
    out_ref[...] = (scale * f32_dot(gather, both_ref[...])).astype(jnp.bfloat16)


def paired_rows(number, capacity):
    owner = jnp.floor((number.astype(jnp.float32) + 0.5) * (1.0 / capacity)).astype(jnp.int32)
    return number + owner * ((PAIR - 1) * capacity)


def group_size(peers, capacity):
    size = 1
    while peers % (2 * size) == 0 and size * PAIR * capacity < 192:
        size *= 2
    return size


def take_apart(landed_ref, capacity, rows_ref, grads_ref):
    size = group_size(landed_ref.shape[0] // (PAIR * capacity), capacity)
    slots, rows = size * capacity, size * PAIR * capacity
    at = lax.broadcasted_iota(jnp.int32, (slots, rows), 1)
    source = paired_rows(lax.broadcasted_iota(jnp.int32, (slots, 1), 0), capacity)
    mover = jnp.concatenate([(at == source + j * capacity).astype(jnp.bfloat16) for j in range(PAIR)], axis=0)
    for i in range(rows_ref.shape[0] // slots):
        taken = f32_dot(mover, landed_ref[i * rows : (i + 1) * rows, :]).astype(jnp.bfloat16)
        rows_ref[i * slots : (i + 1) * slots, :] = taken[:slots]
        grads_ref[i * slots : (i + 1) * slots, :] = taken[slots:]


def fold_rows(plain_ref, capacity, folded_ref, out_ref, sems):
    size = group_size(plain_ref.shape[0] // capacity, capacity)
    slots, rows = size * capacity, size * PAIR * capacity
    width = folded_ref.shape[1]
    at = lax.broadcasted_iota(jnp.int32, (rows, slots), 0)
    target = paired_rows(lax.broadcasted_iota(jnp.int32, (1, slots), 1), capacity)
    mover = jnp.concatenate([(at == target + j * capacity).astype(jnp.bfloat16) for j in range(PAIR)], axis=1)
    copies = []
    for i in range(plain_ref.shape[0] // slots):
        plain = plain_ref[i * slots : (i + 1) * slots, :].astype(jnp.bfloat16)
        halves = jnp.concatenate([plain[:, j * width : (j + 1) * width] for j in range(PAIR)], axis=0)
        part = slice(i * rows, (i + 1) * rows)
        folded_ref[part, :] = f32_dot(mover, halves).astype(jnp.bfloat16)
        copies.append(pltpu.make_async_copy(folded_ref.at[part], out_ref.at[part], sems.at[i]))
        copies[-1].start()
    return copies


def unit_tiles(units):
    size = min(units, TILE)
    return [(start, size) for start in range(0, units, size)]


def expert_kernel(capacity, landed_ref, up_ref, down_ref, hidden_out, grads_out, back_out, *scratch):
    up, down, rows, grads, hidden, masked, total, back, weight_sems, hidden_sems, grads_sem, back_sems = scratch
    tiles = unit_tiles(up.shape[1])

    def weight_copies(i):
        at = pl.ds(*tiles[i])
        return [
            pltpu.make_async_copy(up_ref.at[:, at], up.at[:, at], weight_sems.at[0, i]),
            pltpu.make_async_copy(down_ref.at[at], down.at[at], weight_sems.at[1, i]),
        ]

    def start_weights(i):
        if i < len(tiles):
            arriving[i] = weight_copies(i)
            for copy in arriving[i]:
                copy.start()

    arriving, leaving = {}, []
    for i in range(AHEAD):
        start_weights(i)
    take_apart(landed_ref, capacity, rows, grads)
    leaving.append(pltpu.make_async_copy(grads, grads_out, grads_sem.at[0]))
    leaving[-1].start()
    for i, (start, size) in enumerate(tiles):
        here = slice(start, start + size)
        start_weights(i + AHEAD)
        for copy in arriving[i]:
            copy.wait()
        preact = f32_dot(rows[...], up[:, here])
        hidden_grad = f32_dot(grads[...], down[here, :], ((1,), (1,)))
        hidden[:, here] = jnp.maximum(preact, 0.0).astype(jnp.bfloat16)
        masked[:, here] = jnp.where(preact > 0, hidden_grad, 0.0).astype(jnp.bfloat16)
        leaving.append(pltpu.make_async_copy(hidden.at[:, here], hidden_out.at[:, here], hidden_sems.at[i]))
        leaving[-1].start()
    total[...] = f32_dot(masked[...], up[...], ((1,), (1,)))
    for copy in leaving + fold_rows(total, capacity, back, back_out, back_sems):
        copy.wait()


def down_grad_kernel(grads_ref, hidden_ref, out_ref):
    out_ref[...] = f32_dot(hidden_ref[...], grads_ref[...], ((0,), (0,))).astype(jnp.bfloat16)


def pick_map_kernel(capacity, ids_ref, after_ref, out_ref):
    tok_rows, rows = ids_ref.shape[1], out_ref.shape[1]
    places = row_places(ids_ref[...], rows // (PAIR * capacity), capacity)
    for j in range(PAIR):
        chosen = either(hits_at(rows, [place + j * capacity for place in places]))
        out_ref[j * tok_rows : (j + 1) * tok_rows, :] = chosen.T


def pick_kernel(map_ref, returned_ref, out_ref):
    tok_rows, width = out_ref.shape[0], returned_ref.shape[1]
    picked = f32_dot(map_ref[...], returned_ref[...]).astype(jnp.bfloat16)
    for j in range(PAIR):
        out_ref[:, j * width : (j + 1) * width] = picked[j * tok_rows : (j + 1) * tok_rows]


def exchange(rows):
    axes = ("row", "col")
    peers = lax.axis_size(axes)
    cut = rows.reshape(peers, rows.shape[0] // peers, rows.shape[1])
    return lax.all_to_all(cut, axes, split_axis=0, concat_axis=0, tiled=True).reshape(rows.shape)


def in_hbm(array):
    return pltpu.with_memory_space_constraint(array, pltpu.HBM)


def held(rows, columns, kind=jnp.bfloat16):
    return pltpu.VMEM((rows, columns), kind)


def shards(tokens, out_grad, expert_ids, gates, up_weight, down_weight):
    tok_rows, features = tokens.shape
    top_count = expert_ids.shape[1]
    units = up_weight.shape[2]
    peers = lax.axis_size(("row", "col"))
    capacity = 3 * tok_rows * top_count // (2 * peers)
    slots, rows, width = peers * capacity, peers * PAIR * capacity, features // PAIR
    tile = min(units, TILE // 2)
    steps = units // tile
    bf16, f32 = jnp.bfloat16, jnp.float32
    shape = jax.ShapeDtypeStruct
    dma = pltpu.SemaphoreType.DMA
    flops = 2 * slots * features * units
    weight_bytes = 2 * features * units

    def cost(matmuls, weights):
        return pl.CostEstimate(flops=matmuls * flops, bytes_accessed=weights * weight_bytes, transcendentals=0)

    ids = expert_ids.T
    hbm = pl.BlockSpec(memory_space=pltpu.HBM)
    vmem = pl.BlockSpec(memory_space=pltpu.VMEM)
    anywhere = pl.BlockSpec(memory_space=pl.ANY)
    tiles = unit_tiles(units)

    sent = pl.pallas_call(
        functools.partial(dispatch_kernel, capacity),
        out_shape=shape((rows, features), bf16),
        in_specs=[hbm, hbm, hbm, hbm],
        scratch_shapes=[
            held(top_count, tok_rows, jnp.int32),
            held(top_count, tok_rows, f32),
            held(2 * tok_rows, features),
            dma((4,)),
        ],
        compiler_params=params(),
        name="dispatch",
    )(*[in_hbm(array) for array in (ids, gates.T, tokens, out_grad)])
    landed = exchange(sent)

    hidden, grads, back = pl.pallas_call(
        functools.partial(expert_kernel, capacity),
        out_shape=(
            pltpu.HBM((slots, units), bf16),
            pltpu.HBM((slots, features), bf16),
            pltpu.HBM((rows, width), bf16),
        ),
        in_specs=[vmem, hbm, hbm],
        out_specs=(hbm, hbm, hbm),
        scratch_shapes=[
            held(features, units),
            held(units, features),
            held(slots, features),
            held(slots, features),
            held(slots, units),
            held(slots, units),
            held(slots, features, f32),
            held(rows, width),
            dma((2, len(tiles))),
            dma((len(tiles),)),
            dma((1,)),
            dma((peers // group_size(peers, capacity),)),
        ],
        compiler_params=params(),
        cost_estimate=cost(3, 2),
        name="expert",
    )(landed, in_hbm(up_weight[0]), in_hbm(down_weight[0]))
    returned = exchange(back)

    down_grad = pl.pallas_call(
        down_grad_kernel,
        out_shape=shape((1, units, features), bf16),
        grid=(steps,),
        in_specs=[pl.BlockSpec((slots, features), lambda i: (0, 0)), pl.BlockSpec((slots, tile), lambda i: (0, i))],
        out_specs=pl.BlockSpec((None, tile, features), lambda i: (0, i, 0)),
        compiler_params=params(),
        cost_estimate=cost(1, 1),
        name="down_grad",
    )(in_hbm(grads), in_hbm(hidden))

    pick_map = pl.pallas_call(
        functools.partial(pick_map_kernel, capacity),
        out_shape=shape((PAIR * tok_rows, rows), bf16),
        in_specs=[vmem, anywhere],
        compiler_params=params(),
        name="pick_map",
    )(ids, in_hbm(grads))
    input_grad = pl.pallas_call(
        pick_kernel,
        out_shape=shape((tok_rows, features), bf16),
        compiler_params=params(),
        name="pick",
    )(pick_map, returned)
    return input_grad, down_grad


def pooled_shards(tokens, out_grad, expert_ids, gates, up_weight, down_weight):
    tok_rows = tokens.shape[0]
    top_count = expert_ids.shape[1]
    features = tokens.shape[1]
    groups = lax.axis_size("row")
    col_count = lax.axis_size("col")
    experts = groups * col_count
    capacity = 3 * tok_rows * top_count // (2 * experts)
    flat_ids = expert_ids.reshape(-1)
    onehot = (flat_ids[:, None] == jnp.arange(experts, dtype=jnp.int32)[None, :]).astype(jnp.int32)
    earlier = jnp.cumsum(onehot, axis=0) - onehot
    slot_index = jnp.sum(earlier * onehot, axis=1)
    target = flat_ids * capacity + slot_index
    placer = (jnp.arange(experts * capacity, dtype=jnp.int32)[:, None] == target[None, :]).astype(
        jnp.bfloat16
    )
    token_rows = jnp.repeat(tokens, top_count, axis=0)
    weighted = (
        gates.reshape(-1)[:, None] * jnp.repeat(out_grad, top_count, axis=0).astype(jnp.float32)
    ).astype(jnp.bfloat16)
    send_inputs = jnp.dot(placer, token_rows, preferred_element_type=jnp.float32).astype(
        jnp.bfloat16
    )
    send_grads = jnp.dot(placer, weighted, preferred_element_type=jnp.float32).astype(jnp.bfloat16)
    landed_inputs, landed_grads = (
        lax.all_to_all(
            send_inputs.reshape(experts, capacity, features),
            ("row", "col"),
            split_axis=0,
            concat_axis=0,
            tiled=True,
        ),
        lax.all_to_all(
            send_grads.reshape(experts, capacity, features),
            ("row", "col"),
            split_axis=0,
            concat_axis=0,
            tiled=True,
        ),
    )
    pooled_inputs, pooled_grads = (
        lax.all_gather(landed_inputs, "rep", axis=0, tiled=True),
        lax.all_gather(landed_grads, "rep", axis=0, tiled=True),
    )
    slot_rows = pooled_inputs.shape[0] * capacity
    input_rows = pooled_inputs.reshape(slot_rows, features)
    grad_rows = pooled_grads.reshape(slot_rows, features)
    up_block = up_weight[0]
    down_block = down_weight[0]
    preact = jnp.dot(input_rows, up_block, preferred_element_type=jnp.float32)
    hidden = jnp.maximum(preact, 0.0).astype(jnp.bfloat16)
    hidden_grad = lax.dot_general(
        grad_rows, down_block, (((1,), (1,)), ((), ())), preferred_element_type=jnp.float32
    )
    preact_grad = jnp.where(preact > 0, hidden_grad, 0.0).astype(jnp.bfloat16)
    weight_grad = lax.dot_general(
        hidden, grad_rows, (((0,), (0,)), ((), ())), preferred_element_type=jnp.float32
    )
    down_grad = weight_grad.astype(jnp.bfloat16)[None]
    summed_rows = lax.psum_scatter(
        lax.dot_general(
            preact_grad, up_block, (((1,), (1,)), ((), ())), preferred_element_type=jnp.float32
        ).astype(jnp.bfloat16),
        "rep",
        scatter_dimension=0,
        tiled=True,
    )
    returned = lax.all_to_all(
        summed_rows.reshape(experts, capacity, features),
        ("row", "col"),
        split_axis=0,
        concat_axis=0,
        tiled=True,
    )
    returned = returned.reshape(experts * capacity, features)
    picked = lax.dot_general(
        placer, returned, (((0,), (0,)), ((), ())), preferred_element_type=jnp.float32
    )
    input_grad = jnp.sum(picked.reshape(tok_rows, top_count, features), axis=1).astype(jnp.bfloat16)
    return (input_grad, down_grad)


def solution(mesh):
    by_token = P(("rep", "row", "col"), None)
    by_expert = (P(("row", "col"), None, "rep"), P(("row", "col"), "rep", None))
    return jax.shard_map(
        shards if mesh.shape["rep"] == 1 else pooled_shards,
        mesh=mesh,
        in_specs=(by_token,) * 4 + by_expert,
        out_specs=(by_token, by_expert[1]),
        check_vma=False,
    )
```

```python
import functools

import jax
import jax.numpy as jnp
from jax import lax
from jax.experimental import pallas as pl
from jax.experimental.pallas import tpu as pltpu
from jax.sharding import PartitionSpec as P

VMEM_LIMIT = 44 * 1024 * 1024
PAIR = 2
TILE = 1024
AHEAD = 2
NOWHERE = -(1 << 20)


def f32_dot(lhs, rhs, contract=((1,), (0,))):
    return lax.dot_general(lhs, rhs, (contract, ((), ())), preferred_element_type=jnp.float32)


def params():
    return pltpu.CompilerParams(vmem_limit_bytes=VMEM_LIMIT)


def row_places(ids, experts, capacity):
    tok_rows = ids.shape[1]
    names = lax.broadcasted_iota(jnp.int32, (experts, tok_rows), 0)
    chosen = [names == ids[k : k + 1, :] for k in range(ids.shape[0])]
    member = functools.reduce(jnp.logical_or, chosen).astype(jnp.bfloat16)
    before = (
        lax.broadcasted_iota(jnp.int32, (tok_rows, tok_rows), 0)
        < lax.broadcasted_iota(jnp.int32, (tok_rows, tok_rows), 1)
    ).astype(jnp.bfloat16)
    rank = f32_dot(member, before).astype(jnp.int32)
    place = names * (PAIR * capacity) + rank
    return [jnp.sum(jnp.where(pick, place, 0), axis=0, keepdims=True) for pick in chosen]


def hits_at(rows, places):
    at = lax.broadcasted_iota(jnp.int32, (rows, places[0].shape[1]), 0)
    return [at == place for place in places]


def either(hits):
    return functools.reduce(jnp.logical_or, hits).astype(jnp.bfloat16)


def started(pairs, sems):
    copies = [pltpu.make_async_copy(*pair, sems.at[i]) for i, pair in enumerate(pairs)]
    for copy in copies:
        copy.start()
    return copies


def dispatch_kernel(capacity, *refs):
    sources, (up_ref, down_ref, out_ref, up_out, down_out, ids_ref, gates_ref, both_ref, sems) = refs[:4], refs[4:]
    tok_rows = both_ref.shape[0] // 2
    targets = ids_ref, gates_ref, both_ref.at[pl.ds(0, tok_rows)], both_ref.at[pl.ds(tok_rows, tok_rows)]
    ids_copy, gates_copy, tokens_copy, grad_copy = started(zip(sources, targets), sems)
    first = pl.ds(0, down_out.shape[0])
    weights = (up_ref.at[:, first], up_out), (down_ref.at[first], down_out)
    weight_copies = started(weights, sems.at[pl.ds(4, 2)])
    rows = out_ref.shape[0]
    ids_copy.wait()
    places = row_places(ids_ref[...], rows // (PAIR * capacity), capacity)
    token_hits = hits_at(rows, places)
    grad_hits = hits_at(rows, [place + capacity for place in places])
    gates_copy.wait()
    scales = [jnp.where(hit, 1.0, 0.0) for hit in token_hits]
    scales += [jnp.where(hit, gates_ref[k : k + 1, :], 0.0) for k, hit in enumerate(grad_hits)]
    scale = jnp.sum(sum(scales), axis=1, keepdims=True)
    gather = jnp.concatenate([either(token_hits), either(grad_hits)], axis=1)
    tokens_copy.wait()
    grad_copy.wait()
    out_ref[...] = (scale * f32_dot(gather, both_ref[...])).astype(jnp.bfloat16)
    for copy in weight_copies:
        copy.wait()


def paired_rows(number, capacity):
    owner = jnp.floor((number.astype(jnp.float32) + 0.5) * (1.0 / capacity)).astype(jnp.int32)
    return number + owner * ((PAIR - 1) * capacity)


def group_size(peers, capacity):
    size = 1
    while peers % (2 * size) == 0 and size * PAIR * capacity < 192:
        size *= 2
    return size


def take_apart(landed_ref, capacity, rows_ref, grads_ref):
    size = group_size(landed_ref.shape[0] // (PAIR * capacity), capacity)
    slots, rows = size * capacity, size * PAIR * capacity
    at = lax.broadcasted_iota(jnp.int32, (slots, rows), 1)
    source = paired_rows(lax.broadcasted_iota(jnp.int32, (slots, 1), 0), capacity)
    mover = jnp.concatenate([(at == source + j * capacity).astype(jnp.bfloat16) for j in range(PAIR)], axis=0)
    for i in range(rows_ref.shape[0] // slots):
        taken = f32_dot(mover, landed_ref[i * rows : (i + 1) * rows, :]).astype(jnp.bfloat16)
        rows_ref[i * slots : (i + 1) * slots, :] = taken[:slots]
        grads_ref[i * slots : (i + 1) * slots, :] = taken[slots:]


def fold_rows(plain_ref, capacity, folded_ref, out_ref, sems):
    size = group_size(plain_ref.shape[0] // capacity, capacity)
    slots, rows = size * capacity, size * PAIR * capacity
    width = folded_ref.shape[1]
    at = lax.broadcasted_iota(jnp.int32, (rows, slots), 0)
    target = paired_rows(lax.broadcasted_iota(jnp.int32, (1, slots), 1), capacity)
    mover = jnp.concatenate([(at == target + j * capacity).astype(jnp.bfloat16) for j in range(PAIR)], axis=1)
    copies = []
    for i in range(plain_ref.shape[0] // slots):
        plain = plain_ref[i * slots : (i + 1) * slots, :].astype(jnp.bfloat16)
        halves = jnp.concatenate([plain[:, j * width : (j + 1) * width] for j in range(PAIR)], axis=0)
        part = slice(i * rows, (i + 1) * rows)
        folded_ref[part, :] = f32_dot(mover, halves).astype(jnp.bfloat16)
        copies.append(pltpu.make_async_copy(folded_ref.at[part], out_ref.at[part], sems.at[i]))
        copies[-1].start()
    return copies


def unit_tiles(units):
    size = min(units, TILE)
    return [(start, size) for start in range(0, units, size)]


def expert_kernel(
    capacity, landed_ref, first_up, first_down, up_ref, down_ref, hidden_out, grads_out, back_out, *scratch
):
    up, down, rows, grads, hidden, masked, total, back, weight_sems, hidden_sems, grads_sem, back_sems = scratch
    tiles = unit_tiles(up.shape[1])

    def weight_copies(i):
        at = pl.ds(*tiles[i])
        return [
            pltpu.make_async_copy(up_ref.at[:, at], up.at[:, at], weight_sems.at[0, i]),
            pltpu.make_async_copy(down_ref.at[at], down.at[at], weight_sems.at[1, i]),
        ]

    def start_weights(i):
        if i < len(tiles):
            arriving[i] = weight_copies(i)
            for copy in arriving[i]:
                copy.start()

    def add_row_grad(i):
        start, size = tiles[i]
        weights = up[:, start : start + size] if i else first_up[...]
        part = f32_dot(masked[i % 2, :, :size], weights, ((1,), (1,)))
        total[...] = part if i == 0 else total[...] + part

    arriving, leaving = {}, []
    for i in range(1, AHEAD):
        start_weights(i)
    take_apart(landed_ref, capacity, rows, grads)
    leaving.append(pltpu.make_async_copy(grads, grads_out, grads_sem.at[0]))
    leaving[-1].start()
    for i, (start, size) in enumerate(tiles):
        here = slice(start, start + size)
        start_weights(i + AHEAD)
        for copy in arriving.get(i, ()):
            copy.wait()
        preact = f32_dot(rows[...], up[:, here] if i else first_up[...])
        hidden_grad = f32_dot(grads[...], down[here, :] if i else first_down[...], ((1,), (1,)))
        if i:
            add_row_grad(i - 1)
        hidden[:, here] = jnp.maximum(preact, 0.0).astype(jnp.bfloat16)
        masked[i % 2, :, :size] = jnp.where(preact > 0, hidden_grad, 0.0).astype(jnp.bfloat16)
        leaving.append(pltpu.make_async_copy(hidden.at[:, here], hidden_out.at[:, here], hidden_sems.at[i]))
        leaving[-1].start()
    add_row_grad(len(tiles) - 1)
    for copy in leaving + fold_rows(total, capacity, back, back_out, back_sems):
        copy.wait()


def down_grad_kernel(grads_ref, hidden_ref, out_ref):
    out_ref[...] = f32_dot(hidden_ref[...], grads_ref[...], ((0,), (0,))).astype(jnp.bfloat16)


def pick_map_kernel(capacity, ids_ref, after_ref, out_ref):
    tok_rows, rows = ids_ref.shape[1], out_ref.shape[1]
    places = row_places(ids_ref[...], rows // (PAIR * capacity), capacity)
    for j in range(PAIR):
        chosen = either(hits_at(rows, [place + j * capacity for place in places]))
        out_ref[j * tok_rows : (j + 1) * tok_rows, :] = chosen.T


def pick_kernel(map_ref, returned_ref, out_ref):
    tok_rows, width = out_ref.shape[0], returned_ref.shape[1]
    picked = f32_dot(map_ref[...], returned_ref[...]).astype(jnp.bfloat16)
    for j in range(PAIR):
        out_ref[:, j * width : (j + 1) * width] = picked[j * tok_rows : (j + 1) * tok_rows]


def exchange(rows):
    axes = ("row", "col")
    peers = lax.axis_size(axes)
    cut = rows.reshape(peers, rows.shape[0] // peers, rows.shape[1])
    return lax.all_to_all(cut, axes, split_axis=0, concat_axis=0, tiled=True).reshape(rows.shape)


def in_hbm(array):
    return pltpu.with_memory_space_constraint(array, pltpu.HBM)


def in_vmem(array):
    return pltpu.with_memory_space_constraint(array, pltpu.VMEM)


def held(rows, columns, kind=jnp.bfloat16):
    return pltpu.VMEM((rows, columns), kind)


def shards(tokens, out_grad, expert_ids, gates, up_weight, down_weight):
    tok_rows, features = tokens.shape
    top_count = expert_ids.shape[1]
    units = up_weight.shape[2]
    peers = lax.axis_size(("row", "col"))
    capacity = 3 * tok_rows * top_count // (2 * peers)
    slots, rows, width = peers * capacity, peers * PAIR * capacity, features // PAIR
    tile = min(units, TILE // 2)
    steps = units // tile
    bf16, f32 = jnp.bfloat16, jnp.float32
    shape = jax.ShapeDtypeStruct
    dma = pltpu.SemaphoreType.DMA
    flops = 2 * slots * features * units
    weight_bytes = 2 * features * units

    def cost(matmuls, weights):
        return pl.CostEstimate(flops=matmuls * flops, bytes_accessed=weights * weight_bytes, transcendentals=0)

    ids = expert_ids.T
    hbm = pl.BlockSpec(memory_space=pltpu.HBM)
    vmem = pl.BlockSpec(memory_space=pltpu.VMEM)
    anywhere = pl.BlockSpec(memory_space=pl.ANY)
    tiles = unit_tiles(units)

    size = tiles[0][1]
    weights = in_hbm(up_weight[0]), in_hbm(down_weight[0])
    sent, first_up, first_down = pl.pallas_call(
        functools.partial(dispatch_kernel, capacity),
        out_shape=(
            shape((rows, features), bf16),
            pltpu.VMEM((features, size), bf16),
            pltpu.VMEM((size, features), bf16),
        ),
        in_specs=[hbm, hbm, hbm, hbm, hbm, hbm],
        scratch_shapes=[
            held(top_count, tok_rows, jnp.int32),
            held(top_count, tok_rows, f32),
            held(2 * tok_rows, features),
            dma((6,)),
        ],
        compiler_params=params(),
        name="dispatch",
    )(*[in_hbm(array) for array in (ids, gates.T, tokens, out_grad)], *weights)
    landed = exchange(sent)

    hidden, grads, back = pl.pallas_call(
        functools.partial(expert_kernel, capacity),
        out_shape=(
            pltpu.HBM((slots, units), bf16),
            pltpu.HBM((slots, features), bf16),
            pltpu.HBM((rows, width), bf16),
        ),
        in_specs=[vmem, vmem, vmem, hbm, hbm],
        out_specs=(hbm, hbm, hbm),
        scratch_shapes=[
            held(features, units),
            held(units, features),
            held(slots, features),
            held(slots, features),
            held(slots, units),
            pltpu.VMEM((2, slots, tiles[0][1]), bf16),
            held(slots, features, f32),
            held(rows, width),
            dma((2, len(tiles))),
            dma((len(tiles),)),
            dma((1,)),
            dma((peers // group_size(peers, capacity),)),
        ],
        compiler_params=params(),
        cost_estimate=cost(3, 2),
        name="expert",
    )(landed, in_vmem(first_up), in_vmem(first_down), *weights)
    returned = exchange(back)

    down_grad = pl.pallas_call(
        down_grad_kernel,
        out_shape=shape((1, units, features), bf16),
        grid=(steps,),
        in_specs=[pl.BlockSpec((slots, features), lambda i: (0, 0)), pl.BlockSpec((slots, tile), lambda i: (0, i))],
        out_specs=pl.BlockSpec((None, tile, features), lambda i: (0, i, 0)),
        compiler_params=params(),
        cost_estimate=cost(1, 1),
        name="down_grad",
    )(in_hbm(grads), in_hbm(hidden))

    pick_map = pl.pallas_call(
        functools.partial(pick_map_kernel, capacity),
        out_shape=shape((PAIR * tok_rows, rows), bf16),
        in_specs=[vmem, anywhere],
        compiler_params=params(),
        name="pick_map",
    )(ids, in_hbm(grads))
    input_grad = pl.pallas_call(
        pick_kernel,
        out_shape=shape((tok_rows, features), bf16),
        compiler_params=params(),
        name="pick",
    )(pick_map, returned)
    return input_grad, down_grad


def pooled_shards(tokens, out_grad, expert_ids, gates, up_weight, down_weight):
    tok_rows = tokens.shape[0]
    top_count = expert_ids.shape[1]
    features = tokens.shape[1]
    groups = lax.axis_size("row")
    col_count = lax.axis_size("col")
    experts = groups * col_count
    capacity = 3 * tok_rows * top_count // (2 * experts)
    flat_ids = expert_ids.reshape(-1)
    onehot = (flat_ids[:, None] == jnp.arange(experts, dtype=jnp.int32)[None, :]).astype(jnp.int32)
    earlier = jnp.cumsum(onehot, axis=0) - onehot
    slot_index = jnp.sum(earlier * onehot, axis=1)
    target = flat_ids * capacity + slot_index
    placer = (jnp.arange(experts * capacity, dtype=jnp.int32)[:, None] == target[None, :]).astype(
        jnp.bfloat16
    )
    token_rows = jnp.repeat(tokens, top_count, axis=0)
    weighted = (
        gates.reshape(-1)[:, None] * jnp.repeat(out_grad, top_count, axis=0).astype(jnp.float32)
    ).astype(jnp.bfloat16)
    send_inputs = jnp.dot(placer, token_rows, preferred_element_type=jnp.float32).astype(
        jnp.bfloat16
    )
    send_grads = jnp.dot(placer, weighted, preferred_element_type=jnp.float32).astype(jnp.bfloat16)
    landed_inputs, landed_grads = (
        lax.all_to_all(
            send_inputs.reshape(experts, capacity, features),
            ("row", "col"),
            split_axis=0,
            concat_axis=0,
            tiled=True,
        ),
        lax.all_to_all(
            send_grads.reshape(experts, capacity, features),
            ("row", "col"),
            split_axis=0,
            concat_axis=0,
            tiled=True,
        ),
    )
    pooled_inputs, pooled_grads = (
        lax.all_gather(landed_inputs, "rep", axis=0, tiled=True),
        lax.all_gather(landed_grads, "rep", axis=0, tiled=True),
    )
    slot_rows = pooled_inputs.shape[0] * capacity
    input_rows = pooled_inputs.reshape(slot_rows, features)
    grad_rows = pooled_grads.reshape(slot_rows, features)
    up_block = up_weight[0]
    down_block = down_weight[0]
    preact = jnp.dot(input_rows, up_block, preferred_element_type=jnp.float32)
    hidden = jnp.maximum(preact, 0.0).astype(jnp.bfloat16)
    hidden_grad = lax.dot_general(
        grad_rows, down_block, (((1,), (1,)), ((), ())), preferred_element_type=jnp.float32
    )
    preact_grad = jnp.where(preact > 0, hidden_grad, 0.0).astype(jnp.bfloat16)
    weight_grad = lax.dot_general(
        hidden, grad_rows, (((0,), (0,)), ((), ())), preferred_element_type=jnp.float32
    )
    down_grad = weight_grad.astype(jnp.bfloat16)[None]
    summed_rows = lax.psum_scatter(
        lax.dot_general(
            preact_grad, up_block, (((1,), (1,)), ((), ())), preferred_element_type=jnp.float32
        ).astype(jnp.bfloat16),
        "rep",
        scatter_dimension=0,
        tiled=True,
    )
    returned = lax.all_to_all(
        summed_rows.reshape(experts, capacity, features),
        ("row", "col"),
        split_axis=0,
        concat_axis=0,
        tiled=True,
    )
    returned = returned.reshape(experts * capacity, features)
    picked = lax.dot_general(
        placer, returned, (((0,), (0,)), ((), ())), preferred_element_type=jnp.float32
    )
    input_grad = jnp.sum(picked.reshape(tok_rows, top_count, features), axis=1).astype(jnp.bfloat16)
    return (input_grad, down_grad)


def solution(mesh):
    by_token = P(("rep", "row", "col"), None)
    by_expert = (P(("row", "col"), None, "rep"), P(("row", "col"), "rep", None))
    return jax.shard_map(
        shards if mesh.shape["rep"] == 1 else pooled_shards,
        mesh=mesh,
        in_specs=(by_token,) * 4 + by_expert,
        out_specs=(by_token, by_expert[1]),
        check_vma=False,
    )
```

```python
import functools

import jax
import jax.numpy as jnp
from jax import lax
from jax.experimental import pallas as pl
from jax.experimental.pallas import tpu as pltpu
from jax.sharding import PartitionSpec as P

VMEM_LIMIT = 44 * 1024 * 1024
PAIR = 2
TILE = 1024
AHEAD = 2
NOWHERE = -(1 << 20)


def f32_dot(lhs, rhs, contract=((1,), (0,))):
    return lax.dot_general(lhs, rhs, (contract, ((), ())), preferred_element_type=jnp.float32)


def params():
    return pltpu.CompilerParams(vmem_limit_bytes=VMEM_LIMIT)


def row_places(ids, experts, capacity):
    tok_rows = ids.shape[1]
    names = lax.broadcasted_iota(jnp.int32, (experts, tok_rows), 0)
    chosen = [names == ids[k : k + 1, :] for k in range(ids.shape[0])]
    member = functools.reduce(jnp.logical_or, chosen).astype(jnp.bfloat16)
    before = (
        lax.broadcasted_iota(jnp.int32, (tok_rows, tok_rows), 0)
        < lax.broadcasted_iota(jnp.int32, (tok_rows, tok_rows), 1)
    ).astype(jnp.bfloat16)
    rank = f32_dot(member, before).astype(jnp.int32)
    place = names * (PAIR * capacity) + rank
    return [jnp.sum(jnp.where(pick, place, 0), axis=0, keepdims=True) for pick in chosen]


def hits_at(rows, places):
    at = lax.broadcasted_iota(jnp.int32, (rows, places[0].shape[1]), 0)
    return [at == place for place in places]


def either(hits):
    return functools.reduce(jnp.logical_or, hits).astype(jnp.bfloat16)


def started(pairs, sems):
    copies = [pltpu.make_async_copy(*pair, sems.at[i]) for i, pair in enumerate(pairs)]
    for copy in copies:
        copy.start()
    return copies


def dispatch_kernel(capacity, *refs):
    sources, (up_ref, out_ref, up_out, ids_ref, gates_ref, both_ref, sems) = refs[:4], refs[4:]
    tok_rows = both_ref.shape[0] // 2
    targets = ids_ref, gates_ref, both_ref.at[pl.ds(0, tok_rows)], both_ref.at[pl.ds(tok_rows, tok_rows)]
    ids_copy, gates_copy, tokens_copy, grad_copy = started(zip(sources, targets), sems)
    first_tile = pltpu.make_async_copy(up_ref.at[:, pl.ds(0, up_out.shape[1])], up_out, sems.at[4])
    first_tile.start()
    rows = out_ref.shape[0]
    ids_copy.wait()
    places = row_places(ids_ref[...], rows // (PAIR * capacity), capacity)
    token_hits = hits_at(rows, places)
    grad_hits = hits_at(rows, [place + capacity for place in places])
    gates_copy.wait()
    scales = [jnp.where(hit, 1.0, 0.0) for hit in token_hits]
    scales += [jnp.where(hit, gates_ref[k : k + 1, :], 0.0) for k, hit in enumerate(grad_hits)]
    scale = jnp.sum(sum(scales), axis=1, keepdims=True)
    gather = jnp.concatenate([either(token_hits), either(grad_hits)], axis=1)
    tokens_copy.wait()
    grad_copy.wait()
    out_ref[...] = (scale * f32_dot(gather, both_ref[...])).astype(jnp.bfloat16)
    first_tile.wait()


def paired_rows(number, capacity):
    owner = jnp.floor((number.astype(jnp.float32) + 0.5) * (1.0 / capacity)).astype(jnp.int32)
    return number + owner * ((PAIR - 1) * capacity)


def group_size(peers, capacity):
    size = 1
    while peers % (2 * size) == 0 and size * PAIR * capacity < 192:
        size *= 2
    return size


def take_apart(landed_ref, capacity, rows_ref, grads_ref):
    size = group_size(landed_ref.shape[0] // (PAIR * capacity), capacity)
    slots, rows = size * capacity, size * PAIR * capacity
    at = lax.broadcasted_iota(jnp.int32, (slots, rows), 1)
    source = paired_rows(lax.broadcasted_iota(jnp.int32, (slots, 1), 0), capacity)
    mover = jnp.concatenate([(at == source + j * capacity).astype(jnp.bfloat16) for j in range(PAIR)], axis=0)
    for i in range(rows_ref.shape[0] // slots):
        taken = f32_dot(mover, landed_ref[i * rows : (i + 1) * rows, :]).astype(jnp.bfloat16)
        rows_ref[i * slots : (i + 1) * slots, :] = taken[:slots]
        grads_ref[i * slots : (i + 1) * slots, :] = taken[slots:]


def fold_rows(plain_ref, capacity, folded_ref, out_ref, sems):
    size = group_size(plain_ref.shape[0] // capacity, capacity)
    slots, rows = size * capacity, size * PAIR * capacity
    width = folded_ref.shape[1]
    at = lax.broadcasted_iota(jnp.int32, (rows, slots), 0)
    target = paired_rows(lax.broadcasted_iota(jnp.int32, (1, slots), 1), capacity)
    mover = jnp.concatenate([(at == target + j * capacity).astype(jnp.bfloat16) for j in range(PAIR)], axis=1)
    copies = []
    for i in range(plain_ref.shape[0] // slots):
        plain = plain_ref[i * slots : (i + 1) * slots, :].astype(jnp.bfloat16)
        halves = jnp.concatenate([plain[:, j * width : (j + 1) * width] for j in range(PAIR)], axis=0)
        part = slice(i * rows, (i + 1) * rows)
        folded_ref[part, :] = f32_dot(mover, halves).astype(jnp.bfloat16)
        copies.append(pltpu.make_async_copy(folded_ref.at[part], out_ref.at[part], sems.at[i]))
        copies[-1].start()
    return copies


def unit_tiles(units):
    size = min(units, TILE)
    return [(start, size) for start in range(0, units, size)]


def expert_kernel(
    capacity, landed_ref, first_up, up_ref, down_ref, hidden_out, grads_out, back_out, *scratch
):
    up, down, rows, grads, hidden, masked, total, back, weight_sems, hidden_sems, grads_sem, back_sems = scratch
    tiles = unit_tiles(up.shape[1])

    def weight_copies(i):
        at = pl.ds(*tiles[i])
        copies = [pltpu.make_async_copy(down_ref.at[at], down.at[at], weight_sems.at[1, i])]
        if i:
            copies.append(pltpu.make_async_copy(up_ref.at[:, at], up.at[:, at], weight_sems.at[0, i]))
        return copies

    def start_weights(i):
        if i < len(tiles):
            arriving[i] = weight_copies(i)
            for copy in arriving[i]:
                copy.start()

    def add_row_grad(i):
        start, size = tiles[i]
        weights = up[:, start : start + size] if i else first_up[...]
        part = f32_dot(masked[i % 2, :, :size], weights, ((1,), (1,)))
        total[...] = part if i == 0 else total[...] + part

    arriving, leaving = {}, []
    start_weights(0)
    take_apart(landed_ref, capacity, rows, grads)
    for i in range(1, AHEAD):
        start_weights(i)
    leaving.append(pltpu.make_async_copy(grads, grads_out, grads_sem.at[0]))
    leaving[-1].start()
    for i, (start, size) in enumerate(tiles):
        here = slice(start, start + size)
        start_weights(i + AHEAD)
        for copy in arriving[i][1:]:
            copy.wait()
        preact = f32_dot(rows[...], up[:, here] if i else first_up[...])
        arriving[i][0].wait()
        hidden_grad = f32_dot(grads[...], down[here, :], ((1,), (1,)))
        if i:
            add_row_grad(i - 1)
        hidden[:, here] = jnp.maximum(preact, 0.0).astype(jnp.bfloat16)
        masked[i % 2, :, :size] = jnp.where(preact > 0, hidden_grad, 0.0).astype(jnp.bfloat16)
        leaving.append(pltpu.make_async_copy(hidden.at[:, here], hidden_out.at[:, here], hidden_sems.at[i]))
        leaving[-1].start()
    add_row_grad(len(tiles) - 1)
    for copy in leaving + fold_rows(total, capacity, back, back_out, back_sems):
        copy.wait()


def down_grad_kernel(grads_ref, hidden_ref, out_ref):
    out_ref[...] = f32_dot(hidden_ref[...], grads_ref[...], ((0,), (0,))).astype(jnp.bfloat16)


def pick_map_kernel(capacity, ids_ref, after_ref, out_ref):
    tok_rows, rows = ids_ref.shape[1], out_ref.shape[1]
    places = row_places(ids_ref[...], rows // (PAIR * capacity), capacity)
    for j in range(PAIR):
        chosen = either(hits_at(rows, [place + j * capacity for place in places]))
        out_ref[j * tok_rows : (j + 1) * tok_rows, :] = chosen.T


def pick_kernel(map_ref, returned_ref, out_ref):
    tok_rows, width = out_ref.shape[0], returned_ref.shape[1]
    picked = f32_dot(map_ref[...], returned_ref[...]).astype(jnp.bfloat16)
    for j in range(PAIR):
        out_ref[:, j * width : (j + 1) * width] = picked[j * tok_rows : (j + 1) * tok_rows]


def exchange(rows):
    axes = ("row", "col")
    peers = lax.axis_size(axes)
    cut = rows.reshape(peers, rows.shape[0] // peers, rows.shape[1])
    return lax.all_to_all(cut, axes, split_axis=0, concat_axis=0, tiled=True).reshape(rows.shape)


def in_hbm(array):
    return pltpu.with_memory_space_constraint(array, pltpu.HBM)


def in_vmem(array):
    return pltpu.with_memory_space_constraint(array, pltpu.VMEM)


def held(rows, columns, kind=jnp.bfloat16):
    return pltpu.VMEM((rows, columns), kind)


def shards(tokens, out_grad, expert_ids, gates, up_weight, down_weight):
    tok_rows, features = tokens.shape
    top_count = expert_ids.shape[1]
    units = up_weight.shape[2]
    peers = lax.axis_size(("row", "col"))
    capacity = 3 * tok_rows * top_count // (2 * peers)
    slots, rows, width = peers * capacity, peers * PAIR * capacity, features // PAIR
    tile = min(units, TILE // 2)
    steps = units // tile
    bf16, f32 = jnp.bfloat16, jnp.float32
    shape = jax.ShapeDtypeStruct
    dma = pltpu.SemaphoreType.DMA
    flops = 2 * slots * features * units
    weight_bytes = 2 * features * units

    def cost(matmuls, weights):
        return pl.CostEstimate(flops=matmuls * flops, bytes_accessed=weights * weight_bytes, transcendentals=0)

    ids = expert_ids.T
    hbm = pl.BlockSpec(memory_space=pltpu.HBM)
    vmem = pl.BlockSpec(memory_space=pltpu.VMEM)
    anywhere = pl.BlockSpec(memory_space=pl.ANY)
    tiles = unit_tiles(units)

    size = tiles[0][1]
    weights = in_hbm(up_weight[0]), in_hbm(down_weight[0])
    sent, first_up = pl.pallas_call(
        functools.partial(dispatch_kernel, capacity),
        out_shape=(
            shape((rows, features), bf16),
            pltpu.VMEM((features, size), bf16),
        ),
        in_specs=[hbm, hbm, hbm, hbm, hbm],
        scratch_shapes=[
            held(top_count, tok_rows, jnp.int32),
            held(top_count, tok_rows, f32),
            held(2 * tok_rows, features),
            dma((5,)),
        ],
        compiler_params=params(),
        name="dispatch",
    )(*[in_hbm(array) for array in (ids, gates.T, tokens, out_grad)], weights[0])
    landed = exchange(sent)

    hidden, grads, back = pl.pallas_call(
        functools.partial(expert_kernel, capacity),
        out_shape=(
            pltpu.HBM((slots, units), bf16),
            pltpu.HBM((slots, features), bf16),
            pltpu.HBM((rows, width), bf16),
        ),
        in_specs=[vmem, vmem, hbm, hbm],
        out_specs=(hbm, hbm, hbm),
        scratch_shapes=[
            held(features, units),
            held(units, features),
            held(slots, features),
            held(slots, features),
            held(slots, units),
            pltpu.VMEM((2, slots, tiles[0][1]), bf16),
            held(slots, features, f32),
            held(rows, width),
            dma((2, len(tiles))),
            dma((len(tiles),)),
            dma((1,)),
            dma((peers // group_size(peers, capacity),)),
        ],
        compiler_params=params(),
        cost_estimate=cost(3, 2),
        name="expert",
    )(landed, in_vmem(first_up), *weights)
    returned = exchange(back)

    down_grad = pl.pallas_call(
        down_grad_kernel,
        out_shape=shape((1, units, features), bf16),
        grid=(steps,),
        in_specs=[pl.BlockSpec((slots, features), lambda i: (0, 0)), pl.BlockSpec((slots, tile), lambda i: (0, i))],
        out_specs=pl.BlockSpec((None, tile, features), lambda i: (0, i, 0)),
        compiler_params=params(),
        cost_estimate=cost(1, 1),
        name="down_grad",
    )(in_hbm(grads), in_hbm(hidden))

    pick_map = pl.pallas_call(
        functools.partial(pick_map_kernel, capacity),
        out_shape=shape((PAIR * tok_rows, rows), bf16),
        in_specs=[vmem, anywhere],
        compiler_params=params(),
        name="pick_map",
    )(ids, in_hbm(grads))
    input_grad = pl.pallas_call(
        pick_kernel,
        out_shape=shape((tok_rows, features), bf16),
        compiler_params=params(),
        name="pick",
    )(pick_map, returned)
    return input_grad, down_grad


def pooled_shards(tokens, out_grad, expert_ids, gates, up_weight, down_weight):
    tok_rows = tokens.shape[0]
    top_count = expert_ids.shape[1]
    features = tokens.shape[1]
    groups = lax.axis_size("row")
    col_count = lax.axis_size("col")
    experts = groups * col_count
    capacity = 3 * tok_rows * top_count // (2 * experts)
    flat_ids = expert_ids.reshape(-1)
    onehot = (flat_ids[:, None] == jnp.arange(experts, dtype=jnp.int32)[None, :]).astype(jnp.int32)
    earlier = jnp.cumsum(onehot, axis=0) - onehot
    slot_index = jnp.sum(earlier * onehot, axis=1)
    target = flat_ids * capacity + slot_index
    placer = (jnp.arange(experts * capacity, dtype=jnp.int32)[:, None] == target[None, :]).astype(
        jnp.bfloat16
    )
    token_rows = jnp.repeat(tokens, top_count, axis=0)
    weighted = (
        gates.reshape(-1)[:, None] * jnp.repeat(out_grad, top_count, axis=0).astype(jnp.float32)
    ).astype(jnp.bfloat16)
    send_inputs = jnp.dot(placer, token_rows, preferred_element_type=jnp.float32).astype(
        jnp.bfloat16
    )
    send_grads = jnp.dot(placer, weighted, preferred_element_type=jnp.float32).astype(jnp.bfloat16)
    landed_inputs, landed_grads = (
        lax.all_to_all(
            send_inputs.reshape(experts, capacity, features),
            ("row", "col"),
            split_axis=0,
            concat_axis=0,
            tiled=True,
        ),
        lax.all_to_all(
            send_grads.reshape(experts, capacity, features),
            ("row", "col"),
            split_axis=0,
            concat_axis=0,
            tiled=True,
        ),
    )
    pooled_inputs, pooled_grads = (
        lax.all_gather(landed_inputs, "rep", axis=0, tiled=True),
        lax.all_gather(landed_grads, "rep", axis=0, tiled=True),
    )
    slot_rows = pooled_inputs.shape[0] * capacity
    input_rows = pooled_inputs.reshape(slot_rows, features)
    grad_rows = pooled_grads.reshape(slot_rows, features)
    up_block = up_weight[0]
    down_block = down_weight[0]
    preact = jnp.dot(input_rows, up_block, preferred_element_type=jnp.float32)
    hidden = jnp.maximum(preact, 0.0).astype(jnp.bfloat16)
    hidden_grad = lax.dot_general(
        grad_rows, down_block, (((1,), (1,)), ((), ())), preferred_element_type=jnp.float32
    )
    preact_grad = jnp.where(preact > 0, hidden_grad, 0.0).astype(jnp.bfloat16)
    weight_grad = lax.dot_general(
        hidden, grad_rows, (((0,), (0,)), ((), ())), preferred_element_type=jnp.float32
    )
    down_grad = weight_grad.astype(jnp.bfloat16)[None]
    summed_rows = lax.psum_scatter(
        lax.dot_general(
            preact_grad, up_block, (((1,), (1,)), ((), ())), preferred_element_type=jnp.float32
        ).astype(jnp.bfloat16),
        "rep",
        scatter_dimension=0,
        tiled=True,
    )
    returned = lax.all_to_all(
        summed_rows.reshape(experts, capacity, features),
        ("row", "col"),
        split_axis=0,
        concat_axis=0,
        tiled=True,
    )
    returned = returned.reshape(experts * capacity, features)
    picked = lax.dot_general(
        placer, returned, (((0,), (0,)), ((), ())), preferred_element_type=jnp.float32
    )
    input_grad = jnp.sum(picked.reshape(tok_rows, top_count, features), axis=1).astype(jnp.bfloat16)
    return (input_grad, down_grad)


def solution(mesh):
    by_token = P(("rep", "row", "col"), None)
    by_expert = (P(("row", "col"), None, "rep"), P(("row", "col"), "rep", None))
    return jax.shard_map(
        shards if mesh.shape["rep"] == 1 else pooled_shards,
        mesh=mesh,
        in_specs=(by_token,) * 4 + by_expert,
        out_specs=(by_token, by_expert[1]),
        check_vma=False,
    )
```

```python
import functools

import jax
import jax.numpy as jnp
from jax import lax
from jax.experimental import pallas as pl
from jax.experimental.pallas import tpu as pltpu
from jax.sharding import PartitionSpec as P

VMEM_LIMIT = 44 * 1024 * 1024
PAIR = 2
TILE = 1024
NOWHERE = -(1 << 20)


def f32_dot(lhs, rhs, contract=((1,), (0,))):
    return lax.dot_general(lhs, rhs, (contract, ((), ())), preferred_element_type=jnp.float32)


def params():
    return pltpu.CompilerParams(vmem_limit_bytes=VMEM_LIMIT)


def row_places(ids, experts, capacity):
    tok_rows = ids.shape[1]
    names = lax.broadcasted_iota(jnp.int32, (experts, tok_rows), 0)
    chosen = [names == ids[k : k + 1, :] for k in range(ids.shape[0])]
    member = functools.reduce(jnp.logical_or, chosen).astype(jnp.bfloat16)
    before = (
        lax.broadcasted_iota(jnp.int32, (tok_rows, tok_rows), 0)
        < lax.broadcasted_iota(jnp.int32, (tok_rows, tok_rows), 1)
    ).astype(jnp.bfloat16)
    rank = f32_dot(member, before).astype(jnp.int32)
    place = names * (PAIR * capacity) + rank
    return [jnp.sum(jnp.where(pick, place, 0), axis=0, keepdims=True) for pick in chosen]


def hits_at(rows, places):
    at = lax.broadcasted_iota(jnp.int32, (rows, places[0].shape[1]), 0)
    return [at == place for place in places]


def either(hits):
    return functools.reduce(jnp.logical_or, hits).astype(jnp.bfloat16)


def started(pairs, sems):
    copies = [pltpu.make_async_copy(*pair, sems.at[i]) for i, pair in enumerate(pairs)]
    for copy in copies:
        copy.start()
    return copies


def dispatch_kernel(capacity, *refs):
    sources, (up_ref, down_ref, out_ref, up_out, down_out, ids_ref, gates_ref, both_ref, sems) = refs[:4], refs[4:]
    tok_rows = both_ref.shape[0] // 2
    targets = ids_ref, gates_ref, both_ref.at[pl.ds(0, tok_rows)], both_ref.at[pl.ds(tok_rows, tok_rows)]
    ids_copy, gates_copy, tokens_copy, grad_copy = started(zip(sources, targets), sems)
    first = pl.ds(0, down_out.shape[0])
    weights = (up_ref.at[:, first], up_out), (down_ref.at[first], down_out)
    weight_copies = started(weights, sems.at[pl.ds(4, 2)])
    rows = out_ref.shape[0]
    ids_copy.wait()
    places = row_places(ids_ref[...], rows // (PAIR * capacity), capacity)
    token_hits = hits_at(rows, places)
    grad_hits = hits_at(rows, [place + capacity for place in places])
    gates_copy.wait()
    scales = [jnp.where(hit, 1.0, 0.0) for hit in token_hits]
    scales += [jnp.where(hit, gates_ref[k : k + 1, :], 0.0) for k, hit in enumerate(grad_hits)]
    scale = jnp.sum(sum(scales), axis=1, keepdims=True)
    gather = jnp.concatenate([either(token_hits), either(grad_hits)], axis=1)
    tokens_copy.wait()
    grad_copy.wait()
    out_ref[...] = (scale * f32_dot(gather, both_ref[...])).astype(jnp.bfloat16)
    for copy in weight_copies:
        copy.wait()


def paired_rows(number, capacity):
    owner = jnp.floor((number.astype(jnp.float32) + 0.5) * (1.0 / capacity)).astype(jnp.int32)
    return number + owner * ((PAIR - 1) * capacity)


def group_size(peers, capacity):
    size = 1
    while peers % (2 * size) == 0 and size * PAIR * capacity < 192:
        size *= 2
    return size


def take_apart(landed_ref, capacity, rows_ref, grads_ref):
    size = group_size(landed_ref.shape[0] // (PAIR * capacity), capacity)
    slots, rows = size * capacity, size * PAIR * capacity
    at = lax.broadcasted_iota(jnp.int32, (slots, rows), 1)
    source = paired_rows(lax.broadcasted_iota(jnp.int32, (slots, 1), 0), capacity)
    mover = jnp.concatenate([(at == source + j * capacity).astype(jnp.bfloat16) for j in range(PAIR)], axis=0)
    for i in range(rows_ref.shape[0] // slots):
        taken = f32_dot(mover, landed_ref[i * rows : (i + 1) * rows, :]).astype(jnp.bfloat16)
        rows_ref[i * slots : (i + 1) * slots, :] = taken[:slots]
        grads_ref[i * slots : (i + 1) * slots, :] = taken[slots:]


def fold_rows(plain_ref, capacity, folded_ref, out_ref, sems):
    size = group_size(plain_ref.shape[0] // capacity, capacity)
    slots, rows = size * capacity, size * PAIR * capacity
    width = folded_ref.shape[1]
    at = lax.broadcasted_iota(jnp.int32, (rows, slots), 0)
    target = paired_rows(lax.broadcasted_iota(jnp.int32, (1, slots), 1), capacity)
    mover = jnp.concatenate([(at == target + j * capacity).astype(jnp.bfloat16) for j in range(PAIR)], axis=1)
    copies = []
    for i in range(plain_ref.shape[0] // slots):
        plain = plain_ref[i * slots : (i + 1) * slots, :].astype(jnp.bfloat16)
        halves = jnp.concatenate([plain[:, j * width : (j + 1) * width] for j in range(PAIR)], axis=0)
        part = slice(i * rows, (i + 1) * rows)
        folded_ref[part, :] = f32_dot(mover, halves).astype(jnp.bfloat16)
        copies.append(pltpu.make_async_copy(folded_ref.at[part], out_ref.at[part], sems.at[i]))
        copies[-1].start()
    return copies


def unit_tiles(units):
    if units % (4 * TILE):
        return [(0, units)]
    sizes = [units // 4, units // 4, units // 2]
    return [(sum(sizes[:i]), size) for i, size in enumerate(sizes)]


def expert_kernel(
    capacity, landed_ref, first_up, first_down, up_ref, down_ref, hidden_out, grads_out, back_out, *scratch
):
    up, down, rows, grads, hidden, masked, total, back, weight_sems, hidden_sems, grads_sem, back_sems = scratch
    tiles = unit_tiles(up.shape[1])

    def weight_copies(i):
        at = pl.ds(*tiles[i])
        return [
            pltpu.make_async_copy(up_ref.at[:, at], up.at[:, at], weight_sems.at[0, i]),
            pltpu.make_async_copy(down_ref.at[at], down.at[at], weight_sems.at[1, i]),
        ]

    def start_weights(i):
        if i < len(tiles):
            arriving[i] = weight_copies(i)
            for copy in arriving[i]:
                copy.start()

    def add_row_grad(i):
        start, size = tiles[i]
        weights = up[:, start : start + size] if i else first_up[...]
        part = f32_dot(masked[i % 2, :, :size], weights, ((1,), (1,)))
        total[...] = part if i == 0 else total[...] + part

    arriving, leaving = {}, []
    for i in range(1, len(tiles)):
        start_weights(i)
    take_apart(landed_ref, capacity, rows, grads)
    leaving.append(pltpu.make_async_copy(grads, grads_out, grads_sem.at[0]))
    leaving[-1].start()
    for i, (start, size) in enumerate(tiles):
        here = slice(start, start + size)
        for copy in arriving.get(i, ()):
            copy.wait()
        preact = f32_dot(rows[...], up[:, here] if i else first_up[...])
        hidden_grad = f32_dot(grads[...], down[here, :] if i else first_down[...], ((1,), (1,)))
        if i:
            add_row_grad(i - 1)
        hidden[:, here] = jnp.maximum(preact, 0.0).astype(jnp.bfloat16)
        masked[i % 2, :, :size] = jnp.where(preact > 0, hidden_grad, 0.0).astype(jnp.bfloat16)
        leaving.append(pltpu.make_async_copy(hidden.at[:, here], hidden_out.at[:, here], hidden_sems.at[i]))
        leaving[-1].start()
    add_row_grad(len(tiles) - 1)
    for copy in leaving + fold_rows(total, capacity, back, back_out, back_sems):
        copy.wait()


def down_grad_kernel(grads_ref, hidden_ref, out_ref):
    out_ref[...] = f32_dot(hidden_ref[...], grads_ref[...], ((0,), (0,))).astype(jnp.bfloat16)


def pick_map_kernel(capacity, ids_ref, after_ref, out_ref):
    tok_rows, rows = ids_ref.shape[1], out_ref.shape[1]
    places = row_places(ids_ref[...], rows // (PAIR * capacity), capacity)
    for j in range(PAIR):
        chosen = either(hits_at(rows, [place + j * capacity for place in places]))
        out_ref[j * tok_rows : (j + 1) * tok_rows, :] = chosen.T


def pick_kernel(map_ref, returned_ref, out_ref):
    tok_rows, width = out_ref.shape[0], returned_ref.shape[1]
    picked = f32_dot(map_ref[...], returned_ref[...]).astype(jnp.bfloat16)
    for j in range(PAIR):
        out_ref[:, j * width : (j + 1) * width] = picked[j * tok_rows : (j + 1) * tok_rows]


def exchange(rows):
    axes = ("row", "col")
    peers = lax.axis_size(axes)
    cut = rows.reshape(peers, rows.shape[0] // peers, rows.shape[1])
    return lax.all_to_all(cut, axes, split_axis=0, concat_axis=0, tiled=True).reshape(rows.shape)


def in_hbm(array):
    return pltpu.with_memory_space_constraint(array, pltpu.HBM)


def in_vmem(array):
    return pltpu.with_memory_space_constraint(array, pltpu.VMEM)


def held(rows, columns, kind=jnp.bfloat16):
    return pltpu.VMEM((rows, columns), kind)


def shards(tokens, out_grad, expert_ids, gates, up_weight, down_weight):
    tok_rows, features = tokens.shape
    top_count = expert_ids.shape[1]
    units = up_weight.shape[2]
    peers = lax.axis_size(("row", "col"))
    capacity = 3 * tok_rows * top_count // (2 * peers)
    slots, rows, width = peers * capacity, peers * PAIR * capacity, features // PAIR
    tile = min(units, TILE // 2)
    steps = units // tile
    bf16, f32 = jnp.bfloat16, jnp.float32
    shape = jax.ShapeDtypeStruct
    dma = pltpu.SemaphoreType.DMA
    flops = 2 * slots * features * units
    weight_bytes = 2 * features * units

    def cost(matmuls, weights):
        return pl.CostEstimate(flops=matmuls * flops, bytes_accessed=weights * weight_bytes, transcendentals=0)

    ids = expert_ids.T
    hbm = pl.BlockSpec(memory_space=pltpu.HBM)
    vmem = pl.BlockSpec(memory_space=pltpu.VMEM)
    anywhere = pl.BlockSpec(memory_space=pl.ANY)
    tiles = unit_tiles(units)

    size = tiles[0][1]
    weights = in_hbm(up_weight[0]), in_hbm(down_weight[0])
    sent, first_up, first_down = pl.pallas_call(
        functools.partial(dispatch_kernel, capacity),
        out_shape=(
            shape((rows, features), bf16),
            pltpu.VMEM((features, size), bf16),
            pltpu.VMEM((size, features), bf16),
        ),
        in_specs=[hbm, hbm, hbm, hbm, hbm, hbm],
        scratch_shapes=[
            held(top_count, tok_rows, jnp.int32),
            held(top_count, tok_rows, f32),
            held(2 * tok_rows, features),
            dma((6,)),
        ],
        compiler_params=params(),
        name="dispatch",
    )(*[in_hbm(array) for array in (ids, gates.T, tokens, out_grad)], *weights)
    landed = exchange(sent)

    hidden, grads, back = pl.pallas_call(
        functools.partial(expert_kernel, capacity),
        out_shape=(
            pltpu.HBM((slots, units), bf16),
            pltpu.HBM((slots, features), bf16),
            pltpu.HBM((rows, width), bf16),
        ),
        in_specs=[vmem, vmem, vmem, hbm, hbm],
        out_specs=(hbm, hbm, hbm),
        scratch_shapes=[
            held(features, units),
            held(units, features),
            held(slots, features),
            held(slots, features),
            held(slots, units),
            pltpu.VMEM((2, slots, tiles[-1][1]), bf16),
            held(slots, features, f32),
            held(rows, width),
            dma((2, len(tiles))),
            dma((len(tiles),)),
            dma((1,)),
            dma((peers // group_size(peers, capacity),)),
        ],
        compiler_params=params(),
        cost_estimate=cost(3, 2),
        name="expert",
    )(landed, in_vmem(first_up), in_vmem(first_down), *weights)
    returned = exchange(back)

    down_grad = pl.pallas_call(
        down_grad_kernel,
        out_shape=shape((1, units, features), bf16),
        grid=(steps,),
        in_specs=[pl.BlockSpec((slots, features), lambda i: (0, 0)), pl.BlockSpec((slots, tile), lambda i: (0, i))],
        out_specs=pl.BlockSpec((None, tile, features), lambda i: (0, i, 0)),
        compiler_params=params(),
        cost_estimate=cost(1, 1),
        name="down_grad",
    )(in_hbm(grads), in_hbm(hidden))

    pick_map = pl.pallas_call(
        functools.partial(pick_map_kernel, capacity),
        out_shape=shape((PAIR * tok_rows, rows), bf16),
        in_specs=[vmem, anywhere],
        compiler_params=params(),
        name="pick_map",
    )(ids, in_hbm(grads))
    input_grad = pl.pallas_call(
        pick_kernel,
        out_shape=shape((tok_rows, features), bf16),
        compiler_params=params(),
        name="pick",
    )(pick_map, returned)
    return input_grad, down_grad


def pooled_shards(tokens, out_grad, expert_ids, gates, up_weight, down_weight):
    tok_rows = tokens.shape[0]
    top_count = expert_ids.shape[1]
    features = tokens.shape[1]
    groups = lax.axis_size("row")
    col_count = lax.axis_size("col")
    experts = groups * col_count
    capacity = 3 * tok_rows * top_count // (2 * experts)
    flat_ids = expert_ids.reshape(-1)
    onehot = (flat_ids[:, None] == jnp.arange(experts, dtype=jnp.int32)[None, :]).astype(jnp.int32)
    earlier = jnp.cumsum(onehot, axis=0) - onehot
    slot_index = jnp.sum(earlier * onehot, axis=1)
    target = flat_ids * capacity + slot_index
    placer = (jnp.arange(experts * capacity, dtype=jnp.int32)[:, None] == target[None, :]).astype(
        jnp.bfloat16
    )
    token_rows = jnp.repeat(tokens, top_count, axis=0)
    weighted = (
        gates.reshape(-1)[:, None] * jnp.repeat(out_grad, top_count, axis=0).astype(jnp.float32)
    ).astype(jnp.bfloat16)
    send_inputs = jnp.dot(placer, token_rows, preferred_element_type=jnp.float32).astype(
        jnp.bfloat16
    )
    send_grads = jnp.dot(placer, weighted, preferred_element_type=jnp.float32).astype(jnp.bfloat16)
    landed_inputs, landed_grads = (
        lax.all_to_all(
            send_inputs.reshape(experts, capacity, features),
            ("row", "col"),
            split_axis=0,
            concat_axis=0,
            tiled=True,
        ),
        lax.all_to_all(
            send_grads.reshape(experts, capacity, features),
            ("row", "col"),
            split_axis=0,
            concat_axis=0,
            tiled=True,
        ),
    )
    pooled_inputs, pooled_grads = (
        lax.all_gather(landed_inputs, "rep", axis=0, tiled=True),
        lax.all_gather(landed_grads, "rep", axis=0, tiled=True),
    )
    slot_rows = pooled_inputs.shape[0] * capacity
    input_rows = pooled_inputs.reshape(slot_rows, features)
    grad_rows = pooled_grads.reshape(slot_rows, features)
    up_block = up_weight[0]
    down_block = down_weight[0]
    preact = jnp.dot(input_rows, up_block, preferred_element_type=jnp.float32)
    hidden = jnp.maximum(preact, 0.0).astype(jnp.bfloat16)
    hidden_grad = lax.dot_general(
        grad_rows, down_block, (((1,), (1,)), ((), ())), preferred_element_type=jnp.float32
    )
    preact_grad = jnp.where(preact > 0, hidden_grad, 0.0).astype(jnp.bfloat16)
    weight_grad = lax.dot_general(
        hidden, grad_rows, (((0,), (0,)), ((), ())), preferred_element_type=jnp.float32
    )
    down_grad = weight_grad.astype(jnp.bfloat16)[None]
    summed_rows = lax.psum_scatter(
        lax.dot_general(
            preact_grad, up_block, (((1,), (1,)), ((), ())), preferred_element_type=jnp.float32
        ).astype(jnp.bfloat16),
        "rep",
        scatter_dimension=0,
        tiled=True,
    )
    returned = lax.all_to_all(
        summed_rows.reshape(experts, capacity, features),
        ("row", "col"),
        split_axis=0,
        concat_axis=0,
        tiled=True,
    )
    returned = returned.reshape(experts * capacity, features)
    picked = lax.dot_general(
        placer, returned, (((0,), (0,)), ((), ())), preferred_element_type=jnp.float32
    )
    input_grad = jnp.sum(picked.reshape(tok_rows, top_count, features), axis=1).astype(jnp.bfloat16)
    return (input_grad, down_grad)


def solution(mesh):
    by_token = P(("rep", "row", "col"), None)
    by_expert = (P(("row", "col"), None, "rep"), P(("row", "col"), "rep", None))
    return jax.shard_map(
        shards if mesh.shape["rep"] == 1 else pooled_shards,
        mesh=mesh,
        in_specs=(by_token,) * 4 + by_expert,
        out_specs=(by_token, by_expert[1]),
        check_vma=False,
    )
```

```python
import functools

import jax
import jax.numpy as jnp
from jax import lax
from jax.experimental import pallas as pl
from jax.experimental.pallas import tpu as pltpu
from jax.sharding import PartitionSpec as P

VMEM_LIMIT = 44 * 1024 * 1024
PAIR = 2
TILE = 1024
AHEAD = 2
PIECES = 4
NOWHERE = -(1 << 20)


def f32_dot(lhs, rhs, contract=((1,), (0,))):
    return lax.dot_general(lhs, rhs, (contract, ((), ())), preferred_element_type=jnp.float32)


def params():
    return pltpu.CompilerParams(vmem_limit_bytes=VMEM_LIMIT)


def row_places(ids, experts, capacity):
    tok_rows = ids.shape[1]
    names = lax.broadcasted_iota(jnp.int32, (experts, tok_rows), 0)
    chosen = [names == ids[k : k + 1, :] for k in range(ids.shape[0])]
    member = functools.reduce(jnp.logical_or, chosen).astype(jnp.bfloat16)
    before = (
        lax.broadcasted_iota(jnp.int32, (tok_rows, tok_rows), 0)
        < lax.broadcasted_iota(jnp.int32, (tok_rows, tok_rows), 1)
    ).astype(jnp.bfloat16)
    rank = f32_dot(member, before).astype(jnp.int32)
    place = names * (PAIR * capacity) + rank
    return [jnp.sum(jnp.where(pick, place, 0), axis=0, keepdims=True) for pick in chosen]


def hits_at(rows, places):
    at = lax.broadcasted_iota(jnp.int32, (rows, places[0].shape[1]), 0)
    return [at == place for place in places]


def either(hits):
    return functools.reduce(jnp.logical_or, hits).astype(jnp.bfloat16)


def started(pairs, sems):
    copies = [pltpu.make_async_copy(*pair, sems.at[i]) for i, pair in enumerate(pairs)]
    for copy in copies:
        copy.start()
    return copies


def dispatch_kernel(capacity, *refs):
    sources, (up_ref, down_ref, out_ref, up_out, down_out, ids_ref, gates_ref, both_ref, sems) = refs[:4], refs[4:]
    tok_rows = both_ref.shape[0] // 2
    targets = ids_ref, gates_ref, both_ref.at[pl.ds(0, tok_rows)], both_ref.at[pl.ds(tok_rows, tok_rows)]
    ids_copy, gates_copy, tokens_copy, grad_copy = started(zip(sources, targets), sems)
    first = pl.ds(0, down_out.shape[0])
    weights = (up_ref.at[:, first], up_out), (down_ref.at[first], down_out)
    weight_copies = started(weights, sems.at[pl.ds(4, 2)])
    rows = out_ref.shape[0]
    ids_copy.wait()
    places = row_places(ids_ref[...], rows // (PAIR * capacity), capacity)
    token_hits = hits_at(rows, places)
    grad_hits = hits_at(rows, [place + capacity for place in places])
    gates_copy.wait()
    scales = [jnp.where(hit, 1.0, 0.0) for hit in token_hits]
    scales += [jnp.where(hit, gates_ref[k : k + 1, :], 0.0) for k, hit in enumerate(grad_hits)]
    scale = jnp.sum(sum(scales), axis=1, keepdims=True)
    gather = jnp.concatenate([either(token_hits), either(grad_hits)], axis=1)
    tokens_copy.wait()
    grad_copy.wait()
    out_ref[...] = (scale * f32_dot(gather, both_ref[...])).astype(jnp.bfloat16)
    for copy in weight_copies:
        copy.wait()


def paired_rows(number, capacity):
    owner = jnp.floor((number.astype(jnp.float32) + 0.5) * (1.0 / capacity)).astype(jnp.int32)
    return number + owner * ((PAIR - 1) * capacity)


def group_size(peers, capacity):
    size = 1
    while peers % (2 * size) == 0 and size * PAIR * capacity < 192:
        size *= 2
    return size


def take_apart(landed_ref, capacity, rows_ref, grads_ref):
    size = group_size(landed_ref.shape[0] // (PAIR * capacity), capacity)
    slots, rows = size * capacity, size * PAIR * capacity
    at = lax.broadcasted_iota(jnp.int32, (slots, rows), 1)
    source = paired_rows(lax.broadcasted_iota(jnp.int32, (slots, 1), 0), capacity)
    mover = jnp.concatenate([(at == source + j * capacity).astype(jnp.bfloat16) for j in range(PAIR)], axis=0)
    for i in range(rows_ref.shape[0] // slots):
        taken = f32_dot(mover, landed_ref[i * rows : (i + 1) * rows, :]).astype(jnp.bfloat16)
        rows_ref[i * slots : (i + 1) * slots, :] = taken[:slots]
        grads_ref[i * slots : (i + 1) * slots, :] = taken[slots:]


def fold_rows(plain_ref, capacity, folded_ref, out_ref, sems):
    size = group_size(plain_ref.shape[0] // capacity, capacity)
    slots, rows = size * capacity, size * PAIR * capacity
    width = folded_ref.shape[1]
    at = lax.broadcasted_iota(jnp.int32, (rows, slots), 0)
    target = paired_rows(lax.broadcasted_iota(jnp.int32, (1, slots), 1), capacity)
    mover = jnp.concatenate([(at == target + j * capacity).astype(jnp.bfloat16) for j in range(PAIR)], axis=1)
    copies = []
    for i in range(plain_ref.shape[0] // slots):
        plain = plain_ref[i * slots : (i + 1) * slots, :].astype(jnp.bfloat16)
        halves = jnp.concatenate([plain[:, j * width : (j + 1) * width] for j in range(PAIR)], axis=0)
        part = slice(i * rows, (i + 1) * rows)
        folded_ref[part, :] = f32_dot(mover, halves).astype(jnp.bfloat16)
        copies.append(pltpu.make_async_copy(folded_ref.at[part], out_ref.at[part], sems.at[i]))
        copies[-1].start()
    return copies


def unit_tiles(units):
    size = min(units, TILE)
    return [(start, size) for start in range(0, units, size)]


def expert_kernel(
    capacity, landed_ref, first_up, first_down, up_ref, down_ref, hidden_out, grads_out, back_out, *scratch
):
    up, down, rows, grads, hidden, masked, total, back, weight_sems, hidden_sems, grads_sem, back_sems = scratch
    tiles = unit_tiles(up.shape[1])

    def weight_copies(i):
        start, size = tiles[i]
        copies = []
        for n in range(PIECES):
            part = pl.ds(n * (up.shape[0] // PIECES), up.shape[0] // PIECES), pl.ds(start, size)
            copies.append(pltpu.make_async_copy(up_ref.at[part], up.at[part], weight_sems.at[0, i, n]))
        for n in range(PIECES):
            part = pl.ds(start + n * (size // PIECES), size // PIECES)
            copies.append(pltpu.make_async_copy(down_ref.at[part], down.at[part], weight_sems.at[1, i, n]))
        return copies

    def start_weights(i):
        if i < len(tiles):
            arriving[i] = weight_copies(i)
            for copy in arriving[i]:
                copy.start()

    def add_row_grad(i):
        start, size = tiles[i]
        weights = up[:, start : start + size] if i else first_up[...]
        part = f32_dot(masked[i % 2, :, :size], weights, ((1,), (1,)))
        total[...] = part if i == 0 else total[...] + part

    arriving, leaving = {}, []
    for i in range(1, AHEAD):
        start_weights(i)
    take_apart(landed_ref, capacity, rows, grads)
    leaving.append(pltpu.make_async_copy(grads, grads_out, grads_sem.at[0]))
    leaving[-1].start()
    for i, (start, size) in enumerate(tiles):
        here = slice(start, start + size)
        start_weights(i + AHEAD)
        for copy in arriving.get(i, ()):
            copy.wait()
        preact = f32_dot(rows[...], up[:, here] if i else first_up[...])
        hidden_grad = f32_dot(grads[...], down[here, :] if i else first_down[...], ((1,), (1,)))
        if i:
            add_row_grad(i - 1)
        hidden[:, here] = jnp.maximum(preact, 0.0).astype(jnp.bfloat16)
        masked[i % 2, :, :size] = jnp.where(preact > 0, hidden_grad, 0.0).astype(jnp.bfloat16)
        leaving.append(pltpu.make_async_copy(hidden.at[:, here], hidden_out.at[:, here], hidden_sems.at[i]))
        leaving[-1].start()
    add_row_grad(len(tiles) - 1)
    for copy in leaving + fold_rows(total, capacity, back, back_out, back_sems):
        copy.wait()


def down_grad_kernel(grads_ref, hidden_ref, out_ref):
    out_ref[...] = f32_dot(hidden_ref[...], grads_ref[...], ((0,), (0,))).astype(jnp.bfloat16)


def pick_map_kernel(capacity, ids_ref, after_ref, out_ref):
    tok_rows, rows = ids_ref.shape[1], out_ref.shape[1]
    places = row_places(ids_ref[...], rows // (PAIR * capacity), capacity)
    for j in range(PAIR):
        chosen = either(hits_at(rows, [place + j * capacity for place in places]))
        out_ref[j * tok_rows : (j + 1) * tok_rows, :] = chosen.T


def pick_kernel(map_ref, returned_ref, out_ref):
    tok_rows, width = out_ref.shape[0], returned_ref.shape[1]
    picked = f32_dot(map_ref[...], returned_ref[...]).astype(jnp.bfloat16)
    for j in range(PAIR):
        out_ref[:, j * width : (j + 1) * width] = picked[j * tok_rows : (j + 1) * tok_rows]


def exchange(rows):
    axes = ("row", "col")
    peers = lax.axis_size(axes)
    cut = rows.reshape(peers, rows.shape[0] // peers, rows.shape[1])
    return lax.all_to_all(cut, axes, split_axis=0, concat_axis=0, tiled=True).reshape(rows.shape)


def in_hbm(array):
    return pltpu.with_memory_space_constraint(array, pltpu.HBM)


def in_vmem(array):
    return pltpu.with_memory_space_constraint(array, pltpu.VMEM)


def held(rows, columns, kind=jnp.bfloat16):
    return pltpu.VMEM((rows, columns), kind)


def shards(tokens, out_grad, expert_ids, gates, up_weight, down_weight):
    tok_rows, features = tokens.shape
    top_count = expert_ids.shape[1]
    units = up_weight.shape[2]
    peers = lax.axis_size(("row", "col"))
    capacity = 3 * tok_rows * top_count // (2 * peers)
    slots, rows, width = peers * capacity, peers * PAIR * capacity, features // PAIR
    tile = min(units, TILE // 2)
    steps = units // tile
    bf16, f32 = jnp.bfloat16, jnp.float32
    shape = jax.ShapeDtypeStruct
    dma = pltpu.SemaphoreType.DMA
    flops = 2 * slots * features * units
    weight_bytes = 2 * features * units

    def cost(matmuls, weights):
        return pl.CostEstimate(flops=matmuls * flops, bytes_accessed=weights * weight_bytes, transcendentals=0)

    ids = expert_ids.T
    hbm = pl.BlockSpec(memory_space=pltpu.HBM)
    vmem = pl.BlockSpec(memory_space=pltpu.VMEM)
    anywhere = pl.BlockSpec(memory_space=pl.ANY)
    tiles = unit_tiles(units)

    size = tiles[0][1]
    weights = in_hbm(up_weight[0]), in_hbm(down_weight[0])
    sent, first_up, first_down = pl.pallas_call(
        functools.partial(dispatch_kernel, capacity),
        out_shape=(
            shape((rows, features), bf16),
            pltpu.VMEM((features, size), bf16),
            pltpu.VMEM((size, features), bf16),
        ),
        in_specs=[hbm, hbm, hbm, hbm, hbm, hbm],
        scratch_shapes=[
            held(top_count, tok_rows, jnp.int32),
            held(top_count, tok_rows, f32),
            held(2 * tok_rows, features),
            dma((6,)),
        ],
        compiler_params=params(),
        name="dispatch",
    )(*[in_hbm(array) for array in (ids, gates.T, tokens, out_grad)], *weights)
    landed = exchange(sent)

    hidden, grads, back = pl.pallas_call(
        functools.partial(expert_kernel, capacity),
        out_shape=(
            pltpu.HBM((slots, units), bf16),
            pltpu.HBM((slots, features), bf16),
            pltpu.HBM((rows, width), bf16),
        ),
        in_specs=[vmem, vmem, vmem, hbm, hbm],
        out_specs=(hbm, hbm, hbm),
        scratch_shapes=[
            held(features, units),
            held(units, features),
            held(slots, features),
            held(slots, features),
            held(slots, units),
            pltpu.VMEM((2, slots, tiles[0][1]), bf16),
            held(slots, features, f32),
            held(rows, width),
            dma((2, len(tiles), PIECES)),
            dma((len(tiles),)),
            dma((1,)),
            dma((peers // group_size(peers, capacity),)),
        ],
        compiler_params=params(),
        cost_estimate=cost(3, 2),
        name="expert",
    )(landed, in_vmem(first_up), in_vmem(first_down), *weights)
    returned = exchange(back)

    down_grad = pl.pallas_call(
        down_grad_kernel,
        out_shape=shape((1, units, features), bf16),
        grid=(steps,),
        in_specs=[pl.BlockSpec((slots, features), lambda i: (0, 0)), pl.BlockSpec((slots, tile), lambda i: (0, i))],
        out_specs=pl.BlockSpec((None, tile, features), lambda i: (0, i, 0)),
        compiler_params=params(),
        cost_estimate=cost(1, 1),
        name="down_grad",
    )(in_hbm(grads), in_hbm(hidden))

    pick_map = pl.pallas_call(
        functools.partial(pick_map_kernel, capacity),
        out_shape=shape((PAIR * tok_rows, rows), bf16),
        in_specs=[vmem, anywhere],
        compiler_params=params(),
        name="pick_map",
    )(ids, in_hbm(grads))
    input_grad = pl.pallas_call(
        pick_kernel,
        out_shape=shape((tok_rows, features), bf16),
        compiler_params=params(),
        name="pick",
    )(pick_map, returned)
    return input_grad, down_grad


def pooled_shards(tokens, out_grad, expert_ids, gates, up_weight, down_weight):
    tok_rows = tokens.shape[0]
    top_count = expert_ids.shape[1]
    features = tokens.shape[1]
    groups = lax.axis_size("row")
    col_count = lax.axis_size("col")
    experts = groups * col_count
    capacity = 3 * tok_rows * top_count // (2 * experts)
    flat_ids = expert_ids.reshape(-1)
    onehot = (flat_ids[:, None] == jnp.arange(experts, dtype=jnp.int32)[None, :]).astype(jnp.int32)
    earlier = jnp.cumsum(onehot, axis=0) - onehot
    slot_index = jnp.sum(earlier * onehot, axis=1)
    target = flat_ids * capacity + slot_index
    placer = (jnp.arange(experts * capacity, dtype=jnp.int32)[:, None] == target[None, :]).astype(
        jnp.bfloat16
    )
    token_rows = jnp.repeat(tokens, top_count, axis=0)
    weighted = (
        gates.reshape(-1)[:, None] * jnp.repeat(out_grad, top_count, axis=0).astype(jnp.float32)
    ).astype(jnp.bfloat16)
    send_inputs = jnp.dot(placer, token_rows, preferred_element_type=jnp.float32).astype(
        jnp.bfloat16
    )
    send_grads = jnp.dot(placer, weighted, preferred_element_type=jnp.float32).astype(jnp.bfloat16)
    landed_inputs, landed_grads = (
        lax.all_to_all(
            send_inputs.reshape(experts, capacity, features),
            ("row", "col"),
            split_axis=0,
            concat_axis=0,
            tiled=True,
        ),
        lax.all_to_all(
            send_grads.reshape(experts, capacity, features),
            ("row", "col"),
            split_axis=0,
            concat_axis=0,
            tiled=True,
        ),
    )
    pooled_inputs, pooled_grads = (
        lax.all_gather(landed_inputs, "rep", axis=0, tiled=True),
        lax.all_gather(landed_grads, "rep", axis=0, tiled=True),
    )
    slot_rows = pooled_inputs.shape[0] * capacity
    input_rows = pooled_inputs.reshape(slot_rows, features)
    grad_rows = pooled_grads.reshape(slot_rows, features)
    up_block = up_weight[0]
    down_block = down_weight[0]
    preact = jnp.dot(input_rows, up_block, preferred_element_type=jnp.float32)
    hidden = jnp.maximum(preact, 0.0).astype(jnp.bfloat16)
    hidden_grad = lax.dot_general(
        grad_rows, down_block, (((1,), (1,)), ((), ())), preferred_element_type=jnp.float32
    )
    preact_grad = jnp.where(preact > 0, hidden_grad, 0.0).astype(jnp.bfloat16)
    weight_grad = lax.dot_general(
        hidden, grad_rows, (((0,), (0,)), ((), ())), preferred_element_type=jnp.float32
    )
    down_grad = weight_grad.astype(jnp.bfloat16)[None]
    summed_rows = lax.psum_scatter(
        lax.dot_general(
            preact_grad, up_block, (((1,), (1,)), ((), ())), preferred_element_type=jnp.float32
        ).astype(jnp.bfloat16),
        "rep",
        scatter_dimension=0,
        tiled=True,
    )
    returned = lax.all_to_all(
        summed_rows.reshape(experts, capacity, features),
        ("row", "col"),
        split_axis=0,
        concat_axis=0,
        tiled=True,
    )
    returned = returned.reshape(experts * capacity, features)
    picked = lax.dot_general(
        placer, returned, (((0,), (0,)), ((), ())), preferred_element_type=jnp.float32
    )
    input_grad = jnp.sum(picked.reshape(tok_rows, top_count, features), axis=1).astype(jnp.bfloat16)
    return (input_grad, down_grad)


def solution(mesh):
    by_token = P(("rep", "row", "col"), None)
    by_expert = (P(("row", "col"), None, "rep"), P(("row", "col"), "rep", None))
    return jax.shard_map(
        shards if mesh.shape["rep"] == 1 else pooled_shards,
        mesh=mesh,
        in_specs=(by_token,) * 4 + by_expert,
        out_specs=(by_token, by_expert[1]),
        check_vma=False,
    )
```

```python
import functools

import jax
import jax.numpy as jnp
from jax import lax
from jax.experimental import pallas as pl
from jax.experimental.pallas import tpu as pltpu
from jax.sharding import PartitionSpec as P

VMEM_LIMIT = 44 * 1024 * 1024
PAIR = 2
TILE = 1024
NOWHERE = -(1 << 20)


def f32_dot(lhs, rhs, contract=((1,), (0,))):
    return lax.dot_general(lhs, rhs, (contract, ((), ())), preferred_element_type=jnp.float32)


def params():
    return pltpu.CompilerParams(vmem_limit_bytes=VMEM_LIMIT)


def row_places(ids, experts, capacity):
    tok_rows = ids.shape[1]
    names = lax.broadcasted_iota(jnp.int32, (experts, tok_rows), 0)
    chosen = [names == ids[k : k + 1, :] for k in range(ids.shape[0])]
    member = functools.reduce(jnp.logical_or, chosen).astype(jnp.bfloat16)
    before = (
        lax.broadcasted_iota(jnp.int32, (tok_rows, tok_rows), 0)
        < lax.broadcasted_iota(jnp.int32, (tok_rows, tok_rows), 1)
    ).astype(jnp.bfloat16)
    rank = f32_dot(member, before).astype(jnp.int32)
    place = names * (PAIR * capacity) + rank
    return [jnp.sum(jnp.where(pick, place, 0), axis=0, keepdims=True) for pick in chosen]


def hits_at(rows, places):
    at = lax.broadcasted_iota(jnp.int32, (rows, places[0].shape[1]), 0)
    return [at == place for place in places]


def either(hits):
    return functools.reduce(jnp.logical_or, hits).astype(jnp.bfloat16)


def started(pairs, sems):
    copies = [pltpu.make_async_copy(*pair, sems.at[i]) for i, pair in enumerate(pairs)]
    for copy in copies:
        copy.start()
    return copies


def dispatch_kernel(capacity, *refs):
    sources, (up_ref, down_ref, out_ref, up_out, down_out, ids_ref, gates_ref, both_ref, sems) = refs[:4], refs[4:]
    tok_rows = both_ref.shape[0] // 2
    targets = ids_ref, gates_ref, both_ref.at[pl.ds(0, tok_rows)], both_ref.at[pl.ds(tok_rows, tok_rows)]
    ids_copy, gates_copy, tokens_copy, grad_copy = started(zip(sources, targets), sems)
    first = pl.ds(0, down_out.shape[0])
    weights = (up_ref.at[:, first], up_out), (down_ref.at[first], down_out)
    weight_copies = started(weights, sems.at[pl.ds(4, 2)])
    rows = out_ref.shape[0]
    ids_copy.wait()
    places = row_places(ids_ref[...], rows // (PAIR * capacity), capacity)
    token_hits = hits_at(rows, places)
    grad_hits = hits_at(rows, [place + capacity for place in places])
    gates_copy.wait()
    scales = [jnp.where(hit, 1.0, 0.0) for hit in token_hits]
    scales += [jnp.where(hit, gates_ref[k : k + 1, :], 0.0) for k, hit in enumerate(grad_hits)]
    scale = jnp.sum(sum(scales), axis=1, keepdims=True)
    gather = jnp.concatenate([either(token_hits), either(grad_hits)], axis=1)
    tokens_copy.wait()
    grad_copy.wait()
    out_ref[...] = (scale * f32_dot(gather, both_ref[...])).astype(jnp.bfloat16)
    for copy in weight_copies:
        copy.wait()


def paired_rows(number, capacity):
    owner = jnp.floor((number.astype(jnp.float32) + 0.5) * (1.0 / capacity)).astype(jnp.int32)
    return number + owner * ((PAIR - 1) * capacity)


def group_size(peers, capacity):
    size = 1
    while peers % (2 * size) == 0 and size * PAIR * capacity < 192:
        size *= 2
    return size


def take_apart(landed_ref, capacity, rows_ref, grads_ref):
    size = group_size(landed_ref.shape[0] // (PAIR * capacity), capacity)
    slots, rows = size * capacity, size * PAIR * capacity
    at = lax.broadcasted_iota(jnp.int32, (slots, rows), 1)
    source = paired_rows(lax.broadcasted_iota(jnp.int32, (slots, 1), 0), capacity)
    mover = jnp.concatenate([(at == source + j * capacity).astype(jnp.bfloat16) for j in range(PAIR)], axis=0)
    for i in range(rows_ref.shape[0] // slots):
        taken = f32_dot(mover, landed_ref[i * rows : (i + 1) * rows, :]).astype(jnp.bfloat16)
        rows_ref[i * slots : (i + 1) * slots, :] = taken[:slots]
        grads_ref[i * slots : (i + 1) * slots, :] = taken[slots:]


def fold_rows(plain_ref, capacity, folded_ref, out_ref, sems):
    size = group_size(plain_ref.shape[0] // capacity, capacity)
    slots, rows = size * capacity, size * PAIR * capacity
    width = folded_ref.shape[1]
    at = lax.broadcasted_iota(jnp.int32, (rows, slots), 0)
    target = paired_rows(lax.broadcasted_iota(jnp.int32, (1, slots), 1), capacity)
    mover = jnp.concatenate([(at == target + j * capacity).astype(jnp.bfloat16) for j in range(PAIR)], axis=1)
    copies = []
    for i in range(plain_ref.shape[0] // slots):
        plain = plain_ref[i * slots : (i + 1) * slots, :].astype(jnp.bfloat16)
        halves = jnp.concatenate([plain[:, j * width : (j + 1) * width] for j in range(PAIR)], axis=0)
        part = slice(i * rows, (i + 1) * rows)
        folded_ref[part, :] = f32_dot(mover, halves).astype(jnp.bfloat16)
        copies.append(pltpu.make_async_copy(folded_ref.at[part], out_ref.at[part], sems.at[i]))
        copies[-1].start()
    return copies


def unit_tiles(units):
    size = min(units, TILE)
    return [(start, size) for start in range(0, units, size)]


def expert_kernel(
    capacity, landed_ref, first_up, first_down, up_ref, down_ref, hidden_out, grads_out, back_out, *scratch
):
    up, down, rows, grads, hidden, masked, total, back, weight_sems, hidden_sems, grads_sem, back_sems = scratch
    tiles = unit_tiles(up.shape[1])

    def weight_copies(i):
        at = pl.ds(*tiles[i])
        return [
            pltpu.make_async_copy(up_ref.at[:, at], up.at[:, at], weight_sems.at[0, i]),
            pltpu.make_async_copy(down_ref.at[at], down.at[at], weight_sems.at[1, i]),
        ]

    def start_weights(i):
        if i < len(tiles):
            arriving[i] = weight_copies(i)
            for copy in arriving[i]:
                copy.start()

    def add_row_grad(i):
        start, size = tiles[i]
        weights = up[:, start : start + size] if i else first_up[...]
        part = f32_dot(masked[i % 2, :, :size], weights, ((1,), (1,)))
        total[...] = part if i == 0 else total[...] + part

    arriving, leaving = {}, []
    start_weights(1)
    take_apart(landed_ref, capacity, rows, grads)
    leaving.append(pltpu.make_async_copy(grads, grads_out, grads_sem.at[0]))
    leaving[-1].start()
    for i, (start, size) in enumerate(tiles):
        here = slice(start, start + size)
        for copy in arriving.get(i, ()):
            copy.wait()
        if i:
            start_weights(i + 1)
        preact = f32_dot(rows[...], up[:, here] if i else first_up[...])
        hidden_grad = f32_dot(grads[...], down[here, :] if i else first_down[...], ((1,), (1,)))
        if i:
            add_row_grad(i - 1)
        hidden[:, here] = jnp.maximum(preact, 0.0).astype(jnp.bfloat16)
        masked[i % 2, :, :size] = jnp.where(preact > 0, hidden_grad, 0.0).astype(jnp.bfloat16)
        leaving.append(pltpu.make_async_copy(hidden.at[:, here], hidden_out.at[:, here], hidden_sems.at[i]))
        leaving[-1].start()
    add_row_grad(len(tiles) - 1)
    for copy in leaving + fold_rows(total, capacity, back, back_out, back_sems):
        copy.wait()


def down_grad_kernel(grads_ref, hidden_ref, out_ref):
    out_ref[...] = f32_dot(hidden_ref[...], grads_ref[...], ((0,), (0,))).astype(jnp.bfloat16)


def pick_map_kernel(capacity, ids_ref, after_ref, out_ref):
    tok_rows, rows = ids_ref.shape[1], out_ref.shape[1]
    places = row_places(ids_ref[...], rows // (PAIR * capacity), capacity)
    for j in range(PAIR):
        chosen = either(hits_at(rows, [place + j * capacity for place in places]))
        out_ref[j * tok_rows : (j + 1) * tok_rows, :] = chosen.T


def pick_kernel(map_ref, returned_ref, out_ref):
    tok_rows, width = out_ref.shape[0], returned_ref.shape[1]
    picked = f32_dot(map_ref[...], returned_ref[...]).astype(jnp.bfloat16)
    for j in range(PAIR):
        out_ref[:, j * width : (j + 1) * width] = picked[j * tok_rows : (j + 1) * tok_rows]


def exchange(rows):
    axes = ("row", "col")
    peers = lax.axis_size(axes)
    cut = rows.reshape(peers, rows.shape[0] // peers, rows.shape[1])
    return lax.all_to_all(cut, axes, split_axis=0, concat_axis=0, tiled=True).reshape(rows.shape)


def in_hbm(array):
    return pltpu.with_memory_space_constraint(array, pltpu.HBM)


def in_vmem(array):
    return pltpu.with_memory_space_constraint(array, pltpu.VMEM)


def held(rows, columns, kind=jnp.bfloat16):
    return pltpu.VMEM((rows, columns), kind)


def shards(tokens, out_grad, expert_ids, gates, up_weight, down_weight):
    tok_rows, features = tokens.shape
    top_count = expert_ids.shape[1]
    units = up_weight.shape[2]
    peers = lax.axis_size(("row", "col"))
    capacity = 3 * tok_rows * top_count // (2 * peers)
    slots, rows, width = peers * capacity, peers * PAIR * capacity, features // PAIR
    tile = min(units, TILE // 2)
    steps = units // tile
    bf16, f32 = jnp.bfloat16, jnp.float32
    shape = jax.ShapeDtypeStruct
    dma = pltpu.SemaphoreType.DMA
    flops = 2 * slots * features * units
    weight_bytes = 2 * features * units

    def cost(matmuls, weights):
        return pl.CostEstimate(flops=matmuls * flops, bytes_accessed=weights * weight_bytes, transcendentals=0)

    ids = expert_ids.T
    hbm = pl.BlockSpec(memory_space=pltpu.HBM)
    vmem = pl.BlockSpec(memory_space=pltpu.VMEM)
    anywhere = pl.BlockSpec(memory_space=pl.ANY)
    tiles = unit_tiles(units)

    size = tiles[0][1]
    weights = in_hbm(up_weight[0]), in_hbm(down_weight[0])
    sent, first_up, first_down = pl.pallas_call(
        functools.partial(dispatch_kernel, capacity),
        out_shape=(
            shape((rows, features), bf16),
            pltpu.VMEM((features, size), bf16),
            pltpu.VMEM((size, features), bf16),
        ),
        in_specs=[hbm, hbm, hbm, hbm, hbm, hbm],
        scratch_shapes=[
            held(top_count, tok_rows, jnp.int32),
            held(top_count, tok_rows, f32),
            held(2 * tok_rows, features),
            dma((6,)),
        ],
        compiler_params=params(),
        name="dispatch",
    )(*[in_hbm(array) for array in (ids, gates.T, tokens, out_grad)], *weights)
    landed = exchange(sent)

    hidden, grads, back = pl.pallas_call(
        functools.partial(expert_kernel, capacity),
        out_shape=(
            pltpu.HBM((slots, units), bf16),
            pltpu.HBM((slots, features), bf16),
            pltpu.HBM((rows, width), bf16),
        ),
        in_specs=[vmem, vmem, vmem, hbm, hbm],
        out_specs=(hbm, hbm, hbm),
        scratch_shapes=[
            held(features, units),
            held(units, features),
            held(slots, features),
            held(slots, features),
            held(slots, units),
            pltpu.VMEM((2, slots, tiles[0][1]), bf16),
            held(slots, features, f32),
            held(rows, width),
            dma((2, len(tiles))),
            dma((len(tiles),)),
            dma((1,)),
            dma((peers // group_size(peers, capacity),)),
        ],
        compiler_params=params(),
        cost_estimate=cost(3, 2),
        name="expert",
    )(landed, in_vmem(first_up), in_vmem(first_down), *weights)
    returned = exchange(back)

    down_grad = pl.pallas_call(
        down_grad_kernel,
        out_shape=shape((1, units, features), bf16),
        grid=(steps,),
        in_specs=[pl.BlockSpec((slots, features), lambda i: (0, 0)), pl.BlockSpec((slots, tile), lambda i: (0, i))],
        out_specs=pl.BlockSpec((None, tile, features), lambda i: (0, i, 0)),
        compiler_params=params(),
        cost_estimate=cost(1, 1),
        name="down_grad",
    )(in_hbm(grads), in_hbm(hidden))

    pick_map = pl.pallas_call(
        functools.partial(pick_map_kernel, capacity),
        out_shape=shape((PAIR * tok_rows, rows), bf16),
        in_specs=[vmem, anywhere],
        compiler_params=params(),
        name="pick_map",
    )(ids, in_hbm(grads))
    input_grad = pl.pallas_call(
        pick_kernel,
        out_shape=shape((tok_rows, features), bf16),
        compiler_params=params(),
        name="pick",
    )(pick_map, returned)
    return input_grad, down_grad


def pooled_shards(tokens, out_grad, expert_ids, gates, up_weight, down_weight):
    tok_rows = tokens.shape[0]
    top_count = expert_ids.shape[1]
    features = tokens.shape[1]
    groups = lax.axis_size("row")
    col_count = lax.axis_size("col")
    experts = groups * col_count
    capacity = 3 * tok_rows * top_count // (2 * experts)
    flat_ids = expert_ids.reshape(-1)
    onehot = (flat_ids[:, None] == jnp.arange(experts, dtype=jnp.int32)[None, :]).astype(jnp.int32)
    earlier = jnp.cumsum(onehot, axis=0) - onehot
    slot_index = jnp.sum(earlier * onehot, axis=1)
    target = flat_ids * capacity + slot_index
    placer = (jnp.arange(experts * capacity, dtype=jnp.int32)[:, None] == target[None, :]).astype(
        jnp.bfloat16
    )
    token_rows = jnp.repeat(tokens, top_count, axis=0)
    weighted = (
        gates.reshape(-1)[:, None] * jnp.repeat(out_grad, top_count, axis=0).astype(jnp.float32)
    ).astype(jnp.bfloat16)
    send_inputs = jnp.dot(placer, token_rows, preferred_element_type=jnp.float32).astype(
        jnp.bfloat16
    )
    send_grads = jnp.dot(placer, weighted, preferred_element_type=jnp.float32).astype(jnp.bfloat16)
    landed_inputs, landed_grads = (
        lax.all_to_all(
            send_inputs.reshape(experts, capacity, features),
            ("row", "col"),
            split_axis=0,
            concat_axis=0,
            tiled=True,
        ),
        lax.all_to_all(
            send_grads.reshape(experts, capacity, features),
            ("row", "col"),
            split_axis=0,
            concat_axis=0,
            tiled=True,
        ),
    )
    pooled_inputs, pooled_grads = (
        lax.all_gather(landed_inputs, "rep", axis=0, tiled=True),
        lax.all_gather(landed_grads, "rep", axis=0, tiled=True),
    )
    slot_rows = pooled_inputs.shape[0] * capacity
    input_rows = pooled_inputs.reshape(slot_rows, features)
    grad_rows = pooled_grads.reshape(slot_rows, features)
    up_block = up_weight[0]
    down_block = down_weight[0]
    preact = jnp.dot(input_rows, up_block, preferred_element_type=jnp.float32)
    hidden = jnp.maximum(preact, 0.0).astype(jnp.bfloat16)
    hidden_grad = lax.dot_general(
        grad_rows, down_block, (((1,), (1,)), ((), ())), preferred_element_type=jnp.float32
    )
    preact_grad = jnp.where(preact > 0, hidden_grad, 0.0).astype(jnp.bfloat16)
    weight_grad = lax.dot_general(
        hidden, grad_rows, (((0,), (0,)), ((), ())), preferred_element_type=jnp.float32
    )
    down_grad = weight_grad.astype(jnp.bfloat16)[None]
    summed_rows = lax.psum_scatter(
        lax.dot_general(
            preact_grad, up_block, (((1,), (1,)), ((), ())), preferred_element_type=jnp.float32
        ).astype(jnp.bfloat16),
        "rep",
        scatter_dimension=0,
        tiled=True,
    )
    returned = lax.all_to_all(
        summed_rows.reshape(experts, capacity, features),
        ("row", "col"),
        split_axis=0,
        concat_axis=0,
        tiled=True,
    )
    returned = returned.reshape(experts * capacity, features)
    picked = lax.dot_general(
        placer, returned, (((0,), (0,)), ((), ())), preferred_element_type=jnp.float32
    )
    input_grad = jnp.sum(picked.reshape(tok_rows, top_count, features), axis=1).astype(jnp.bfloat16)
    return (input_grad, down_grad)


def solution(mesh):
    by_token = P(("rep", "row", "col"), None)
    by_expert = (P(("row", "col"), None, "rep"), P(("row", "col"), "rep", None))
    return jax.shard_map(
        shards if mesh.shape["rep"] == 1 else pooled_shards,
        mesh=mesh,
        in_specs=(by_token,) * 4 + by_expert,
        out_specs=(by_token, by_expert[1]),
        check_vma=False,
    )
```

```python
import functools

import jax
import jax.numpy as jnp
from jax import lax
from jax.experimental import pallas as pl
from jax.experimental.pallas import tpu as pltpu
from jax.sharding import PartitionSpec as P

VMEM_LIMIT = 44 * 1024 * 1024
PAIR = 2
TILE = 1024
AHEAD = 2
NOWHERE = -(1 << 20)


def f32_dot(lhs, rhs, contract=((1,), (0,))):
    return lax.dot_general(lhs, rhs, (contract, ((), ())), preferred_element_type=jnp.float32)


def params():
    return pltpu.CompilerParams(vmem_limit_bytes=VMEM_LIMIT)


def row_places(ids, experts, capacity):
    tok_rows = ids.shape[1]
    names = lax.broadcasted_iota(jnp.int32, (experts, tok_rows), 0)
    chosen = [names == ids[k : k + 1, :] for k in range(ids.shape[0])]
    member = functools.reduce(jnp.logical_or, chosen).astype(jnp.bfloat16)
    before = (
        lax.broadcasted_iota(jnp.int32, (tok_rows, tok_rows), 0)
        < lax.broadcasted_iota(jnp.int32, (tok_rows, tok_rows), 1)
    ).astype(jnp.bfloat16)
    rank = f32_dot(member, before).astype(jnp.int32)
    place = names * (PAIR * capacity) + rank
    return [jnp.sum(jnp.where(pick, place, 0), axis=0, keepdims=True) for pick in chosen]


def hits_at(rows, places):
    at = lax.broadcasted_iota(jnp.int32, (rows, places[0].shape[1]), 0)
    return [at == place for place in places]


def either(hits):
    return functools.reduce(jnp.logical_or, hits).astype(jnp.bfloat16)


def started(pairs, sems):
    copies = [pltpu.make_async_copy(*pair, sems.at[i]) for i, pair in enumerate(pairs)]
    for copy in copies:
        copy.start()
    return copies


def dispatch_kernel(capacity, *refs):
    sources, (up_ref, down_ref, out_ref, up_out, down_out, ids_ref, gates_ref, both_ref, sems) = refs[:4], refs[4:]
    tok_rows = both_ref.shape[0] // 2
    targets = ids_ref, gates_ref, both_ref.at[pl.ds(0, tok_rows)], both_ref.at[pl.ds(tok_rows, tok_rows)]
    ids_copy, gates_copy, tokens_copy, grad_copy = started(zip(sources, targets), sems)
    first = pl.ds(0, down_out.shape[0])
    weights = (up_ref.at[:, first], up_out), (down_ref.at[first], down_out)
    weight_copies = started(weights, sems.at[pl.ds(4, 2)])
    rows = out_ref.shape[0]
    ids_copy.wait()
    places = row_places(ids_ref[...], rows // (PAIR * capacity), capacity)
    token_hits = hits_at(rows, places)
    grad_hits = hits_at(rows, [place + capacity for place in places])
    gates_copy.wait()
    scales = [jnp.where(hit, 1.0, 0.0) for hit in token_hits]
    scales += [jnp.where(hit, gates_ref[k : k + 1, :], 0.0) for k, hit in enumerate(grad_hits)]
    scale = jnp.sum(sum(scales), axis=1, keepdims=True)
    gather = jnp.concatenate([either(token_hits), either(grad_hits)], axis=1)
    tokens_copy.wait()
    grad_copy.wait()
    out_ref[...] = (scale * f32_dot(gather, both_ref[...])).astype(jnp.bfloat16)
    for copy in weight_copies:
        copy.wait()


def paired_rows(number, capacity):
    owner = jnp.floor((number.astype(jnp.float32) + 0.5) * (1.0 / capacity)).astype(jnp.int32)
    return number + owner * ((PAIR - 1) * capacity)


def group_size(peers, capacity):
    size = 1
    while peers % (2 * size) == 0 and size * PAIR * capacity < 192:
        size *= 2
    return size


def take_apart(landed_ref, capacity, rows_ref, grads_ref):
    size = group_size(landed_ref.shape[0] // (PAIR * capacity), capacity)
    slots, rows = size * capacity, size * PAIR * capacity
    at = lax.broadcasted_iota(jnp.int32, (slots, rows), 1)
    source = paired_rows(lax.broadcasted_iota(jnp.int32, (slots, 1), 0), capacity)
    mover = jnp.concatenate([(at == source + j * capacity).astype(jnp.bfloat16) for j in range(PAIR)], axis=0)
    for i in range(rows_ref.shape[0] // slots):
        taken = f32_dot(mover, landed_ref[i * rows : (i + 1) * rows, :]).astype(jnp.bfloat16)
        rows_ref[i * slots : (i + 1) * slots, :] = taken[:slots]
        grads_ref[i * slots : (i + 1) * slots, :] = taken[slots:]


def fold_rows(plain_ref, capacity, folded_ref, out_ref, sems):
    size = group_size(plain_ref.shape[0] // capacity, capacity)
    slots, rows = size * capacity, size * PAIR * capacity
    width = folded_ref.shape[1]
    at = lax.broadcasted_iota(jnp.int32, (rows, slots), 0)
    target = paired_rows(lax.broadcasted_iota(jnp.int32, (1, slots), 1), capacity)
    mover = jnp.concatenate([(at == target + j * capacity).astype(jnp.bfloat16) for j in range(PAIR)], axis=1)
    copies = []
    for i in range(plain_ref.shape[0] // slots):
        plain = plain_ref[i * slots : (i + 1) * slots, :].astype(jnp.bfloat16)
        halves = jnp.concatenate([plain[:, j * width : (j + 1) * width] for j in range(PAIR)], axis=0)
        part = slice(i * rows, (i + 1) * rows)
        folded_ref[part, :] = f32_dot(mover, halves).astype(jnp.bfloat16)
        copies.append(pltpu.make_async_copy(folded_ref.at[part], out_ref.at[part], sems.at[i]))
        copies[-1].start()
    return copies


def unit_tiles(units):
    size = min(units, TILE)
    return [(start, size) for start in range(0, units, size)]


def expert_kernel(
    capacity, landed_ref, first_up, first_down, up_ref, down_ref, hidden_out, grads_out, back_out, *scratch
):
    up, down, rows, grads, hidden, masked, total, back, weight_sems, hidden_sems, grads_sem, back_sems = scratch
    tiles = unit_tiles(up.shape[1])

    def weight_copies(i):
        at = pl.ds(*tiles[i])
        return [
            pltpu.make_async_copy(up_ref.at[:, at], up.at[:, at], weight_sems.at[0, i]),
            pltpu.make_async_copy(down_ref.at[at], down.at[at], weight_sems.at[1, i]),
        ]

    def start_weights(i):
        if i < len(tiles):
            arriving[i] = weight_copies(i)
            for copy in arriving[i]:
                copy.start()

    def add_row_grad(i):
        start, size = tiles[i]
        weights = up[:, start : start + size] if i else first_up[...]
        part = f32_dot(masked[i % 2, :, :size], weights, ((1,), (1,)))
        total[...] = part if i == 0 else total[...] + part

    arriving, leaving = {}, []
    for i in range(1, AHEAD):
        start_weights(i)
    take_apart(landed_ref, capacity, rows, grads)
    leaving.append(pltpu.make_async_copy(grads, grads_out, grads_sem.at[0]))
    for i, (start, size) in enumerate(tiles):
        here = slice(start, start + size)
        start_weights(i + AHEAD)
        for copy in arriving.get(i, ()):
            copy.wait()
        preact = f32_dot(rows[...], up[:, here] if i else first_up[...])
        hidden_grad = f32_dot(grads[...], down[here, :] if i else first_down[...], ((1,), (1,)))
        if i:
            add_row_grad(i - 1)
        hidden[:, here] = jnp.maximum(preact, 0.0).astype(jnp.bfloat16)
        masked[i % 2, :, :size] = jnp.where(preact > 0, hidden_grad, 0.0).astype(jnp.bfloat16)
        leaving.append(pltpu.make_async_copy(hidden.at[:, here], hidden_out.at[:, here], hidden_sems.at[i]))
    for copy in leaving:
        copy.start()
    add_row_grad(len(tiles) - 1)
    for copy in leaving + fold_rows(total, capacity, back, back_out, back_sems):
        copy.wait()


def down_grad_kernel(grads_ref, hidden_ref, out_ref):
    out_ref[...] = f32_dot(hidden_ref[...], grads_ref[...], ((0,), (0,))).astype(jnp.bfloat16)


def pick_map_kernel(capacity, ids_ref, after_ref, out_ref):
    tok_rows, rows = ids_ref.shape[1], out_ref.shape[1]
    places = row_places(ids_ref[...], rows // (PAIR * capacity), capacity)
    for j in range(PAIR):
        chosen = either(hits_at(rows, [place + j * capacity for place in places]))
        out_ref[j * tok_rows : (j + 1) * tok_rows, :] = chosen.T


def pick_kernel(map_ref, returned_ref, out_ref):
    tok_rows, width = out_ref.shape[0], returned_ref.shape[1]
    picked = f32_dot(map_ref[...], returned_ref[...]).astype(jnp.bfloat16)
    for j in range(PAIR):
        out_ref[:, j * width : (j + 1) * width] = picked[j * tok_rows : (j + 1) * tok_rows]


def exchange(rows):
    axes = ("row", "col")
    peers = lax.axis_size(axes)
    cut = rows.reshape(peers, rows.shape[0] // peers, rows.shape[1])
    return lax.all_to_all(cut, axes, split_axis=0, concat_axis=0, tiled=True).reshape(rows.shape)


def in_hbm(array):
    return pltpu.with_memory_space_constraint(array, pltpu.HBM)


def in_vmem(array):
    return pltpu.with_memory_space_constraint(array, pltpu.VMEM)


def held(rows, columns, kind=jnp.bfloat16):
    return pltpu.VMEM((rows, columns), kind)


def shards(tokens, out_grad, expert_ids, gates, up_weight, down_weight):
    tok_rows, features = tokens.shape
    top_count = expert_ids.shape[1]
    units = up_weight.shape[2]
    peers = lax.axis_size(("row", "col"))
    capacity = 3 * tok_rows * top_count // (2 * peers)
    slots, rows, width = peers * capacity, peers * PAIR * capacity, features // PAIR
    tile = min(units, TILE // 2)
    steps = units // tile
    bf16, f32 = jnp.bfloat16, jnp.float32
    shape = jax.ShapeDtypeStruct
    dma = pltpu.SemaphoreType.DMA
    flops = 2 * slots * features * units
    weight_bytes = 2 * features * units

    def cost(matmuls, weights):
        return pl.CostEstimate(flops=matmuls * flops, bytes_accessed=weights * weight_bytes, transcendentals=0)

    ids = expert_ids.T
    hbm = pl.BlockSpec(memory_space=pltpu.HBM)
    vmem = pl.BlockSpec(memory_space=pltpu.VMEM)
    anywhere = pl.BlockSpec(memory_space=pl.ANY)
    tiles = unit_tiles(units)

    size = tiles[0][1]
    weights = in_hbm(up_weight[0]), in_hbm(down_weight[0])
    sent, first_up, first_down = pl.pallas_call(
        functools.partial(dispatch_kernel, capacity),
        out_shape=(
            shape((rows, features), bf16),
            pltpu.VMEM((features, size), bf16),
            pltpu.VMEM((size, features), bf16),
        ),
        in_specs=[hbm, hbm, hbm, hbm, hbm, hbm],
        scratch_shapes=[
            held(top_count, tok_rows, jnp.int32),
            held(top_count, tok_rows, f32),
            held(2 * tok_rows, features),
            dma((6,)),
        ],
        compiler_params=params(),
        name="dispatch",
    )(*[in_hbm(array) for array in (ids, gates.T, tokens, out_grad)], *weights)
    landed = exchange(sent)

    hidden, grads, back = pl.pallas_call(
        functools.partial(expert_kernel, capacity),
        out_shape=(
            pltpu.HBM((slots, units), bf16),
            pltpu.HBM((slots, features), bf16),
            pltpu.HBM((rows, width), bf16),
        ),
        in_specs=[vmem, vmem, vmem, hbm, hbm],
        out_specs=(hbm, hbm, hbm),
        scratch_shapes=[
            held(features, units),
            held(units, features),
            held(slots, features),
            held(slots, features),
            held(slots, units),
            pltpu.VMEM((2, slots, tiles[0][1]), bf16),
            held(slots, features, f32),
            held(rows, width),
            dma((2, len(tiles))),
            dma((len(tiles),)),
            dma((1,)),
            dma((peers // group_size(peers, capacity),)),
        ],
        compiler_params=params(),
        cost_estimate=cost(3, 2),
        name="expert",
    )(landed, in_vmem(first_up), in_vmem(first_down), *weights)
    returned = exchange(back)

    down_grad = pl.pallas_call(
        down_grad_kernel,
        out_shape=shape((1, units, features), bf16),
        grid=(steps,),
        in_specs=[pl.BlockSpec((slots, features), lambda i: (0, 0)), pl.BlockSpec((slots, tile), lambda i: (0, i))],
        out_specs=pl.BlockSpec((None, tile, features), lambda i: (0, i, 0)),
        compiler_params=params(),
        cost_estimate=cost(1, 1),
        name="down_grad",
    )(in_hbm(grads), in_hbm(hidden))

    pick_map = pl.pallas_call(
        functools.partial(pick_map_kernel, capacity),
        out_shape=shape((PAIR * tok_rows, rows), bf16),
        in_specs=[vmem, anywhere],
        compiler_params=params(),
        name="pick_map",
    )(ids, in_hbm(grads))
    input_grad = pl.pallas_call(
        pick_kernel,
        out_shape=shape((tok_rows, features), bf16),
        compiler_params=params(),
        name="pick",
    )(pick_map, returned)
    return input_grad, down_grad


def pooled_shards(tokens, out_grad, expert_ids, gates, up_weight, down_weight):
    tok_rows = tokens.shape[0]
    top_count = expert_ids.shape[1]
    features = tokens.shape[1]
    groups = lax.axis_size("row")
    col_count = lax.axis_size("col")
    experts = groups * col_count
    capacity = 3 * tok_rows * top_count // (2 * experts)
    flat_ids = expert_ids.reshape(-1)
    onehot = (flat_ids[:, None] == jnp.arange(experts, dtype=jnp.int32)[None, :]).astype(jnp.int32)
    earlier = jnp.cumsum(onehot, axis=0) - onehot
    slot_index = jnp.sum(earlier * onehot, axis=1)
    target = flat_ids * capacity + slot_index
    placer = (jnp.arange(experts * capacity, dtype=jnp.int32)[:, None] == target[None, :]).astype(
        jnp.bfloat16
    )
    token_rows = jnp.repeat(tokens, top_count, axis=0)
    weighted = (
        gates.reshape(-1)[:, None] * jnp.repeat(out_grad, top_count, axis=0).astype(jnp.float32)
    ).astype(jnp.bfloat16)
    send_inputs = jnp.dot(placer, token_rows, preferred_element_type=jnp.float32).astype(
        jnp.bfloat16
    )
    send_grads = jnp.dot(placer, weighted, preferred_element_type=jnp.float32).astype(jnp.bfloat16)
    landed_inputs, landed_grads = (
        lax.all_to_all(
            send_inputs.reshape(experts, capacity, features),
            ("row", "col"),
            split_axis=0,
            concat_axis=0,
            tiled=True,
        ),
        lax.all_to_all(
            send_grads.reshape(experts, capacity, features),
            ("row", "col"),
            split_axis=0,
            concat_axis=0,
            tiled=True,
        ),
    )
    pooled_inputs, pooled_grads = (
        lax.all_gather(landed_inputs, "rep", axis=0, tiled=True),
        lax.all_gather(landed_grads, "rep", axis=0, tiled=True),
    )
    slot_rows = pooled_inputs.shape[0] * capacity
    input_rows = pooled_inputs.reshape(slot_rows, features)
    grad_rows = pooled_grads.reshape(slot_rows, features)
    up_block = up_weight[0]
    down_block = down_weight[0]
    preact = jnp.dot(input_rows, up_block, preferred_element_type=jnp.float32)
    hidden = jnp.maximum(preact, 0.0).astype(jnp.bfloat16)
    hidden_grad = lax.dot_general(
        grad_rows, down_block, (((1,), (1,)), ((), ())), preferred_element_type=jnp.float32
    )
    preact_grad = jnp.where(preact > 0, hidden_grad, 0.0).astype(jnp.bfloat16)
    weight_grad = lax.dot_general(
        hidden, grad_rows, (((0,), (0,)), ((), ())), preferred_element_type=jnp.float32
    )
    down_grad = weight_grad.astype(jnp.bfloat16)[None]
    summed_rows = lax.psum_scatter(
        lax.dot_general(
            preact_grad, up_block, (((1,), (1,)), ((), ())), preferred_element_type=jnp.float32
        ).astype(jnp.bfloat16),
        "rep",
        scatter_dimension=0,
        tiled=True,
    )
    returned = lax.all_to_all(
        summed_rows.reshape(experts, capacity, features),
        ("row", "col"),
        split_axis=0,
        concat_axis=0,
        tiled=True,
    )
    returned = returned.reshape(experts * capacity, features)
    picked = lax.dot_general(
        placer, returned, (((0,), (0,)), ((), ())), preferred_element_type=jnp.float32
    )
    input_grad = jnp.sum(picked.reshape(tok_rows, top_count, features), axis=1).astype(jnp.bfloat16)
    return (input_grad, down_grad)


def solution(mesh):
    by_token = P(("rep", "row", "col"), None)
    by_expert = (P(("row", "col"), None, "rep"), P(("row", "col"), "rep", None))
    return jax.shard_map(
        shards if mesh.shape["rep"] == 1 else pooled_shards,
        mesh=mesh,
        in_specs=(by_token,) * 4 + by_expert,
        out_specs=(by_token, by_expert[1]),
        check_vma=False,
    )
```
